32 devices in a mesh: gx: 4 (over y, core), gy: 8 (over z, x).
Axes of the slice: x: 2, y: 2, z: 4, core: 2. Of those that a mesh axis runs over, the one named last changes fastest.
Arguments:
- features: bfloat16 [128, 128, 64, 128], P('gx', 'gy'), may hold values from -6 to 6
- voxel_mask: int32 [128, 128, 64], P('gx', 'gy'), may hold values 0 or 1
- brick_mask: int32 [8, 8, 4], P('gx', 'gy'), may hold values from 0 to 1
- owner: int32 [4, 8, 8, 1], P('gx', 'gy'), may hold values from 0 to 7, as said below
- weights: bfloat16 [3, 3, 3, 128, 64], replicated, may hold values from -0.109375 to 0.109375
- bias: float32 [64], replicated, may hold values from -0.5 to 0.5
Outputs:
- decoded: bfloat16 [4, 64, 64, 4096], P('gx', 'gy')
The draws below stay inside these ranges and needn't reach their ends.
Inputs may be any that keep to these rules, and one draw needn't show every extreme that they name: Active bricks are spread unevenly over tiles. Among one device's 8 bricks no owner index appears more than 1 times, and some index appears exactly 1 times. Owners are chosen from the active-brick counts so that over all sources of one brick-grid row no owner receives more than 8 active bricks.
All inputs are finite; a program needn't handle non-finite values. No bound on the sum of `voxel_mask` on one device may be relied on, other than what follows from the above.
Results may differ from the reference program's by a relative error of at most 0.001.
Values may be sent and summed in bfloat16 or wider, within the bound.
No kernel may reach another device: no remote copies, remote signals or barrier semaphores. Data moves between devices by JAX's collectives and lax.ppermute only.
A program may use at most 256 MiB of HBM per device.

```python
import jax
import jax.numpy as jnp
from jax import lax

C = 64
CIN = 128
EDGE = 16
BX = 2
BY = 1
BZ = 4
BRICKS = 8
CAP = 1
NXV = 128
NYV = 128
NZV = 64
N_GX = 4
N_GY = 8


def tile_activity(key):
    tile_key = jax.random.fold_in(key, 11)
    brick_key = jax.random.fold_in(key, 12)
    first = jax.random.randint(jax.random.fold_in(tile_key, 1), (N_GX, N_GY), 0, 9)
    second = jax.random.randint(jax.random.fold_in(tile_key, 2), (N_GX, N_GY), 0, 9)
    level = jnp.minimum(8, 1 + first * second // 8)
    picks = jax.random.randint(brick_key, (N_GX, N_GY, BRICKS), 0, 8)
    return (picks < level[:, :, None]).astype(jnp.int32)


def draw_brick_mask(key, part):
    tile = tile_activity(key)
    grid = tile.reshape(N_GX, N_GY, BX, BY, BZ).transpose(0, 2, 1, 3, 4)
    return grid.reshape(N_GX * BX, N_GY * BY, BZ)


def draw_owner(key, part):
    tile = tile_activity(key)
    active = jnp.sum(tile, axis=2)
    before = jnp.cumsum(active, axis=1) - active
    spare = 1 - tile
    active_rank = jnp.cumsum(tile, axis=2) - tile
    spare_rank = jnp.cumsum(spare, axis=2) - spare
    position = jnp.where(tile == 1, active_rank, active[:, :, None] + spare_rank)
    owners = (before[:, :, None] + position) % N_GY
    return owners[..., None].astype(jnp.int32)


def set_ends(drawn, own_key, least, top_value):
    dims = drawn.shape
    place = [jax.random.randint(jax.random.fold_in(own_key, axis), (), 0, dims[axis]) for axis in range(len(dims))]
    drawn = drawn.at[tuple(place)].set(least)
    longest = dims.index(max(dims))
    place[longest] = (place[longest] + 1) % dims[longest]
    return drawn.at[tuple(place)].set(top_value)


def levels(stream_key, extent, shards, least, top_value):
    def one(dim, blocks):
        heights = jax.random.uniform(jax.random.fold_in(jax.random.fold_in(stream_key, 6), dim), (blocks,), jnp.float32, least / len(shards), top_value / len(shards))
        return jnp.repeat(jnp.exp(heights), extent[dim] // blocks).reshape((-1,) + (1,) * (len(extent) - dim - 1))

    gain = one(*shards[0])
    for cut in shards[1:]:
        gain = gain * one(*cut)
    return gain


def scatter_about(stream_key, shape, scale, most, pieces=(), kind=jnp.bfloat16):
    drawn = scale * jax.random.normal(stream_key, shape, jnp.float32)
    if pieces:
        drawn = drawn * levels(stream_key, shape, pieces, -0.22, 0.18)
    return jnp.clip(drawn, -most, most).astype(kind)


def setup_inputs(seed: int = 0) -> dict:
    keys = jax.random.split(jax.random.key(seed), 7)
    features = scatter_about(keys[0], (NXV, NYV, NZV, CIN), 1.0, 6.0, ((0, 4), (1, 8)))
    voxel_mask = set_ends((jax.random.randint(keys[1], (NXV, NYV, NZV), 0, 3) < 2).astype(jnp.int32), jax.random.fold_in(keys[1], 1), 0, 1)
    brick_mask = draw_brick_mask(jax.random.fold_in(keys[6], 71), 0)
    owner = draw_owner(jax.random.fold_in(keys[6], 71), 0)
    weights = scatter_about(keys[4], (3, 3, 3, CIN, C), (27 * CIN) ** -0.5, 0.109375)
    bias = jnp.clip(jax.random.uniform(keys[5], (C,), jnp.float32, -0.5, 0.5), -0.5, 0.5)
    return {"features": features, "voxel_mask": voxel_mask, "brick_mask": brick_mask, "owner": owner, "weights": weights, "bias": bias}


def expand_bricks(brick_mask):
    grown = jnp.repeat(brick_mask, EDGE, axis=0)
    grown = jnp.repeat(grown, EDGE, axis=1)
    return jnp.repeat(grown, EDGE, axis=2)


def reference(features, voxel_mask, brick_mask, owner, weights, bias):
    live = voxel_mask * expand_bricks(brick_mask)
    inputs = features * live.astype(jnp.bfloat16)[..., None]
    padded = jnp.pad(inputs, ((1, 1), (1, 1), (1, 1), (0, 0)))
    kernel = weights.astype(jnp.float32)
    live_float = live.astype(jnp.float32)
    rows = BX * EDGE
    order = jnp.arange(BRICKS, dtype=jnp.int32)
    earlier = order[None, :] < order[:, None]

    def strip(index):
        piece = lax.dynamic_slice_in_dim(padded, index * rows, rows + 2, 0).astype(jnp.float32)
        pre = lax.conv_general_dilated(piece[None], kernel, (1, 1, 1), "VALID",
                                       dimension_numbers=("NDHWC", "DHWIO", "NCDHW"),
                                       precision=lax.Precision.HIGHEST)[0]
        mask_strip = lax.dynamic_slice_in_dim(live_float, index * rows, rows, 0)
        value = (jnp.maximum(pre + bias[:, None, None, None], 0.0) * mask_strip[None]).astype(jnp.bfloat16)
        value = value.reshape(C, BX, EDGE, N_GY, BY, EDGE, BZ, EDGE)
        value = value.transpose(3, 1, 4, 6, 0, 2, 5, 7).reshape(N_GY * BRICKS, C, EDGE**3)
        ids = lax.dynamic_index_in_dim(owner, index, 0, keepdims=False).reshape(N_GY, BRICKS)
        same = ids[:, :, None] == ids[:, None, :]
        rank = jnp.sum(jnp.logical_and(same, earlier[None]).astype(jnp.int32), axis=2)
        source = jnp.arange(N_GY, dtype=jnp.int32)[:, None]
        dest = ids * (N_GY * CAP) + source * CAP + rank
        empty = jnp.zeros((N_GY * N_GY * CAP, C, EDGE**3), jnp.bfloat16)
        return empty.at[dest.reshape(-1)].set(value)

    return lax.map(strip, jnp.arange(N_GX, dtype=jnp.int32))
```

```python
import functools

import jax
import jax.numpy as jnp
from jax import lax
from jax.experimental import pallas as pl
from jax.experimental.pallas import tpu as pltpu
from jax.sharding import PartitionSpec as P

C = 64
EDGE = 16
AREA = EDGE * EDGE
VOXELS = EDGE**3
PAIRS = EDGE // 2


def fetches(brick, layers, main, face_x, face_y, edge, raw, sem):
    bx = brick // layers
    bz = brick % layers
    rows = EDGE + 1
    groups = []
    for j in range(3):
        tile = jnp.clip(bz - 1 + j, 0, layers - 1)
        inside = jnp.logical_and(bz - 1 + j >= 0, bz - 1 + j < layers)
        first = bx * (EDGE - 1)
        into = 1 - bx
        copies = [
            (main.at[pl.ds(first, rows), :, tile], raw.at[pl.ds(into, rows), pl.ds(1, EDGE), j]),
            (face_x.at[bx, :, tile], raw.at[bx * rows, pl.ds(1, EDGE), j]),
        ]
        for side in range(2):
            column = side * rows
            copies.append((face_y.at[side, pl.ds(first, rows), tile], raw.at[pl.ds(into, rows), column, j]))
            copies.append((edge.at[side, bx, tile], raw.at[bx * rows, column, j]))
        groups.append((inside, [pltpu.make_async_copy(a, b, sem.at[j, n]) for n, (a, b) in enumerate(copies)]))
    return groups


def conv_kernel(layers, info, main, face_x, face_y, edge, weights, bias, masks, out, raw, stage_a, stage_b, high, sems):
    step = pl.program_id(0)
    steps = pl.num_programs(0)
    cin = main.shape[-1]

    def start(index, slot):
        brick = info[index]
        for j, (inside, copies) in enumerate(fetches(brick, layers, main, face_x, face_y, edge, raw.at[slot], sems.at[slot])):

            @pl.when(inside)
            def _():
                for copy in copies:
                    copy.start()

            @pl.when(jnp.logical_not(inside))
            def _():
                raw[slot, :, :, j] = jnp.zeros(raw.shape[1:3] + raw.shape[4:], raw.dtype)

    @pl.when(jnp.logical_and(step == 0, info[steps] > 0))
    def _():
        start(0, 0)

    following = jnp.minimum(step + 1, steps - 1)

    @pl.when(jnp.logical_and(step + 1 < steps, info[steps + following] > 0))
    def _():
        start(following, following % 2)

    @pl.when(info[steps + step] == 0)
    def _():
        out[...] = jnp.zeros_like(out)

    @pl.when(info[steps + step] > 0)
    def _():
        slot = step % 2
        brick = info[step]
        for inside, copies in fetches(brick, layers, main, face_x, face_y, edge, raw.at[slot], sems.at[slot]):

            @pl.when(inside)
            def _():
                for copy in copies:
                    copy.wait()

        top = lax.broadcasted_iota(jnp.int32, (EDGE + 2, EDGE, cin), 1)

        def build(stage, pair):
            for j in range(2):
                plane = 2 * pair + j
                centre = raw[slot, plane, :, 1]
                below = raw[slot, plane, :, 0].astype(jnp.float32)
                middle = centre.astype(jnp.float32)
                above = raw[slot, plane, :, 2].astype(jnp.float32)
                up = jnp.where(top == 0, pltpu.roll(below, 1, 1), pltpu.roll(middle, 1, 1))
                down = jnp.where(top == EDGE - 1, pltpu.roll(above, EDGE - 1, 1), pltpu.roll(middle, EDGE - 1, 1))
                for c, value in enumerate((up, centre, down)):
                    stage[:, pl.ds((3 * j + c) * cin, cin)] = value.astype(jnp.bfloat16).reshape((EDGE + 2) * EDGE, cin)

        def taps(stage, columns):
            total = jnp.dot(stage[0:AREA, :], weights[0, :, columns], preferred_element_type=jnp.float32)
            for b in range(1, 3):
                total += jnp.dot(stage[b * EDGE : b * EDGE + AREA, :], weights[b, :, columns], preferred_element_type=jnp.float32)
            return total

        def emit(q, low):
            value = jnp.maximum(high[...] + low + bias[...], 0.0).T
            mask = masks[brick, q]
            block = jnp.concatenate([value[:C] * mask[0:1], value[C:] * mask[1:2]], axis=1)
            out[0, :, pl.ds(pl.multiple_of(q * 2 * AREA, 2 * AREA), 2 * AREA)] = block.astype(out.dtype)

        high[...] = jnp.zeros_like(high)
        build(stage_a, 0)

        @pl.loop(0, PAIRS // 2)
        def _(i):
            total = taps(stage_a, slice(None))
            build(stage_b, 2 * i + 1)
            emit(jnp.maximum(2 * i - 1, 0), total[:, : 2 * C])
            high[...] = total[:, 2 * C :]
            total = taps(stage_b, slice(None))
            build(stage_a, 2 * i + 2)
            emit(2 * i, total[:, : 2 * C])
            high[...] = total[:, 2 * C :]

        emit(PAIRS - 1, taps(stage_a, slice(0, 2 * C)))


def convolve(info, main, face_x, face_y, edge, weights, bias, masks):
    steps = info.shape[0] // 2
    layers = main.shape[2]
    cin = main.shape[-1]
    span = EDGE + 2
    flops = 2 * (PAIRS + 1) * AREA * 18 * cin * 4 * C * steps
    return pl.pallas_call(
        functools.partial(conv_kernel, layers),
        out_shape=jax.ShapeDtypeStruct((steps, C, VOXELS), jnp.bfloat16),
        grid_spec=pltpu.PrefetchScalarGridSpec(
            num_scalar_prefetch=1,
            grid=(steps,),
            in_specs=[pl.BlockSpec(memory_space=pl.ANY)] * 4
            + [pl.BlockSpec(memory_space=pltpu.VMEM)] * 3,
            out_specs=pl.BlockSpec((1, C, VOXELS), lambda i, info: (i, 0, 0)),
            scratch_shapes=[
                pltpu.VMEM((2, span, span, 3, EDGE, cin), jnp.bfloat16),
                pltpu.VMEM((span * EDGE, 6 * cin), jnp.bfloat16),
                pltpu.VMEM((span * EDGE, 6 * cin), jnp.bfloat16),
                pltpu.VMEM((AREA, 2 * C), jnp.float32),
                pltpu.SemaphoreType.DMA((2, 3, 6)),
            ],
        ),
        compiler_params=pltpu.CompilerParams(vmem_limit_bytes=40 * 1024 * 1024),
        cost_estimate=pl.CostEstimate(flops=flops, bytes_accessed=16 << 20, transcendentals=0),
    )(info, main, face_x, face_y, edge, weights, bias, masks)


def paired_weights(weights):
    zero = jnp.zeros_like(weights[0])
    planes = []
    for j in range(2):
        planes.append(jnp.stack([weights[2 + j - t] if 0 <= 2 + j - t <= 2 else zero for t in range(4)], axis=3))
    both = jnp.stack(planes, axis=1)
    return both.reshape(3, 6 * weights.shape[3], 4 * weights.shape[4])


def shift(value, axis, up):
    count = lax.axis_size(axis)
    if up:
        return lax.ppermute(value, axis, [(i, i + 1) for i in range(count - 1)])
    return lax.ppermute(value, axis, [(i + 1, i) for i in range(count - 1)])


def per_device(features, voxel_mask, brick_mask, owner, weights, bias):
    extent_x, extent_y, extent_z, channels_in = features.shape
    bricks_x, bricks_y, bricks_z = extent_x // EDGE, extent_y // EDGE, extent_z // EDGE
    count = bricks_x * bricks_y * bricks_z
    groups = lax.axis_size("gy")
    me = lax.axis_index("gy")

    ids = owner.reshape(count)
    active = brick_mask.reshape(count)
    peers = jnp.arange(groups, dtype=jnp.int32)
    match = (ids[None, :] == peers[:, None]).astype(jnp.int32)
    brick_of = jnp.sum(match * jnp.arange(count, dtype=jnp.int32)[None, :], axis=1)
    sends = jnp.sum(match * active[None, :], axis=1)
    everyone = lax.all_gather(sends, "gy")

    grown = jnp.repeat(brick_mask, EDGE, axis=0)
    grown = jnp.repeat(grown, EDGE, axis=1)
    grown = jnp.repeat(grown, EDGE, axis=2)
    live = voxel_mask * grown
    live_bf = live.astype(jnp.bfloat16)

    def masked(values, where):
        return (values * where[..., None]).reshape(values.shape[:2] + (bricks_z, EDGE, channels_in))

    x_first = masked(features[:1], live_bf[:1])
    x_last = masked(features[-1:], live_bf[-1:])
    y_first = masked(features[:, :1], live_bf[:, :1])
    y_last = masked(features[:, -1:], live_bf[:, -1:])
    x_low = shift(x_last, "gx", True)
    x_high = shift(x_first, "gx", False)
    y_low = shift(y_last, "gy", True)
    y_high = shift(y_first, "gy", False)
    face_x = jnp.concatenate([x_low, x_high], axis=0)
    edge_low = shift(face_x[:, -1], "gy", True)
    edge_high = shift(face_x[:, 0], "gy", False)
    edge = jnp.stack([edge_low, edge_high])
    face_y = jnp.stack([y_low[:, 0], y_high[:, 0]])
    main = masked(features, live_bf)

    masks = live.astype(jnp.float32).reshape(bricks_x, EDGE, bricks_y, EDGE, bricks_z, EDGE)
    masks = masks.transpose(0, 2, 4, 1, 3, 5).reshape(count, PAIRS, 2, AREA)
    order = jnp.bitwise_xor(peers, me)
    info = jnp.concatenate([brick_of[order], sends[order]])
    wide_bias = jnp.concatenate([bias, bias])[None, :]
    bricks = convolve(info, main, face_x, face_y, edge, paired_weights(weights), wide_bias, masks)

    decoded = jnp.zeros((groups, C, VOXELS), jnp.bfloat16)
    decoded = lax.dynamic_update_slice_in_dim(decoded, bricks[:1], me, 0)
    for k in range(1, groups):
        peer = order[k]
        mine = sends[peer]
        theirs = everyone[peer, me]
        upward = [(i, i ^ k) for i in range(groups) if i < i ^ k]
        downward = [(b, a) for a, b in upward]
        lower = me < peer
        case = jnp.where(lower, mine, theirs) + 2 * jnp.where(lower, theirs, mine)
        branches = [jnp.zeros_like]
        for pairs in (upward, downward, upward + downward):
            branches.append(functools.partial(lambda pairs, v: lax.ppermute(v, "gy", pairs), pairs))
        got = lax.switch(case, branches, bricks[k : k + 1])
        decoded = lax.dynamic_update_slice_in_dim(decoded, got, peer, 0)
    return decoded[None]


def solution(mesh):
    return jax.shard_map(
        per_device,
        mesh=mesh,
        in_specs=(
            P("gx", "gy", None, None),
            P("gx", "gy", None),
            P("gx", "gy", None),
            P("gx", "gy", None, None),
            P(),
            P(),
        ),
        out_specs=P("gx", "gy", None, None),
        check_vma=False,
    )
```

```python
import functools

import jax
import jax.numpy as jnp
from jax import lax
from jax.experimental import pallas as pl
from jax.experimental.pallas import tpu as pltpu
from jax.sharding import PartitionSpec as P

C = 64
EDGE = 16
AREA = EDGE * EDGE
VOXELS = EDGE**3
PAIRS = EDGE // 2
SPAN = EDGE + 2


def weight_kernel(weights, out):
    cin = weights.shape[-1]
    for b in range(3):
        for j in range(2):
            for c in range(3):
                parts = []
                for t in range(4):
                    a = 2 + j - t
                    tap = weights[(a * 3 + b) * 3 + c] if 0 <= a <= 2 else jnp.zeros(weights.shape[1:], weights.dtype)
                    parts.append(tap.astype(jnp.float32))
                block = jnp.concatenate(parts, axis=0).T
                out[b, (3 * j + c) * cin : (3 * j + c + 1) * cin, :] = block.astype(out.dtype)


def paired_weights(weights):
    cin, cout = weights.shape[3:]
    taps = weights.transpose(0, 1, 2, 4, 3).reshape(27, cout, cin)
    return pl.pallas_call(
        weight_kernel,
        out_shape=jax.ShapeDtypeStruct((3, 6 * cin, 4 * cout), weights.dtype),
        in_specs=[pl.BlockSpec(memory_space=pltpu.VMEM)],
        out_specs=pl.BlockSpec(memory_space=pltpu.VMEM),
        cost_estimate=pl.CostEstimate(flops=0, bytes_accessed=2 << 20, transcendentals=0),
    )(taps)


def conv_kernel(index, info, main, x_low, x_high, y_low, y_high, e_low, e_high, weights, masks, bias, out, raw, wide, live, stage_a, stage_b, high, sems, sem):
    layers = main.shape[2]
    cin = main.shape[-1]
    brick = info[index]
    bx = brick // layers
    bz = brick % layers
    rows = EDGE + 1

    def copies(bx, j):
        tile = jnp.clip(bz - 1 + j, 0, layers - 1)
        body = pl.ds(1 - bx, rows)
        source = pl.ds(bx * (EDGE - 1), rows)
        end = bx * rows
        x_face = (x_low, x_high)[bx]
        pairs = [
            (main.at[source, :, tile], raw.at[body, pl.ds(1, EDGE), j]),
            (x_face.at[0, :, tile], raw.at[end, pl.ds(1, EDGE), j]),
        ]
        for column, face, edge in ((0, y_low, e_low), (rows, y_high, e_high)):
            pairs.append((face.at[source, 0, tile], raw.at[body, column, j]))
            pairs.append((edge.at[bx, tile], raw.at[end, column, j]))
        return [pltpu.make_async_copy(a, b, sems.at[j, n]) for n, (a, b) in enumerate(pairs)]

    @pl.when(info[info.shape[0] // 3 + index] > 0)
    def _():
        loads = [pltpu.make_async_copy(weights, wide, sem.at[0]), pltpu.make_async_copy(masks.at[brick], live, sem.at[1])]
        inside = [jnp.logical_and(bz - 1 + j >= 0, bz - 1 + j < layers) for j in range(3)]
        for side in range(2):

            @pl.when(bx == side)
            def _():
                for j in range(3):

                    @pl.when(inside[j])
                    def _():
                        for copy in copies(side, j):
                            copy.start()

        for load in loads:
            load.start()
        for j in range(3):

            @pl.when(jnp.logical_not(inside[j]))
            def _():
                raw[:, :, j] = jnp.zeros(raw.shape[:2] + raw.shape[3:], raw.dtype)

        for side in range(2):

            @pl.when(bx == side)
            def _():
                for j in range(3):

                    @pl.when(inside[j])
                    def _():
                        for copy in copies(side, j):
                            copy.wait()

        top = lax.broadcasted_iota(jnp.int32, (SPAN, EDGE, cin), 1)

        def build(stage, pair):
            for j in range(2):
                plane = 2 * pair + j
                centre = raw[plane, :, 1]
                below = raw[plane, :, 0].astype(jnp.float32)
                middle = centre.astype(jnp.float32)
                above = raw[plane, :, 2].astype(jnp.float32)
                up = jnp.where(top == 0, pltpu.roll(below, 1, 1), pltpu.roll(middle, 1, 1))
                down = jnp.where(top == EDGE - 1, pltpu.roll(above, EDGE - 1, 1), pltpu.roll(middle, EDGE - 1, 1))
                for c, value in enumerate((up, centre, down)):
                    stage[:, pl.ds((3 * j + c) * cin, cin)] = value.astype(jnp.bfloat16).reshape(SPAN * EDGE, cin)

        def taps(stage, columns):
            total = jnp.dot(stage[0:AREA, :], wide[0, :, columns], preferred_element_type=jnp.float32)
            for b in range(1, 3):
                total += jnp.dot(stage[b * EDGE : b * EDGE + AREA, :], wide[b, :, columns], preferred_element_type=jnp.float32)
            return total

        def emit(q, low):
            value = jnp.maximum(high[...] + low + bias[...], 0.0).T
            mask = live[q]
            block = jnp.concatenate([value[:C] * mask[0:1], value[C:] * mask[1:2]], axis=1)
            out[:, pl.ds(pl.multiple_of(q * 2 * AREA, 2 * AREA), 2 * AREA)] = block.astype(out.dtype)

        high[...] = jnp.zeros_like(high)
        build(stage_a, 0)
        for load in loads:
            load.wait()

        @pl.loop(0, PAIRS // 2)
        def _(i):
            total = taps(stage_a, slice(None))
            build(stage_b, 2 * i + 1)
            emit(jnp.maximum(2 * i - 1, 0), total[:, : 2 * C])
            high[...] = total[:, 2 * C :]
            total = taps(stage_b, slice(None))
            build(stage_a, 2 * i + 2)
            emit(2 * i, total[:, : 2 * C])
            high[...] = total[:, 2 * C :]

        emit(PAIRS - 1, taps(stage_a, slice(0, 2 * C)))


def convolve(index, info, operands):
    cin = operands[0].shape[-1]
    wide, masks = operands[7:9]
    flops = 2 * (PAIRS + 1) * AREA * 18 * cin * 4 * C
    return pl.pallas_call(
        functools.partial(conv_kernel, index),
        out_shape=jax.ShapeDtypeStruct((C, VOXELS), jnp.bfloat16),
        in_specs=[pl.BlockSpec(memory_space=pltpu.SMEM)]
        + [pl.BlockSpec(memory_space=pl.ANY)] * 9
        + [pl.BlockSpec(memory_space=pltpu.VMEM)],
        out_specs=pl.BlockSpec(memory_space=pltpu.VMEM),
        scratch_shapes=[
            pltpu.VMEM((SPAN, SPAN, 3, EDGE, cin), jnp.bfloat16),
            pltpu.VMEM(wide.shape, wide.dtype),
            pltpu.VMEM(masks.shape[1:], masks.dtype),
            pltpu.VMEM((SPAN * EDGE, 6 * cin), jnp.bfloat16),
            pltpu.VMEM((SPAN * EDGE, 6 * cin), jnp.bfloat16),
            pltpu.VMEM((AREA, 2 * C), jnp.float32),
            pltpu.SemaphoreType.DMA((3, 6)),
            pltpu.SemaphoreType.DMA((2,)),
        ],
        compiler_params=pltpu.CompilerParams(vmem_limit_bytes=24 * 1024 * 1024),
        cost_estimate=pl.CostEstimate(flops=flops, bytes_accessed=8 << 20, transcendentals=0),
    )(info, *operands)


def gather_kernel(info, *refs):
    groups = info.shape[0] // 3
    bricks, out, zero, sems = refs[:groups], refs[groups], refs[groups + 1], refs[groups + 2]
    chunks = sems.shape[1]
    size = C // chunks
    me = lax.axis_index("gy")
    zero[...] = jnp.zeros_like(zero)

    def copies(k, full):
        for n in range(chunks):
            rows = pl.ds(n * size, size)
            yield pltpu.make_async_copy(bricks[k].at[rows] if full else zero, out.at[me ^ k, rows], sems.at[k, n])

    for act in ("start", "wait"):
        for k in range(groups):
            for full in (True, False):

                @pl.when((info[2 * groups + k] > 0) == full)
                def _():
                    for copy in copies(k, full):
                        getattr(copy, act)()


def gather(info, bricks):
    groups = len(bricks)
    chunks = 4
    return pl.pallas_call(
        gather_kernel,
        out_shape=jax.ShapeDtypeStruct((groups, C, VOXELS), jnp.bfloat16),
        in_specs=[pl.BlockSpec(memory_space=pltpu.SMEM)] + [pl.BlockSpec(memory_space=pl.ANY)] * groups,
        out_specs=pl.BlockSpec(memory_space=pl.ANY),
        scratch_shapes=[
            pltpu.VMEM((C // chunks, VOXELS), jnp.bfloat16),
            pltpu.SemaphoreType.DMA((groups, chunks)),
        ],
        cost_estimate=pl.CostEstimate(flops=0, bytes_accessed=8 << 20, transcendentals=0),
    )(info, *bricks)


def shift(value, axis, up):
    count = lax.axis_size(axis)
    if up:
        return lax.ppermute(value, axis, [(i, i + 1) for i in range(count - 1)])
    return lax.ppermute(value, axis, [(i + 1, i) for i in range(count - 1)])


def per_device(features, voxel_mask, brick_mask, owner, weights, bias):
    extent_x, extent_y, extent_z, channels_in = features.shape
    bricks_x, bricks_y, bricks_z = extent_x // EDGE, extent_y // EDGE, extent_z // EDGE
    count = bricks_x * bricks_y * bricks_z
    groups = lax.axis_size("gy")
    me = lax.axis_index("gy")

    ids = owner.reshape(count)
    active = brick_mask.reshape(count)
    offsets = jnp.arange(groups, dtype=jnp.int32)
    peers = jnp.bitwise_xor(offsets, me)
    match = (ids[None, :] == peers[:, None]).astype(jnp.int32)
    brick_of = jnp.sum(match * jnp.arange(count, dtype=jnp.int32)[None, :], axis=1)
    mine = jnp.sum(match * active[None, :], axis=1)
    known = jnp.sum(jnp.left_shift(active, ids), keepdims=True)
    step = 1
    while step < groups:
        known = jnp.concatenate([known, lax.ppermute(known, "gy", [(i, i ^ step) for i in range(groups)])])
        step *= 2
    theirs = jnp.bitwise_and(jnp.right_shift(known, me), 1)
    lower = peers > me
    cases = jnp.where(lower, mine + 2 * theirs, theirs + 2 * mine)
    packed = jnp.sum(jnp.left_shift(cases[1:], 2 * offsets[:-1]))
    info = jnp.concatenate([brick_of, mine, theirs])

    grown = jnp.repeat(brick_mask, EDGE, axis=0)
    grown = jnp.repeat(grown, EDGE, axis=1)
    grown = jnp.repeat(grown, EDGE, axis=2)
    live = voxel_mask * grown
    live_bf = live.astype(jnp.bfloat16)

    def masked(values, where):
        return (values * where[..., None]).reshape(values.shape[:2] + (bricks_z, EDGE, channels_in))

    x_first = masked(features[:1], live_bf[:1])
    x_last = masked(features[-1:], live_bf[-1:])
    y_first = masked(features[:, :1], live_bf[:, :1])
    y_last = masked(features[:, -1:], live_bf[:, -1:])
    x_low = shift(x_last, "gx", True)
    x_high = shift(x_first, "gx", False)
    y_low = shift(y_last, "gy", True)
    y_high = shift(y_first, "gy", False)
    e_low = shift(jnp.concatenate([x_low[:, -1], x_high[:, -1]]), "gy", True)
    e_high = shift(jnp.concatenate([x_low[:, 0], x_high[:, 0]]), "gy", False)
    main = masked(features, live_bf)

    masks = live.astype(jnp.float32).reshape(bricks_x, EDGE, bricks_y, EDGE, bricks_z, EDGE)
    masks = masks.transpose(0, 2, 4, 1, 3, 5).reshape(count, PAIRS, 2, AREA)
    wide_bias = jnp.concatenate([bias, bias])[None, :]
    operands = (main, x_low, x_high, y_low, y_high, e_low, e_high, paired_weights(weights), masks, wide_bias)

    received = [None] * groups
    brick = convolve(1, info, operands)
    for k in range(1, groups):
        following = (k + 1) % groups
        upward = [(i, i ^ k) for i in range(groups) if i < i ^ k]
        downward = [(b, a) for a, b in upward]

        def exchange(pairs, value, info, *operands):
            got = lax.ppermute(value, "gy", pairs) if pairs else jnp.zeros_like(value)
            return got, convolve(following, info, operands)

        branches = [functools.partial(exchange, pairs) for pairs in ([], upward, downward, upward + downward)]
        case = jnp.bitwise_and(jnp.right_shift(packed, 2 * (k - 1)), 3)
        received[k], brick = lax.switch(case, branches, brick, info, *operands)
    received[0] = brick
    return gather(info, received)[None]


def solution(mesh):
    return jax.shard_map(
        per_device,
        mesh=mesh,
        in_specs=(
            P("gx", "gy", None, None),
            P("gx", "gy", None),
            P("gx", "gy", None),
            P("gx", "gy", None, None),
            P(),
            P(),
        ),
        out_specs=P("gx", "gy", None, None),
        check_vma=False,
    )
```

```python
import functools

import jax
import jax.numpy as jnp
from jax import lax
from jax.experimental import pallas as pl
from jax.experimental.pallas import tpu as pltpu
from jax.sharding import PartitionSpec as P

C = 64
EDGE = 16
AREA = EDGE * EDGE
VOXELS = EDGE**3
PAIRS = EDGE // 2
SPAN = EDGE + 2


def weight_kernel(weights, out):
    cin = weights.shape[-1]
    for b in range(3):
        for j in range(2):
            for c in range(3):
                parts = []
                for t in range(4):
                    a = 2 + j - t
                    tap = weights[(a * 3 + b) * 3 + c] if 0 <= a <= 2 else jnp.zeros(weights.shape[1:], weights.dtype)
                    parts.append(tap.astype(jnp.float32))
                block = jnp.concatenate(parts, axis=0).T
                out[b, (3 * j + c) * cin : (3 * j + c + 1) * cin, :] = block.astype(out.dtype)


def paired_weights(weights):
    cin, cout = weights.shape[3:]
    taps = weights.transpose(0, 1, 2, 4, 3).reshape(27, cout, cin)
    return pl.pallas_call(
        weight_kernel,
        out_shape=jax.ShapeDtypeStruct((3, 6 * cin, 4 * cout), weights.dtype),
        in_specs=[pl.BlockSpec(memory_space=pltpu.VMEM)],
        out_specs=pl.BlockSpec(memory_space=pltpu.VMEM),
        cost_estimate=pl.CostEstimate(flops=0, bytes_accessed=2 << 20, transcendentals=0),
    )(taps)


def conv_kernel(picks, spare, info, main, x_low, x_high, y_low, y_high, e_low, e_high, weights, masks, bias, *refs):
    many = len(picks)
    outs, refs = refs[:many], refs[many + spare :]
    raw, wide, live, stage_a, stage_b, high, result, raw_sems, wide_sem, live_sems, out_sems = refs
    groups = info.shape[0] // 3
    layers = main.shape[2]
    cin = main.shape[-1]
    rows = EDGE + 1
    chunks = [(0, 2)] + [(4 * c + 2, 4) for c in range(PAIRS // 2)]

    def place(brick):
        bz = brick % layers
        return brick // layers, bz, jnp.clip(bz - 1, 0, layers - 3)

    def start(i, brick):
        bx, _, first = place(brick)
        tiles = pl.ds(first, 3)
        for side in range(2):

            @pl.when(bx == side)
            def _():
                for c, (plane, size) in enumerate(chunks):
                    pairs = []
                    if plane <= side * rows < plane + size:
                        end = side * rows
                        pairs.append(((x_low, x_high)[side].at[0, :, tiles], raw.at[i, end, pl.ds(1, EDGE)]))
                        pairs.append((e_low.at[side, tiles], raw.at[i, end, 0]))
                        pairs.append((e_high.at[side, tiles], raw.at[i, end, rows]))
                        size -= 1
                        plane += side == 0
                    planes = pl.ds(plane, size)
                    source = pl.ds(plane - 1 + side * EDGE, size)
                    pairs.append((main.at[source, :, tiles], raw.at[i, planes, pl.ds(1, EDGE)]))
                    pairs.append((y_low.at[source, 0, tiles], raw.at[i, planes, 0]))
                    pairs.append((y_high.at[source, 0, tiles], raw.at[i, planes, rows]))
                    for a, b in pairs:
                        pltpu.make_async_copy(a, b, raw_sems.at[i, c]).start()

    def arrived(i, c, size):
        whole = raw.at[i, pl.ds(0, size)]
        pltpu.make_async_copy(whole, whole, raw_sems.at[i, c]).wait()

    def store(i):
        return pltpu.make_async_copy(result.at[i], outs[i], out_sems.at[i])

    active = [info[groups + k] > 0 for k in picks]
    some = functools.reduce(jnp.logical_or, active)
    load = pltpu.make_async_copy(weights, wide, wide_sem)
    for i, k in enumerate(picks):

        @pl.when(active[i])
        def _():
            start(i, info[k])
            pltpu.make_async_copy(masks.at[info[k]], live.at[i], live_sems.at[i]).start()

        if i == 0:

            @pl.when(some)
            def _():
                load.start()

    @pl.when(some)
    def _():
        load.wait()

    row = lax.broadcasted_iota(jnp.int32, (SPAN, 8, cin), 1)

    @pl.loop(0, many)
    def _(i):
        k = functools.reduce(lambda old, n: jnp.where(i == n, picks[n], old), range(1, many), picks[0])
        brick = info[k]
        _, bz, first = place(brick)
        centre = bz - first
        under = jnp.maximum(centre - 1, 0)
        over = jnp.minimum(centre + 1, 2)
        has_under = (bz > 0).astype(jnp.float32)
        has_over = (bz < layers - 1).astype(jnp.float32)

        def build(stage, pair):
            for j in range(2):
                plane = 2 * pair + j
                same = raw[i, plane, :, centre]
                middle = same.astype(jnp.float32)
                m0, m1 = middle[:, :8], middle[:, 8:]
                below = raw[i, plane, :, under].astype(jnp.float32)[:, 8:] * has_under
                above = raw[i, plane, :, over].astype(jnp.float32)[:, :8] * has_over
                u0 = jnp.where(row == 0, pltpu.roll(below, 1, 1), pltpu.roll(m0, 1, 1))
                u1 = jnp.where(row == 0, pltpu.roll(m0, 1, 1), pltpu.roll(m1, 1, 1))
                d0 = jnp.where(row == 7, pltpu.roll(m1, 7, 1), pltpu.roll(m0, 7, 1))
                d1 = jnp.where(row == 7, pltpu.roll(above, 7, 1), pltpu.roll(m1, 7, 1))
                up = jnp.concatenate([u0, u1], axis=1).astype(jnp.bfloat16)
                down = jnp.concatenate([d0, d1], axis=1).astype(jnp.bfloat16)
                for c, value in enumerate((up, same, down)):
                    stage[:, pl.ds((3 * j + c) * cin, cin)] = value.reshape(SPAN * EDGE, cin)

        def taps(stage, columns):
            total = jnp.dot(stage[0:AREA, :], wide[0, :, columns], preferred_element_type=jnp.float32)
            for b in range(1, 3):
                total += jnp.dot(stage[b * EDGE : b * EDGE + AREA, :], wide[b, :, columns], preferred_element_type=jnp.float32)
            return total

        def emit(q, low):
            value = jnp.maximum(high[...] + low + bias[...], 0.0).T
            mask = live[i, q]
            block = jnp.concatenate([value[:C] * mask[0:1], value[C:] * mask[1:2]], axis=1)
            result[i, :, pl.ds(pl.multiple_of(q * 2 * AREA, 2 * AREA), 2 * AREA)] = block.astype(result.dtype)

        @pl.when(info[groups + k] > 0)
        def _():
            pltpu.make_async_copy(masks.at[brick], live.at[i], live_sems.at[i]).wait()
            high[...] = jnp.zeros_like(high)
            arrived(i, 0, 2)
            build(stage_a, 0)

            @pl.loop(0, PAIRS // 2)
            def _(n):
                arrived(i, n + 1, 4)
                total = taps(stage_a, slice(None))
                build(stage_b, 2 * n + 1)
                emit(jnp.maximum(2 * n - 1, 0), total[:, : 2 * C])
                high[...] = total[:, 2 * C :]
                total = taps(stage_b, slice(None))
                build(stage_a, 2 * n + 2)
                emit(2 * n, total[:, : 2 * C])
                high[...] = total[:, 2 * C :]

            emit(PAIRS - 1, taps(stage_a, slice(0, 2 * C)))
            for n in range(many):

                @pl.when(i == n)
                def _():
                    store(n).start()

    for i in range(many):

        @pl.when(active[i])
        def _():
            store(i).wait()


def convolve(picks, info, operands, spare=0):
    cin = operands[0].shape[-1]
    wide, masks = operands[7:9]
    many = len(picks)
    flops = 2 * (PAIRS + 1) * AREA * 18 * cin * 4 * C * many
    return pl.pallas_call(
        functools.partial(conv_kernel, picks, spare),
        out_shape=[jax.ShapeDtypeStruct((C, VOXELS), jnp.bfloat16)] * (many + spare),
        in_specs=[pl.BlockSpec(memory_space=pltpu.SMEM)]
        + [pl.BlockSpec(memory_space=pl.ANY)] * 9
        + [pl.BlockSpec(memory_space=pltpu.VMEM)],
        out_specs=[pl.BlockSpec(memory_space=pl.ANY)] * (many + spare),
        scratch_shapes=[
            pltpu.VMEM((many, SPAN, SPAN, 3, EDGE, cin), jnp.bfloat16),
            pltpu.VMEM(wide.shape, wide.dtype),
            pltpu.VMEM((many,) + masks.shape[1:], masks.dtype),
            pltpu.VMEM((SPAN * EDGE, 6 * cin), jnp.bfloat16),
            pltpu.VMEM((SPAN * EDGE, 6 * cin), jnp.bfloat16),
            pltpu.VMEM((AREA, 2 * C), jnp.float32),
            pltpu.VMEM((many, C, VOXELS), jnp.bfloat16),
            pltpu.SemaphoreType.DMA((many, 1 + PAIRS // 2)),
            pltpu.SemaphoreType.DMA,
            pltpu.SemaphoreType.DMA((many,)),
            pltpu.SemaphoreType.DMA((many,)),
        ],
        compiler_params=pltpu.CompilerParams(vmem_limit_bytes=24 * 1024 * 1024),
        cost_estimate=pl.CostEstimate(flops=flops, bytes_accessed=8 << 20, transcendentals=0),
    )(info, *operands)


def plan_kernel(count, said, info, packed):
    groups = said.shape[0] // 8
    me = lax.axis_index("gy")

    def distance(k, total):
        peer = me ^ k

        def look(b, found):
            brick, sent, received = found
            here = said[8 * me, b] == peer
            there = said[8 * peer, b] == me
            return (
                jnp.where(here, b, brick),
                jnp.where(here, said[8 * me + 1, b], sent),
                jnp.where(there, said[8 * peer + 1, b], received),
            )

        brick, sent, received = lax.fori_loop(0, count, look, (jnp.int32(0),) * 3)
        info[k] = brick
        info[groups + k] = sent
        info[2 * groups + k] = received
        case = jnp.where(peer > me, sent + 2 * received, received + 2 * sent)
        return total + jnp.where(k > 0, case << (2 * jnp.maximum(k - 1, 0)), 0)

    packed[0] = lax.fori_loop(0, groups, distance, jnp.int32(0))


def plan(said, groups, count):
    return pl.pallas_call(
        functools.partial(plan_kernel, count),
        out_shape=[jax.ShapeDtypeStruct((3 * groups,), jnp.int32), jax.ShapeDtypeStruct((1,), jnp.int32)],
        in_specs=[pl.BlockSpec(memory_space=pltpu.SMEM)],
        out_specs=[pl.BlockSpec(memory_space=pltpu.SMEM)] * 2,
    )(said)


def gather_kernel(info, *refs):
    groups = info.shape[0] // 3
    bricks, (out, held, zero, in_sems, out_sems) = refs[:groups], refs[groups:]
    me = lax.axis_index("gy")

    def load(k):
        return pltpu.make_async_copy(bricks[k], held.at[k], in_sems.at[k])

    def store(k, source):
        return pltpu.make_async_copy(source, out.at[me ^ k], out_sems.at[k])

    full = [info[2 * groups + k] > 0 for k in range(groups)]
    for k in range(groups):

        @pl.when(full[k])
        def _():
            load(k).start()

    zero[...] = jnp.zeros_like(zero)
    for k in range(groups):

        @pl.when(jnp.logical_not(full[k]))
        def _():
            store(k, zero).start()

    for k in range(groups):

        @pl.when(full[k])
        def _():
            load(k).wait()
            store(k, held.at[k]).start()

    for k in range(groups):
        store(k, zero).wait()


def gather(info, bricks):
    groups = len(bricks)
    return pl.pallas_call(
        gather_kernel,
        out_shape=jax.ShapeDtypeStruct((groups, C, VOXELS), jnp.bfloat16),
        in_specs=[pl.BlockSpec(memory_space=pltpu.SMEM)] + [pl.BlockSpec(memory_space=pl.ANY)] * groups,
        out_specs=pl.BlockSpec(memory_space=pl.ANY),
        scratch_shapes=[
            pltpu.VMEM((groups, C, VOXELS), jnp.bfloat16),
            pltpu.VMEM((C, VOXELS), jnp.bfloat16),
            pltpu.SemaphoreType.DMA((groups,)),
            pltpu.SemaphoreType.DMA((groups,)),
        ],
        compiler_params=pltpu.CompilerParams(vmem_limit_bytes=24 * 1024 * 1024),
        cost_estimate=pl.CostEstimate(flops=0, bytes_accessed=8 << 20, transcendentals=0),
    )(info, *bricks)


def shift(value, axis, up):
    count = lax.axis_size(axis)
    if up:
        return lax.ppermute(value, axis, [(i, i + 1) for i in range(count - 1)])
    return lax.ppermute(value, axis, [(i + 1, i) for i in range(count - 1)])


def per_device(features, voxel_mask, brick_mask, owner, weights, bias):
    extent_x, extent_y, extent_z, channels_in = features.shape
    bricks_x, bricks_y, bricks_z = extent_x // EDGE, extent_y // EDGE, extent_z // EDGE
    count = bricks_x * bricks_y * bricks_z
    groups = lax.axis_size("gy")

    said = jnp.stack([owner.reshape(count), brick_mask.reshape(count)])
    said = jnp.pad(said, ((0, 6), (0, 128 - count)))
    said = lax.all_gather(said, "gy", tiled=True)

    grown = jnp.repeat(brick_mask, EDGE, axis=0)
    grown = jnp.repeat(grown, EDGE, axis=1)
    grown = jnp.repeat(grown, EDGE, axis=2)
    live = voxel_mask * grown
    live_bf = live.astype(jnp.bfloat16)

    def masked(values, where):
        return (values * where[..., None]).reshape(values.shape[:2] + (bricks_z, EDGE, channels_in))

    y_first = masked(features[:, :1], live_bf[:, :1])
    y_last = masked(features[:, -1:], live_bf[:, -1:])
    y_low = shift(y_last, "gy", True)
    y_high = shift(y_first, "gy", False)
    x_first = masked(features[:1], live_bf[:1])
    x_last = masked(features[-1:], live_bf[-1:])
    x_low = shift(x_last, "gx", True)
    x_high = shift(x_first, "gx", False)
    e_low = shift(jnp.concatenate([x_low[:, -1], x_high[:, -1]]), "gy", True)
    e_high = shift(jnp.concatenate([x_low[:, 0], x_high[:, 0]]), "gy", False)
    main = masked(features, live_bf)

    masks = live.astype(jnp.float32).reshape(bricks_x, EDGE, bricks_y, EDGE, bricks_z, EDGE)
    masks = masks.transpose(0, 2, 4, 1, 3, 5).reshape(count, PAIRS, 2, AREA)
    wide_bias = jnp.concatenate([bias, bias])[None, :]
    operands = (main, x_low, x_high, y_low, y_high, e_low, e_high, paired_weights(weights), masks, wide_bias)
    info, packed = plan(said, groups, count)
    packed = packed[0]

    far = list(range(groups - 1, groups // 2 - 1, -1))
    near = list(range(groups // 2 - 1, 0, -1))
    received = [None] * groups
    (brick,) = convolve((far[0],), info, operands)
    for n, k in enumerate(far):
        picks = ((near + [0])[n],) + tuple(far[n + 1 : n + 2])
        upward = [(i, i ^ k) for i in range(groups) if i < i ^ k]
        downward = [(b, a) for a, b in upward]

        def exchange(pairs, value, info, *operands):
            if not pairs:
                *made, got = convolve(picks, info, operands, spare=1)
            else:
                got = lax.ppermute(value, "gy", pairs)
                made = convolve(picks, info, operands)
            return got, *made

        branches = [functools.partial(exchange, pairs) for pairs in ([], upward, downward, upward + downward)]
        case = jnp.bitwise_and(jnp.right_shift(packed, 2 * (k - 1)), 3)
        received[k], local, *ahead = lax.switch(case, branches, brick, info, *operands)
        if picks[0]:
            received[picks[0]] = lax.ppermute(local, "gy", [(i, i ^ picks[0]) for i in range(groups)])
        else:
            received[0] = local
        brick = ahead[0] if ahead else None
    return gather(info, received)[None]


def solution(mesh):
    return jax.shard_map(
        per_device,
        mesh=mesh,
        in_specs=(
            P("gx", "gy", None, None),
            P("gx", "gy", None),
            P("gx", "gy", None),
            P("gx", "gy", None, None),
            P(),
            P(),
        ),
        out_specs=P("gx", "gy", None, None),
        check_vma=False,
    )
```

```python
import functools

import jax
import jax.numpy as jnp
from jax import lax
from jax.experimental import pallas as pl
from jax.experimental.pallas import tpu as pltpu
from jax.sharding import PartitionSpec as P

C = 64
EDGE = 16
AREA = EDGE * EDGE
VOXELS = EDGE**3
PAIRS = EDGE // 2
SPAN = EDGE + 2


def activity(voxels, flags, bx):
    layer = lax.broadcasted_iota(jnp.int32, voxels.shape, 2) // EDGE
    chosen = jnp.zeros(voxels.shape, jnp.int32)
    for bz in range(flags.shape[2]):
        chosen = jnp.where(layer == bz, flags[bx, 0, bz], chosen)
    return (voxels * chosen).astype(jnp.float32)


def spread(values, mask):
    n, y, z, c = values.shape
    wide = jnp.broadcast_to(mask[..., None], values.shape).astype(jnp.bfloat16)
    return (values * wide).reshape(n, y, z // EDGE, EDGE, c)


def face_kernel(flags, voxels, features, x_first, x_last, y_first, y_last, x_raw, y_raw, sems):
    rows = features.shape[0]
    sides = (0, rows - 1)
    columns = (0, features.shape[1] - 1)
    copies = [pltpu.make_async_copy(features.at[:, pl.ds(y, 1)], y_raw.at[n], sems.at[n]) for n, y in enumerate(columns)]
    copies += [pltpu.make_async_copy(features.at[pl.ds(x, 1)], x_raw.at[n], sems.at[2 + n]) for n, x in enumerate(sides)]
    for copy in copies:
        copy.start()
    for n, out in enumerate((y_first, y_last)):
        copies[n].wait()
        for bx in range(rows // EDGE):
            span = slice(bx * EDGE, (bx + 1) * EDGE)
            y = columns[n]
            out[span] = spread(y_raw[n, span], activity(voxels[span, y : y + 1], flags, bx))
    for n, out in enumerate((x_first, x_last)):
        copies[2 + n].wait()
        x = sides[n]
        out[...] = spread(x_raw[n], activity(voxels[x : x + 1], flags, x // EDGE))


def faces(brick_mask, voxel_mask, features):
    ex, ey, ez, cin = features.shape
    shapes = [(1, ey, ez // EDGE, EDGE, cin)] * 2 + [(ex, 1, ez // EDGE, EDGE, cin)] * 2
    return pl.pallas_call(
        face_kernel,
        out_shape=[jax.ShapeDtypeStruct(shape, features.dtype) for shape in shapes],
        in_specs=[
            pl.BlockSpec(memory_space=pltpu.SMEM),
            pl.BlockSpec(memory_space=pltpu.VMEM),
            pl.BlockSpec(memory_space=pl.ANY),
        ],
        out_specs=[pl.BlockSpec(memory_space=pltpu.VMEM)] * 4,
        scratch_shapes=[
            pltpu.VMEM((2, 1, ey, ez, cin), features.dtype),
            pltpu.VMEM((2, ex, 1, ez, cin), features.dtype),
            pltpu.SemaphoreType.DMA((4,)),
        ],
        compiler_params=pltpu.CompilerParams(vmem_limit_bytes=24 * 1024 * 1024),
        cost_estimate=pl.CostEstimate(flops=0, bytes_accessed=3 << 20, transcendentals=0),
    )(brick_mask, voxel_mask, features)


SLAB = 8


def prepare_kernel(flags, voxels, features, weights, main, masks, wide):
    step = pl.program_id(0)
    n, y, z = voxels.shape
    mask = activity(voxels[...], flags, step // (EDGE // SLAB))
    main[...] = spread(features[...], mask)

    lanes = masks.shape[1]
    source = lax.broadcasted_iota(jnp.int32, (z, lanes), 0)
    lane = lax.broadcasted_iota(jnp.int32, (z, lanes), 1)
    pick = jnp.logical_and(source // EDGE == lane // AREA, source % EDGE == lane % EDGE)
    every = jnp.dot(
        mask.reshape(n * y, z).astype(jnp.bfloat16),
        jnp.where(pick, 1.0, 0.0).astype(jnp.bfloat16),
        preferred_element_type=jnp.float32,
    ).reshape(n, y, lanes)
    row = lax.broadcasted_iota(jnp.int32, (n, y, lanes), 1)
    column = lax.broadcasted_iota(jnp.int32, (n, y, lanes), 2) % AREA // EDGE
    masks[...] = jnp.sum(jnp.where(row == column, every, 0.0), axis=1)

    @pl.when(step == 0)
    def _():
        cin = weights.shape[-1]
        for b in range(3):
            for j in range(2):
                for c in range(3):
                    parts = []
                    for t in range(4):
                        a = 2 + j - t
                        tap = weights[(a * 3 + b) * 3 + c] if 0 <= a <= 2 else jnp.zeros(weights.shape[1:], weights.dtype)
                        parts.append(tap.astype(jnp.float32))
                    block = jnp.concatenate(parts, axis=0).T
                    wide[b, (3 * j + c) * cin : (3 * j + c + 1) * cin, :] = block.astype(wide.dtype)


def prepare(brick_mask, voxel_mask, features, weights):
    ex, ey, ez, cin = features.shape
    cout = weights.shape[4]
    taps = weights.transpose(0, 1, 2, 4, 3).reshape(27, cout, cin)
    return pl.pallas_call(
        prepare_kernel,
        out_shape=[
            jax.ShapeDtypeStruct((ex, ey, ez // EDGE, EDGE, cin), features.dtype),
            jax.ShapeDtypeStruct((ex, ez // EDGE * AREA), jnp.float32),
            jax.ShapeDtypeStruct((3, 6 * cin, 4 * cout), weights.dtype),
        ],
        grid=(ex // SLAB,),
        in_specs=[
            pl.BlockSpec(memory_space=pltpu.SMEM),
            pl.BlockSpec((SLAB, ey, ez), lambda i: (i, 0, 0)),
            pl.BlockSpec((SLAB, ey, ez, cin), lambda i: (i, 0, 0, 0)),
            pl.BlockSpec((27, cout, cin), lambda i: (0, 0, 0)),
        ],
        out_specs=[
            pl.BlockSpec((SLAB, ey, ez // EDGE, EDGE, cin), lambda i: (i, 0, 0, 0, 0)),
            pl.BlockSpec((SLAB, ez // EDGE * AREA), lambda i: (i, 0)),
            pl.BlockSpec((3, 6 * cin, 4 * cout), lambda i: (0, 0, 0)),
        ],
        compiler_params=pltpu.CompilerParams(vmem_limit_bytes=32 * 1024 * 1024),
        cost_estimate=pl.CostEstimate(flops=0, bytes_accessed=20 << 20, transcendentals=0),
    )(brick_mask, voxel_mask, features, taps)


def conv_kernel(picks, spare, info, main, x_low, x_high, y_low, y_high, e_low, e_high, weights, masks, bias, *refs):
    many = len(picks)
    outs, refs = refs[:many], refs[many + spare :]
    raw, wide, live, stage_a, stage_b, high, result, raw_sems, wide_sem, live_sems, out_sems = refs
    groups = info.shape[0] // 3
    layers = main.shape[2]
    cin = main.shape[-1]
    rows = EDGE + 1
    chunks = [(0, 2)] + [(4 * c + 2, 4) for c in range(PAIRS // 2)]

    def place(brick):
        bz = brick % layers
        return brick // layers, bz, jnp.clip(bz - 1, 0, layers - 3)

    def start(i, brick):
        bx, _, first = place(brick)
        tiles = pl.ds(first, 3)
        for side in range(2):

            @pl.when(bx == side)
            def _():
                for c, (plane, size) in enumerate(chunks):
                    pairs = []
                    if plane <= side * rows < plane + size:
                        end = side * rows
                        pairs.append(((x_low, x_high)[side].at[0, :, tiles], raw.at[i, end, pl.ds(1, EDGE)]))
                        pairs.append((e_low.at[side, tiles], raw.at[i, end, 0]))
                        pairs.append((e_high.at[side, tiles], raw.at[i, end, rows]))
                        size -= 1
                        plane += side == 0
                    planes = pl.ds(plane, size)
                    source = pl.ds(plane - 1 + side * EDGE, size)
                    pairs.append((main.at[source, :, tiles], raw.at[i, planes, pl.ds(1, EDGE)]))
                    pairs.append((y_low.at[source, 0, tiles], raw.at[i, planes, 0]))
                    pairs.append((y_high.at[source, 0, tiles], raw.at[i, planes, rows]))
                    for a, b in pairs:
                        pltpu.make_async_copy(a, b, raw_sems.at[i, c]).start()

    def arrived(i, c, size):
        whole = raw.at[i, pl.ds(0, size)]
        pltpu.make_async_copy(whole, whole, raw_sems.at[i, c]).wait()

    def mask_copy(i, brick):
        bx, bz, _ = place(brick)
        rows = pl.ds(pl.multiple_of(bx * EDGE, EDGE), EDGE)
        lanes = pl.ds(pl.multiple_of(bz * AREA, AREA), AREA)
        return pltpu.make_async_copy(masks.at[rows, lanes], live.at[i], live_sems.at[i])

    def store(i):
        return pltpu.make_async_copy(result.at[i], outs[i], out_sems.at[i])

    active = [info[groups + k] > 0 for k in picks]
    some = functools.reduce(jnp.logical_or, active)
    load = pltpu.make_async_copy(weights, wide, wide_sem)
    for i, k in enumerate(picks):

        @pl.when(active[i])
        def _():
            start(i, info[k])
            mask_copy(i, info[k]).start()

        if i == 0:

            @pl.when(some)
            def _():
                load.start()

    @pl.when(some)
    def _():
        load.wait()

    row = lax.broadcasted_iota(jnp.int32, (SPAN, 8, cin), 1)

    @pl.loop(0, many)
    def _(i):
        k = functools.reduce(lambda old, n: jnp.where(i == n, picks[n], old), range(1, many), picks[0])
        brick = info[k]
        _, bz, first = place(brick)
        centre = bz - first
        under = jnp.maximum(centre - 1, 0)
        over = jnp.minimum(centre + 1, 2)
        has_under = (bz > 0).astype(jnp.float32)
        has_over = (bz < layers - 1).astype(jnp.float32)

        def build(stage, pair):
            for j in range(2):
                plane = 2 * pair + j
                same = raw[i, plane, :, centre]
                middle = same.astype(jnp.float32)
                m0, m1 = middle[:, :8], middle[:, 8:]
                below = raw[i, plane, :, under].astype(jnp.float32)[:, 8:] * has_under
                above = raw[i, plane, :, over].astype(jnp.float32)[:, :8] * has_over
                u0 = jnp.where(row == 0, pltpu.roll(below, 1, 1), pltpu.roll(m0, 1, 1))
                u1 = jnp.where(row == 0, pltpu.roll(m0, 1, 1), pltpu.roll(m1, 1, 1))
                d0 = jnp.where(row == 7, pltpu.roll(m1, 7, 1), pltpu.roll(m0, 7, 1))
                d1 = jnp.where(row == 7, pltpu.roll(above, 7, 1), pltpu.roll(m1, 7, 1))
                up = jnp.concatenate([u0, u1], axis=1).astype(jnp.bfloat16)
                down = jnp.concatenate([d0, d1], axis=1).astype(jnp.bfloat16)
                for c, value in enumerate((up, same, down)):
                    stage[:, pl.ds((3 * j + c) * cin, cin)] = value.reshape(SPAN * EDGE, cin)

        def taps(stage, columns):
            total = jnp.dot(stage[0:AREA, :], wide[0, :, columns], preferred_element_type=jnp.float32)
            for b in range(1, 3):
                total += jnp.dot(stage[b * EDGE : b * EDGE + AREA, :], wide[b, :, columns], preferred_element_type=jnp.float32)
            return total

        def emit(q, low):
            value = jnp.maximum(high[...] + low + bias[...], 0.0).astype(result.dtype).T
            for n in range(2):
                mask = live[i, pl.ds(2 * q + n, 1)].astype(result.dtype)
                lanes = pl.ds(pl.multiple_of((2 * q + n) * AREA, AREA), AREA)
                result[i, :, lanes] = value[n * C : (n + 1) * C] * mask

        @pl.when(info[groups + k] > 0)
        def _():
            mask_copy(i, brick).wait()
            high[...] = jnp.zeros_like(high)
            arrived(i, 0, 2)
            build(stage_a, 0)

            @pl.loop(0, PAIRS // 2)
            def _(n):
                arrived(i, n + 1, 4)
                total = taps(stage_a, slice(None))
                build(stage_b, 2 * n + 1)
                emit(jnp.maximum(2 * n - 1, 0), total[:, : 2 * C])
                high[...] = total[:, 2 * C :]
                total = taps(stage_b, slice(None))
                build(stage_a, 2 * n + 2)
                emit(2 * n, total[:, : 2 * C])
                high[...] = total[:, 2 * C :]

            emit(PAIRS - 1, taps(stage_a, slice(0, 2 * C)))
            for n in range(many):

                @pl.when(i == n)
                def _():
                    store(n).start()

    for i in range(many):

        @pl.when(active[i])
        def _():
            store(i).wait()


def convolve(picks, info, operands, spare=0):
    cin = operands[0].shape[-1]
    wide, masks = operands[7:9]
    many = len(picks)
    flops = 2 * (PAIRS + 1) * AREA * 18 * cin * 4 * C * many
    return pl.pallas_call(
        functools.partial(conv_kernel, picks, spare),
        out_shape=[jax.ShapeDtypeStruct((C, VOXELS), jnp.bfloat16)] * (many + spare),
        in_specs=[pl.BlockSpec(memory_space=pltpu.SMEM)]
        + [pl.BlockSpec(memory_space=pl.ANY)] * 9
        + [pl.BlockSpec(memory_space=pltpu.VMEM)],
        out_specs=[pl.BlockSpec(memory_space=pl.ANY)] * (many + spare),
        scratch_shapes=[
            pltpu.VMEM((many, SPAN, SPAN, 3, EDGE, cin), jnp.bfloat16),
            pltpu.VMEM(wide.shape, wide.dtype),
            pltpu.VMEM((many, EDGE, AREA), masks.dtype),
            pltpu.VMEM((SPAN * EDGE, 6 * cin), jnp.bfloat16),
            pltpu.VMEM((SPAN * EDGE, 6 * cin), jnp.bfloat16),
            pltpu.VMEM((AREA, 2 * C), jnp.float32),
            pltpu.VMEM((many, C, VOXELS), jnp.bfloat16),
            pltpu.SemaphoreType.DMA((many, 1 + PAIRS // 2)),
            pltpu.SemaphoreType.DMA,
            pltpu.SemaphoreType.DMA((many,)),
            pltpu.SemaphoreType.DMA((many,)),
        ],
        compiler_params=pltpu.CompilerParams(vmem_limit_bytes=24 * 1024 * 1024),
        cost_estimate=pl.CostEstimate(flops=flops, bytes_accessed=8 << 20, transcendentals=0),
    )(info, *operands)


def plan_kernel(owner, flags, *refs):
    *words, info, packed = refs
    groups = info.shape[0] // 3
    layers = flags.shape[2]
    me = lax.axis_index("gy")
    for k in range(groups):
        info[k] = 0
    own = jnp.int32(0)
    for b in range(owner.shape[2]):
        target = owner[0, 0, b, 0]
        info[target ^ me] = b
        own = own | (flags[b // layers, 0, b % layers] << target)
    total = jnp.int32(0)
    for k in range(groups):
        word = words[k // 4][k % 4]
        peer = me ^ k
        sent = (own >> peer) & 1
        received = (word >> me) & 1
        info[groups + k] = sent
        info[2 * groups + k] = received
        if k:
            total = total | (jnp.where(peer > me, sent + 2 * received, received + 2 * sent) << (2 * (k - 1)))
    packed[0] = total


def plan(owner, brick_mask, words, groups):
    return pl.pallas_call(
        plan_kernel,
        out_shape=[jax.ShapeDtypeStruct((3 * groups,), jnp.int32), jax.ShapeDtypeStruct((1,), jnp.int32)],
        in_specs=[pl.BlockSpec(memory_space=pltpu.SMEM)] * (2 + len(words)),
        out_specs=[pl.BlockSpec(memory_space=pltpu.SMEM)] * 2,
    )(owner, brick_mask, *words)


def gather_kernel(info, *refs):
    groups = info.shape[0] // 3
    bricks, (out, held, zero, in_sems, out_sems) = refs[:groups], refs[groups:]
    me = lax.axis_index("gy")

    def load(k):
        return pltpu.make_async_copy(bricks[k], held.at[k], in_sems.at[k])

    def store(k, source):
        return pltpu.make_async_copy(source, out.at[me ^ k], out_sems.at[k])

    full = [info[2 * groups + k] > 0 for k in range(groups)]
    for k in range(groups):

        @pl.when(full[k])
        def _():
            load(k).start()

    zero[...] = jnp.zeros_like(zero)
    for k in range(groups):

        @pl.when(jnp.logical_not(full[k]))
        def _():
            store(k, zero).start()

    for k in range(groups):

        @pl.when(full[k])
        def _():
            load(k).wait()
            store(k, held.at[k]).start()

    for k in range(groups):
        store(k, zero).wait()


def gather(info, bricks):
    groups = len(bricks)
    return pl.pallas_call(
        gather_kernel,
        out_shape=jax.ShapeDtypeStruct((groups, C, VOXELS), jnp.bfloat16),
        in_specs=[pl.BlockSpec(memory_space=pltpu.SMEM)] + [pl.BlockSpec(memory_space=pl.ANY)] * groups,
        out_specs=pl.BlockSpec(memory_space=pl.ANY),
        scratch_shapes=[
            pltpu.VMEM((groups, C, VOXELS), jnp.bfloat16),
            pltpu.VMEM((C, VOXELS), jnp.bfloat16),
            pltpu.SemaphoreType.DMA((groups,)),
            pltpu.SemaphoreType.DMA((groups,)),
        ],
        compiler_params=pltpu.CompilerParams(vmem_limit_bytes=24 * 1024 * 1024),
        cost_estimate=pl.CostEstimate(flops=0, bytes_accessed=8 << 20, transcendentals=0),
    )(info, *bricks)


def shift(value, axis, up):
    count = lax.axis_size(axis)
    if up:
        return lax.ppermute(value, axis, [(i, i + 1) for i in range(count - 1)])
    return lax.ppermute(value, axis, [(i + 1, i) for i in range(count - 1)])


def per_device(features, voxel_mask, brick_mask, owner, weights, bias):
    extent_x, extent_y, extent_z, channels_in = features.shape
    bricks_x, bricks_y, bricks_z = extent_x // EDGE, extent_y // EDGE, extent_z // EDGE
    count = bricks_x * bricks_y * bricks_z
    groups = lax.axis_size("gy")

    x_first, x_last, y_first, y_last = faces(brick_mask, voxel_mask, features)
    y_low = shift(y_last, "gy", True)
    y_high = shift(y_first, "gy", False)
    x_low = shift(x_last, "gx", True)
    x_high = shift(x_first, "gx", False)

    def partner(value, k):
        return lax.ppermute(value, "gy", [(i, i ^ k) for i in range(groups)])

    word = jnp.sum(jnp.left_shift(brick_mask.reshape(count), owner.reshape(count)), keepdims=True)
    quad = jnp.concatenate([word] + [partner(word, k) for k in range(1, 4)])
    words = [quad] + [partner(quad, k) for k in range(4, groups, 4)]

    e_low = shift(jnp.concatenate([x_low[:, -1], x_high[:, -1]]), "gy", True)
    e_high = shift(jnp.concatenate([x_low[:, 0], x_high[:, 0]]), "gy", False)
    main, masks, wide = prepare(brick_mask, voxel_mask, features, weights)
    wide_bias = jnp.concatenate([bias, bias])[None, :]
    operands = (main, x_low, x_high, y_low, y_high, e_low, e_high, wide, masks, wide_bias)
    info, packed = plan(owner, brick_mask, words, groups)
    packed = packed[0]

    far = list(range(groups - 1, groups // 2 - 1, -1))
    near = list(range(groups // 2 - 1, 0, -1))
    received = [None] * groups
    (brick,) = convolve((far[0],), info, operands)
    for n, k in enumerate(far):
        picks = ((near + [0])[n],) + tuple(far[n + 1 : n + 2])
        upward = [(i, i ^ k) for i in range(groups) if i < i ^ k]
        downward = [(b, a) for a, b in upward]

        def exchange(pairs, value, info, *operands):
            if not pairs:
                *made, got = convolve(picks, info, operands, spare=1)
            else:
                got = lax.ppermute(value, "gy", pairs)
                made = convolve(picks, info, operands)
            return got, *made

        branches = [functools.partial(exchange, pairs) for pairs in ([], upward, downward, upward + downward)]
        case = jnp.bitwise_and(jnp.right_shift(packed, 2 * (k - 1)), 3)
        received[k], local, *ahead = lax.switch(case, branches, brick, info, *operands)
        if picks[0]:
            received[picks[0]] = partner(local, picks[0])
        else:
            received[0] = local
        brick = ahead[0] if ahead else None
    return gather(info, received)[None]


def solution(mesh):
    return jax.shard_map(
        per_device,
        mesh=mesh,
        in_specs=(
            P("gx", "gy", None, None),
            P("gx", "gy", None),
            P("gx", "gy", None),
            P("gx", "gy", None, None),
            P(),
            P(),
        ),
        out_specs=P("gx", "gy", None, None),
        check_vma=False,
    )
```

```python
import functools

import jax
import jax.numpy as jnp
from jax import lax
from jax.experimental import pallas as pl
from jax.experimental.pallas import tpu as pltpu
from jax.sharding import PartitionSpec as P

C = 64
EDGE = 16
AREA = EDGE * EDGE
VOXELS = EDGE**3
PAIRS = EDGE // 2
SPAN = EDGE + 2
LITTLE = pl.CostEstimate(flops=0, bytes_accessed=1024, transcendentals=0)


def activity(voxels, flags, bx):
    layer = lax.broadcasted_iota(jnp.int32, voxels.shape, 2) // EDGE
    chosen = jnp.zeros(voxels.shape, jnp.int32)
    for bz in range(flags.shape[2]):
        chosen = jnp.where(layer == bz, flags[bx, 0, bz], chosen)
    return (voxels * chosen).astype(jnp.float32)


def spread(values, mask):
    n, y, z, c = values.shape
    wide = jnp.broadcast_to(mask[..., None], values.shape).astype(jnp.bfloat16)
    return (values * wide).reshape(n, y, z // EDGE, EDGE, c)


def face_kernel(flags, owner, voxels, features, x_first, x_last, y_first, y_last, word, v_raw, x_raw, y_raw, sems):
    rows = features.shape[0]
    sides = (0, rows - 1)
    columns = (0, features.shape[1] - 1)
    copies = [pltpu.make_async_copy(voxels, v_raw, sems.at[4])]
    copies += [pltpu.make_async_copy(features.at[:, pl.ds(y, 1)], y_raw.at[n], sems.at[n]) for n, y in enumerate(columns)]
    copies += [pltpu.make_async_copy(features.at[pl.ds(x, 1)], x_raw.at[n], sems.at[2 + n]) for n, x in enumerate(sides)]
    for copy in copies:
        copy.start()
    layers = flags.shape[2]
    bits = jnp.int32(0)
    for b in range(owner.shape[2]):
        bits = bits | (flags[b // layers, 0, b % layers] << owner[0, 0, b, 0])
    word[0] = bits
    for copy in copies:
        copy.wait()
    for n, out in enumerate((y_first, y_last)):
        for bx in range(rows // EDGE):
            span = slice(bx * EDGE, (bx + 1) * EDGE)
            y = columns[n]
            out[span] = spread(y_raw[n, span], activity(v_raw[span, y : y + 1], flags, bx))
    for n, out in enumerate((x_first, x_last)):
        x = sides[n]
        out[...] = spread(x_raw[n], activity(v_raw[x : x + 1], flags, x // EDGE))


def faces(brick_mask, owner, voxel_mask, features):
    ex, ey, ez, cin = features.shape
    layers = ez // EDGE
    shapes = [(1, ey, layers, EDGE, cin)] * 2 + [(ex, 1, layers, EDGE, cin)] * 2
    return pl.pallas_call(
        face_kernel,
        out_shape=[jax.ShapeDtypeStruct(shape, features.dtype) for shape in shapes] + [jax.ShapeDtypeStruct((1,), jnp.int32)],
        in_specs=[pl.BlockSpec(memory_space=pltpu.SMEM)] * 2 + [pl.BlockSpec(memory_space=pltpu.HBM)] * 2,
        out_specs=[pl.BlockSpec(memory_space=pltpu.VMEM)] * 4 + [pl.BlockSpec(memory_space=pltpu.SMEM)],
        scratch_shapes=[
            pltpu.VMEM(voxel_mask.shape, voxel_mask.dtype),
            pltpu.VMEM((2, 1, ey, ez, cin), features.dtype),
            pltpu.VMEM((2, ex, 1, ez, cin), features.dtype),
            pltpu.SemaphoreType.DMA((5,)),
        ],
        compiler_params=pltpu.CompilerParams(vmem_limit_bytes=24 * 1024 * 1024),
        cost_estimate=LITTLE,
    )(brick_mask, owner, *(pltpu.with_memory_space_constraint(a, pltpu.HBM) for a in (voxel_mask, features)))


SLAB = 8


def prepare_kernel(flags, voxels, features, weights, main, masks, wide):
    step = pl.program_id(0)
    n, y, z = voxels.shape
    mask = activity(voxels[...], flags, step // (EDGE // SLAB))
    main[...] = spread(features[...], mask)

    lanes = masks.shape[1]
    source = lax.broadcasted_iota(jnp.int32, (z, lanes), 0)
    lane = lax.broadcasted_iota(jnp.int32, (z, lanes), 1)
    pick = jnp.logical_and(source // EDGE == lane // AREA, source % EDGE == lane % EDGE)
    every = jnp.dot(
        mask.reshape(n * y, z).astype(jnp.bfloat16),
        jnp.where(pick, 1.0, 0.0).astype(jnp.bfloat16),
        preferred_element_type=jnp.float32,
    ).reshape(n, y, lanes)
    row = lax.broadcasted_iota(jnp.int32, (n, y, lanes), 1)
    column = lax.broadcasted_iota(jnp.int32, (n, y, lanes), 2) % AREA // EDGE
    masks[...] = jnp.sum(jnp.where(row == column, every, 0.0), axis=1)

    @pl.when(step == 0)
    def _():
        cin = weights.shape[-1]
        for b in range(3):
            for j in range(2):
                for c in range(3):
                    parts = []
                    for t in range(4):
                        a = 2 + j - t
                        tap = weights[(a * 3 + b) * 3 + c] if 0 <= a <= 2 else jnp.zeros(weights.shape[1:], weights.dtype)
                        parts.append(tap.astype(jnp.float32))
                    block = jnp.concatenate(parts, axis=0).T
                    wide[b, (3 * j + c) * cin : (3 * j + c + 1) * cin, :] = block.astype(wide.dtype)


def prepare(brick_mask, voxel_mask, features, weights):
    ex, ey, ez, cin = features.shape
    cout = weights.shape[4]
    taps = weights.transpose(0, 1, 2, 4, 3).reshape(27, cout, cin)
    return pl.pallas_call(
        prepare_kernel,
        out_shape=[
            jax.ShapeDtypeStruct((ex, ey, ez // EDGE, EDGE, cin), features.dtype),
            jax.ShapeDtypeStruct((ex, ez // EDGE * AREA), jnp.float32),
            jax.ShapeDtypeStruct((3, 6 * cin, 4 * cout), weights.dtype),
        ],
        grid=(ex // SLAB,),
        in_specs=[
            pl.BlockSpec(memory_space=pltpu.SMEM),
            pl.BlockSpec((SLAB, ey, ez), lambda i: (i, 0, 0)),
            pl.BlockSpec((SLAB, ey, ez, cin), lambda i: (i, 0, 0, 0)),
            pl.BlockSpec((27, cout, cin), lambda i: (0, 0, 0)),
        ],
        out_specs=[
            pl.BlockSpec((SLAB, ey, ez // EDGE, EDGE, cin), lambda i: (i, 0, 0, 0, 0)),
            pl.BlockSpec((SLAB, ez // EDGE * AREA), lambda i: (i, 0)),
            pl.BlockSpec((3, 6 * cin, 4 * cout), lambda i: (0, 0, 0)),
        ],
        compiler_params=pltpu.CompilerParams(vmem_limit_bytes=32 * 1024 * 1024),
        cost_estimate=pl.CostEstimate(flops=0, bytes_accessed=40 << 20, transcendentals=0),
    )(brick_mask, voxel_mask, pltpu.with_memory_space_constraint(features, pltpu.HBM), taps)


def conv_kernel(picks, spare, info, main, x_low, x_high, y_low, y_high, e_low, e_high, weights, masks, bias, *refs):
    many = len(picks)
    outs, refs = refs[:many], refs[many + spare :]
    raw, wide, live, stage_a, stage_b, high, result, raw_sems, wide_sem, live_sems, out_sems = refs
    groups = info.shape[0] // 3
    layers = main.shape[2]
    cin = main.shape[-1]
    rows = EDGE + 1
    chunks = ((0, 4), (4, 8), (12, 6))

    def place(brick):
        bz = brick % layers
        return brick // layers, bz, jnp.clip(bz - 1, 0, layers - 3)

    def start(i, brick):
        bx, _, first = place(brick)
        tiles = pl.ds(first, 3)
        for side in range(2):

            @pl.when(bx == side)
            def _():
                for c, (plane, size) in enumerate(chunks):
                    pairs = []
                    if plane <= side * rows < plane + size:
                        end = side * rows
                        pairs.append(((x_low, x_high)[side].at[0, :, tiles], raw.at[i, end, pl.ds(1, EDGE)]))
                        pairs.append((e_low.at[side, tiles], raw.at[i, end, 0]))
                        pairs.append((e_high.at[side, tiles], raw.at[i, end, rows]))
                        size -= 1
                        plane += side == 0
                    planes = pl.ds(plane, size)
                    source = pl.ds(plane - 1 + side * EDGE, size)
                    pairs.append((main.at[source, :, tiles], raw.at[i, planes, pl.ds(1, EDGE)]))
                    pairs.append((y_low.at[source, 0, tiles], raw.at[i, planes, 0]))
                    pairs.append((y_high.at[source, 0, tiles], raw.at[i, planes, rows]))
                    for a, b in pairs:
                        pltpu.make_async_copy(a, b, raw_sems.at[i, c]).start()

    def arrived(i, c):
        whole = raw.at[i, pl.ds(*chunks[c])]
        pltpu.make_async_copy(whole, whole, raw_sems.at[i, c]).wait()

    def mask_copy(i, brick):
        bx, bz, _ = place(brick)
        rows = pl.ds(pl.multiple_of(bx * EDGE, EDGE), EDGE)
        lanes = pl.ds(pl.multiple_of(bz * AREA, AREA), AREA)
        return pltpu.make_async_copy(masks.at[rows, lanes], live.at[i], live_sems.at[i])

    def store(i):
        return pltpu.make_async_copy(result.at[i], outs[i], out_sems.at[i])

    active = [info[groups + k] > 0 for k in picks]
    some = functools.reduce(jnp.logical_or, active)
    filled = [jnp.logical_or(on, k < groups // 2) for on, k in zip(active, picks)]
    load = pltpu.make_async_copy(weights, wide, wide_sem)
    for i, k in enumerate(picks):

        @pl.when(active[i])
        def _():
            start(i, info[k])
            mask_copy(i, info[k]).start()

        if i == 0:

            @pl.when(some)
            def _():
                load.start()

    @pl.when(some)
    def _():
        load.wait()

    row = lax.broadcasted_iota(jnp.int32, (SPAN, 8, cin), 1)

    @pl.loop(0, many)
    def _(i):
        k = functools.reduce(lambda old, n: jnp.where(i == n, picks[n], old), range(1, many), picks[0])
        brick = info[k]
        _, bz, first = place(brick)
        centre = bz - first
        under = jnp.maximum(centre - 1, 0)
        over = jnp.minimum(centre + 1, 2)
        has_under = (bz > 0).astype(jnp.float32)
        has_over = (bz < layers - 1).astype(jnp.float32)

        def build(stage, pair):
            for n in range(4):
                plane = jnp.minimum(2 * pair + n, SPAN - 1)
                same = raw[i, plane, :, centre]
                middle = same.astype(jnp.float32)
                m0, m1 = middle[:, :8], middle[:, 8:]
                below = raw[i, plane, :, under].astype(jnp.float32)[:, 8:] * has_under
                above = raw[i, plane, :, over].astype(jnp.float32)[:, :8] * has_over
                u0 = jnp.where(row == 0, pltpu.roll(below, 1, 1), pltpu.roll(m0, 1, 1))
                u1 = jnp.where(row == 0, pltpu.roll(m0, 1, 1), pltpu.roll(m1, 1, 1))
                d0 = jnp.where(row == 7, pltpu.roll(m1, 7, 1), pltpu.roll(m0, 7, 1))
                d1 = jnp.where(row == 7, pltpu.roll(above, 7, 1), pltpu.roll(m1, 7, 1))
                up = jnp.concatenate([u0, u1], axis=1).astype(jnp.bfloat16)
                down = jnp.concatenate([d0, d1], axis=1).astype(jnp.bfloat16)
                for c, value in enumerate((up, same, down)):
                    stage[n // 2, :, pl.ds((3 * (n % 2) + c) * cin, cin)] = value.reshape(SPAN * EDGE, cin)

        def taps(stage, pairs, columns):
            total = None
            for b in range(3):
                window = stage[0:pairs, b * EDGE : b * EDGE + AREA, :].reshape(pairs * AREA, 6 * cin)
                term = jnp.dot(window, wide[b, :, columns], preferred_element_type=jnp.float32)
                total = term if total is None else total + term
            return total

        def emit(q, value):
            value = jnp.maximum(value + bias[...], 0.0).astype(result.dtype).T
            for n in range(2):
                mask = live[i, pl.ds(2 * q + n, 1)].astype(result.dtype)
                lanes = pl.ds(pl.multiple_of((2 * q + n) * AREA, AREA), AREA)
                result[i, :, lanes] = value[n * C : (n + 1) * C] * mask

        def advance(pair, stage):
            total = taps(stage, 2, slice(None))
            emit(jnp.maximum(pair - 1, 0), high[...] + total[:AREA, : 2 * C])
            emit(pair, total[:AREA, 2 * C :] + total[AREA:, : 2 * C])
            high[...] = total[AREA:, 2 * C :]

        @pl.when(info[groups + k] > 0)
        def _():
            mask_copy(i, brick).wait()
            high[...] = jnp.zeros_like(high)
            arrived(i, 0)
            build(stage_a, 0)

            @pl.loop(0, 2)
            def _(n):
                for c in (1, 2):

                    @pl.when(n == c - 1)
                    def _():
                        arrived(i, c)

                build(stage_b, 4 * n + 2)
                advance(4 * n, stage_a)
                build(stage_a, 4 * n + 4)
                advance(4 * n + 2, stage_b)

            emit(PAIRS - 1, high[...] + taps(stage_a, 1, slice(0, 2 * C)))

        @pl.when(jnp.logical_and(info[groups + k] == 0, k < groups // 2))
        def _():
            result[i] = jnp.zeros(result.shape[1:], result.dtype)

        for n in range(many):

            @pl.when(jnp.logical_and(i == n, filled[n]))
            def _():
                store(n).start()

    for i in range(many):

        @pl.when(filled[i])
        def _():
            store(i).wait()


def convolve(picks, info, operands, spare=0):
    cin = operands[0].shape[-1]
    wide, masks = operands[7:9]
    many = len(picks)
    flops = 2 * (PAIRS + 1) * AREA * 18 * cin * 4 * C * many
    return pl.pallas_call(
        functools.partial(conv_kernel, picks, spare),
        out_shape=[pltpu.VMEM((C, VOXELS), jnp.bfloat16)] * (many + spare),
        in_specs=[pl.BlockSpec(memory_space=pltpu.SMEM)]
        + [pl.BlockSpec(memory_space=pl.ANY)] * 9
        + [pl.BlockSpec(memory_space=pltpu.VMEM)],
        out_specs=[pl.BlockSpec(memory_space=pl.ANY)] * (many + spare),
        scratch_shapes=[
            pltpu.VMEM((many, SPAN, SPAN, 3, EDGE, cin), jnp.bfloat16),
            pltpu.VMEM(wide.shape, wide.dtype),
            pltpu.VMEM((many, EDGE, AREA), masks.dtype),
            pltpu.VMEM((2, SPAN * EDGE, 6 * cin), jnp.bfloat16),
            pltpu.VMEM((2, SPAN * EDGE, 6 * cin), jnp.bfloat16),
            pltpu.VMEM((AREA, 2 * C), jnp.float32),
            pltpu.VMEM((many, C, VOXELS), jnp.bfloat16),
            pltpu.SemaphoreType.DMA((many, 3)),
            pltpu.SemaphoreType.DMA,
            pltpu.SemaphoreType.DMA((many,)),
            pltpu.SemaphoreType.DMA((many,)),
        ],
        compiler_params=pltpu.CompilerParams(vmem_limit_bytes=24 * 1024 * 1024),
        cost_estimate=pl.CostEstimate(flops=flops, bytes_accessed=8 << 20, transcendentals=0),
    )(info, *operands)


def plan_kernel(owner, word, *refs):
    *words, info, packed = refs
    far = len(words)
    groups = 2 * far
    me = lax.axis_index("gy")
    for k in range(groups):
        info[k] = 0
    for b in range(owner.shape[2]):
        info[owner[0, 0, b, 0] ^ me] = b
    total = jnp.int32(0)
    for k in range(groups):
        peer = me ^ k
        sent = (word[0] >> peer) & 1
        received = (words[k - far][0] >> me) & 1 if k >= far else jnp.int32(1)
        info[groups + k] = sent
        info[2 * groups + k] = received
        if k >= far:
            total = total | (jnp.where(peer > me, sent + 2 * received, received + 2 * sent) << (2 * (k - far)))
    packed[0] = total


def plan(owner, words):
    groups = 2 * (len(words) - 1)
    return pl.pallas_call(
        plan_kernel,
        out_shape=[jax.ShapeDtypeStruct((3 * groups,), jnp.int32), jax.ShapeDtypeStruct((1,), jnp.int32)],
        in_specs=[pl.BlockSpec(memory_space=pltpu.SMEM)] * (1 + len(words)),
        out_specs=[pl.BlockSpec(memory_space=pltpu.SMEM)] * 2,
        cost_estimate=LITTLE,
    )(owner, *words)


def gather_kernel(info, *refs):
    groups = info.shape[0] // 3
    bricks, (out, held, zero, in_sems, out_sems) = refs[:groups], refs[groups:]
    me = lax.axis_index("gy")

    def load(k):
        return pltpu.make_async_copy(bricks[k], held.at[k], in_sems.at[k])

    def store(k, source):
        return pltpu.make_async_copy(source, out.at[me ^ k], out_sems.at[k])

    full = [info[2 * groups + k] > 0 for k in range(groups)]
    for k in range(groups):

        @pl.when(full[k])
        def _():
            load(k).start()

    zero[...] = jnp.zeros_like(zero)
    for k in range(groups):

        @pl.when(jnp.logical_not(full[k]))
        def _():
            store(k, zero).start()

    for k in range(groups):

        @pl.when(full[k])
        def _():
            load(k).wait()
            store(k, held.at[k]).start()

    for k in range(groups):
        store(k, zero).wait()


def gather(info, bricks):
    groups = len(bricks)
    return pl.pallas_call(
        gather_kernel,
        out_shape=jax.ShapeDtypeStruct((groups, C, VOXELS), jnp.bfloat16),
        in_specs=[pl.BlockSpec(memory_space=pltpu.SMEM)] + [pl.BlockSpec(memory_space=pl.ANY)] * groups,
        out_specs=pl.BlockSpec(memory_space=pl.ANY),
        scratch_shapes=[
            pltpu.VMEM((groups, C, VOXELS), jnp.bfloat16),
            pltpu.VMEM((C, VOXELS), jnp.bfloat16),
            pltpu.SemaphoreType.DMA((groups,)),
            pltpu.SemaphoreType.DMA((groups,)),
        ],
        compiler_params=pltpu.CompilerParams(vmem_limit_bytes=24 * 1024 * 1024),
        cost_estimate=pl.CostEstimate(flops=0, bytes_accessed=8 << 20, transcendentals=0),
    )(info, *bricks)


def shift(value, axis, up):
    count = lax.axis_size(axis)
    if up:
        return lax.ppermute(value, axis, [(i, i + 1) for i in range(count - 1)])
    return lax.ppermute(value, axis, [(i + 1, i) for i in range(count - 1)])


def per_device(features, voxel_mask, brick_mask, owner, weights, bias):
    extent_x, extent_y, extent_z, channels_in = features.shape
    bricks_x, bricks_y, bricks_z = extent_x // EDGE, extent_y // EDGE, extent_z // EDGE
    count = bricks_x * bricks_y * bricks_z
    groups = lax.axis_size("gy")

    x_first, x_last, y_first, y_last, word = faces(brick_mask, owner, voxel_mask, features)
    y_low = shift(y_last, "gy", True)
    y_high = shift(y_first, "gy", False)
    x_low = shift(x_last, "gx", True)
    x_high = shift(x_first, "gx", False)
    e_low = shift(jnp.concatenate([x_low[:, -1], x_high[:, -1]]), "gy", True)
    e_high = shift(jnp.concatenate([x_low[:, 0], x_high[:, 0]]), "gy", False)

    def partner(value, k):
        return lax.ppermute(value, "gy", [(i, i ^ k) for i in range(groups)])

    words = [word] + [partner(word, k) for k in range(groups // 2, groups)]
    main, masks, wide = prepare(brick_mask, voxel_mask, features, weights)
    wide_bias = jnp.concatenate([bias, bias])[None, :]
    operands = (main, x_low, x_high, y_low, y_high, e_low, e_high, wide, masks, wide_bias)
    info, packed = plan(owner, words)
    packed = packed[0]

    far = list(range(groups - 1, groups // 2 - 1, -1))
    near = list(range(groups // 2 - 1, 0, -1))
    received = [None] * groups
    (brick,) = convolve((far[0],), info, operands)
    for n, k in enumerate(far):
        picks = ((near + [0])[n],) + tuple(far[n + 1 : n + 2])
        upward = [(i, i ^ k) for i in range(groups) if i < i ^ k]
        downward = [(b, a) for a, b in upward]

        def exchange(pairs, value, info, *operands):
            if not pairs:
                *made, got = convolve(picks, info, operands, spare=1)
            else:
                got = lax.ppermute(value, "gy", pairs)
                made = convolve(picks, info, operands)
            return got, *made

        branches = [functools.partial(exchange, pairs) for pairs in ([], upward, downward, upward + downward)]
        case = jnp.bitwise_and(jnp.right_shift(packed, 2 * (k - groups // 2)), 3)
        received[k], local, *ahead = lax.switch(case, branches, brick, info, *operands)
        if picks[0]:
            received[picks[0]] = partner(local, picks[0])
        else:
            received[0] = local
        brick = ahead[0] if ahead else None
    return gather(info, received)[None]


def solution(mesh):
    return jax.shard_map(
        per_device,
        mesh=mesh,
        in_specs=(
            P("gx", "gy", None, None),
            P("gx", "gy", None),
            P("gx", "gy", None),
            P("gx", "gy", None, None),
            P(),
            P(),
        ),
        out_specs=P("gx", "gy", None, None),
        check_vma=False,
    )
```

```python
import functools

import jax
import jax.numpy as jnp
from jax import lax
from jax.experimental import pallas as pl
from jax.experimental.pallas import tpu as pltpu
from jax.sharding import PartitionSpec as P

C = 64
EDGE = 16
AREA = EDGE * EDGE
VOXELS = EDGE**3
PAIRS = EDGE // 2
SPAN = EDGE + 2
LITTLE = pl.CostEstimate(flops=0, bytes_accessed=1024, transcendentals=0)


def activity(voxels, flags, bx):
    layer = lax.broadcasted_iota(jnp.int32, voxels.shape, 2) // EDGE
    chosen = jnp.zeros(voxels.shape, jnp.int32)
    for bz in range(flags.shape[2]):
        chosen = jnp.where(layer == bz, flags[bx, 0, bz], chosen)
    return (voxels * chosen).astype(jnp.float32)


def spread(values, mask):
    n, y, z, c = values.shape
    wide = jnp.broadcast_to(mask[..., None], values.shape).astype(jnp.bfloat16)
    return (values * wide).reshape(n, y, z // EDGE, EDGE, c)


def face_kernel(flags, owner, voxels, features, x_first, x_last, y_first, y_last, word, v_raw, x_raw, y_raw, sems):
    rows = features.shape[0]
    sides = (0, rows - 1)
    columns = (0, features.shape[1] - 1)
    copies = [pltpu.make_async_copy(voxels, v_raw, sems.at[4])]
    copies += [pltpu.make_async_copy(features.at[:, pl.ds(y, 1)], y_raw.at[n], sems.at[n]) for n, y in enumerate(columns)]
    copies += [pltpu.make_async_copy(features.at[pl.ds(x, 1)], x_raw.at[n], sems.at[2 + n]) for n, x in enumerate(sides)]
    for copy in copies:
        copy.start()
    layers = flags.shape[2]
    bits = jnp.int32(0)
    for b in range(owner.shape[0]):
        bits = bits | (flags[b // layers, 0, b % layers] << owner[b])
    word[0] = bits
    for copy in copies:
        copy.wait()
    for n, out in enumerate((y_first, y_last)):
        for bx in range(rows // EDGE):
            span = slice(bx * EDGE, (bx + 1) * EDGE)
            y = columns[n]
            out[span] = spread(y_raw[n, span], activity(v_raw[span, y : y + 1], flags, bx))
    for n, out in enumerate((x_first, x_last)):
        x = sides[n]
        out[...] = spread(x_raw[n], activity(v_raw[x : x + 1], flags, x // EDGE))


def faces(brick_mask, owner, voxel_mask, features):
    ex, ey, ez, cin = features.shape
    layers = ez // EDGE
    shapes = [(1, ey, layers, EDGE, cin)] * 2 + [(ex, 1, layers, EDGE, cin)] * 2
    return pl.pallas_call(
        face_kernel,
        out_shape=[jax.ShapeDtypeStruct(shape, features.dtype) for shape in shapes] + [jax.ShapeDtypeStruct((1,), jnp.int32)],
        in_specs=[pl.BlockSpec(memory_space=pltpu.SMEM)] * 2 + [pl.BlockSpec(memory_space=pltpu.HBM)] * 2,
        out_specs=[pl.BlockSpec(memory_space=pltpu.VMEM)] * 4 + [pl.BlockSpec(memory_space=pltpu.SMEM)],
        scratch_shapes=[
            pltpu.VMEM(voxel_mask.shape, voxel_mask.dtype),
            pltpu.VMEM((2, 1, ey, ez, cin), features.dtype),
            pltpu.VMEM((2, ex, 1, ez, cin), features.dtype),
            pltpu.SemaphoreType.DMA((5,)),
        ],
        compiler_params=pltpu.CompilerParams(vmem_limit_bytes=24 * 1024 * 1024),
        cost_estimate=LITTLE,
    )(brick_mask, owner, *(pltpu.with_memory_space_constraint(a, pltpu.HBM) for a in (voxel_mask, features)))


SLAB = 8


def plan(owner, word, words, info, packed):
    far = len(words)
    groups = 2 * far
    me = lax.axis_index("gy")
    for k in range(groups):
        info[k] = 0
    for b in range(owner.shape[0]):
        info[owner[b] ^ me] = b
    total = jnp.int32(0)
    for k in range(groups):
        peer = me ^ k
        sent = (word[0] >> peer) & 1
        received = (words[k - far][0] >> me) & 1 if k >= far else jnp.int32(1)
        info[groups + k] = sent
        info[2 * groups + k] = received
        if k >= far:
            total = total | (jnp.where(peer > me, sent + 2 * received, received + 2 * sent) << (2 * (k - far)))
    packed[0] = total


def prepare_kernel(flags, owner, word, *refs):
    *words, voxels, features, weights, main, masks, wide, info, packed = refs
    step = pl.program_id(0)
    n, y, z = voxels.shape
    mask = activity(voxels[...], flags, step // (EDGE // SLAB))
    main[...] = spread(features[...], mask)

    lanes = masks.shape[1]
    source = lax.broadcasted_iota(jnp.int32, (z, lanes), 0)
    lane = lax.broadcasted_iota(jnp.int32, (z, lanes), 1)
    pick = jnp.logical_and(source // EDGE == lane // AREA, source % EDGE == lane % EDGE)
    every = jnp.dot(
        mask.reshape(n * y, z).astype(jnp.bfloat16),
        jnp.where(pick, 1.0, 0.0).astype(jnp.bfloat16),
        preferred_element_type=jnp.float32,
    ).reshape(n, y, lanes)
    row = lax.broadcasted_iota(jnp.int32, (n, y, lanes), 1)
    column = lax.broadcasted_iota(jnp.int32, (n, y, lanes), 2) % AREA // EDGE
    masks[...] = jnp.sum(jnp.where(row == column, every, 0.0), axis=1)

    @pl.when(step == 0)
    def _():
        plan(owner, word, words, info, packed)
        cin = weights.shape[-1]
        for b in range(3):
            for j in range(2):
                for c in range(3):
                    parts = []
                    for t in range(4):
                        a = 2 + j - t
                        tap = weights[(a * 3 + b) * 3 + c] if 0 <= a <= 2 else jnp.zeros(weights.shape[1:], weights.dtype)
                        parts.append(tap.astype(jnp.float32))
                    block = jnp.concatenate(parts, axis=0).T
                    wide[b, (3 * j + c) * cin : (3 * j + c + 1) * cin, :] = block.astype(wide.dtype)


def prepare(brick_mask, owner, words, voxel_mask, features, weights):
    ex, ey, ez, cin = features.shape
    groups = 2 * (len(words) - 1)
    cout = weights.shape[4]
    taps = weights.transpose(0, 1, 2, 4, 3).reshape(27, cout, cin)
    return pl.pallas_call(
        prepare_kernel,
        out_shape=[
            jax.ShapeDtypeStruct((ex, ey, ez // EDGE, EDGE, cin), features.dtype),
            jax.ShapeDtypeStruct((ex, ez // EDGE * AREA), jnp.float32),
            jax.ShapeDtypeStruct((3, 6 * cin, 4 * cout), weights.dtype),
            jax.ShapeDtypeStruct((3 * groups,), jnp.int32),
            jax.ShapeDtypeStruct((1,), jnp.int32),
        ],
        grid=(ex // SLAB,),
        in_specs=[pl.BlockSpec(memory_space=pltpu.SMEM)] * (2 + len(words))
        + [
            pl.BlockSpec((SLAB, ey, ez), lambda i: (i, 0, 0)),
            pl.BlockSpec((SLAB, ey, ez, cin), lambda i: (i, 0, 0, 0)),
            pl.BlockSpec((27, cout, cin), lambda i: (0, 0, 0)),
        ],
        out_specs=[
            pl.BlockSpec((SLAB, ey, ez // EDGE, EDGE, cin), lambda i: (i, 0, 0, 0, 0)),
            pl.BlockSpec((SLAB, ez // EDGE * AREA), lambda i: (i, 0)),
            pl.BlockSpec((3, 6 * cin, 4 * cout), lambda i: (0, 0, 0)),
            pl.BlockSpec(memory_space=pltpu.SMEM),
            pl.BlockSpec(memory_space=pltpu.SMEM),
        ],
        compiler_params=pltpu.CompilerParams(vmem_limit_bytes=32 * 1024 * 1024),
        cost_estimate=pl.CostEstimate(flops=0, bytes_accessed=40 << 20, transcendentals=0),
    )(brick_mask, owner, *words, voxel_mask, pltpu.with_memory_space_constraint(features, pltpu.HBM), taps)


def conv_kernel(picks, spare, info, main, x_low, x_high, y_low, y_high, e_low, e_high, weights, masks, bias, *refs):
    many = len(picks)
    outs, refs = refs[:many], refs[many + spare :]
    raw, wide, live, stage_a, stage_b, high, result, raw_sems, wide_sem, live_sems, out_sems = refs
    groups = info.shape[0] // 3
    layers = main.shape[2]
    cin = main.shape[-1]
    rows = EDGE + 1
    chunks = ((0, 4), (4, 8), (12, 6))

    def place(brick):
        bz = brick % layers
        return brick // layers, bz, jnp.clip(bz - 1, 0, layers - 3)

    def start(i, brick):
        bx, _, first = place(brick)
        tiles = pl.ds(first, 3)
        for side in range(2):

            @pl.when(bx == side)
            def _():
                for c, (plane, size) in enumerate(chunks):
                    pairs = []
                    if plane <= side * rows < plane + size:
                        end = side * rows
                        pairs.append(((x_low, x_high)[side].at[0, :, tiles], raw.at[i, end, pl.ds(1, EDGE)]))
                        pairs.append((e_low.at[side, tiles], raw.at[i, end, 0]))
                        pairs.append((e_high.at[side, tiles], raw.at[i, end, rows]))
                        size -= 1
                        plane += side == 0
                    planes = pl.ds(plane, size)
                    source = pl.ds(plane - 1 + side * EDGE, size)
                    pairs.append((main.at[source, :, tiles], raw.at[i, planes, pl.ds(1, EDGE)]))
                    pairs.append((y_low.at[source, 0, tiles], raw.at[i, planes, 0]))
                    pairs.append((y_high.at[source, 0, tiles], raw.at[i, planes, rows]))
                    for a, b in pairs:
                        pltpu.make_async_copy(a, b, raw_sems.at[i, c]).start()

    def arrived(i, c):
        whole = raw.at[i, pl.ds(*chunks[c])]
        pltpu.make_async_copy(whole, whole, raw_sems.at[i, c]).wait()

    def mask_copy(i, brick):
        bx, bz, _ = place(brick)
        rows = pl.ds(pl.multiple_of(bx * EDGE, EDGE), EDGE)
        lanes = pl.ds(pl.multiple_of(bz * AREA, AREA), AREA)
        return pltpu.make_async_copy(masks.at[rows, lanes], live.at[i], live_sems.at[i])

    def store(i):
        return pltpu.make_async_copy(result.at[i], outs[i], out_sems.at[i])

    active = [info[groups + k] > 0 for k in picks]
    some = functools.reduce(jnp.logical_or, active)
    filled = [jnp.logical_or(on, k < groups // 2) for on, k in zip(active, picks)]
    load = pltpu.make_async_copy(weights, wide, wide_sem)
    for i, k in enumerate(picks):

        @pl.when(active[i])
        def _():
            start(i, info[k])
            mask_copy(i, info[k]).start()

        if i == 0:

            @pl.when(some)
            def _():
                load.start()

    @pl.when(some)
    def _():
        load.wait()

    row = lax.broadcasted_iota(jnp.int32, (SPAN, 8, cin), 1)

    @pl.loop(0, many)
    def _(i):
        k = functools.reduce(lambda old, n: jnp.where(i == n, picks[n], old), range(1, many), picks[0])
        brick = info[k]
        _, bz, first = place(brick)
        centre = bz - first
        under = jnp.maximum(centre - 1, 0)
        over = jnp.minimum(centre + 1, 2)
        has_under = (bz > 0).astype(jnp.float32)
        has_over = (bz < layers - 1).astype(jnp.float32)

        def build(stage, pair):
            for n in range(4):
                plane = jnp.minimum(2 * pair + n, SPAN - 1)
                same = raw[i, plane, :, centre]
                middle = same.astype(jnp.float32)
                m0, m1 = middle[:, :8], middle[:, 8:]
                below = raw[i, plane, :, under].astype(jnp.float32)[:, 8:] * has_under
                above = raw[i, plane, :, over].astype(jnp.float32)[:, :8] * has_over
                u0 = jnp.where(row == 0, pltpu.roll(below, 1, 1), pltpu.roll(m0, 1, 1))
                u1 = jnp.where(row == 0, pltpu.roll(m0, 1, 1), pltpu.roll(m1, 1, 1))
                d0 = jnp.where(row == 7, pltpu.roll(m1, 7, 1), pltpu.roll(m0, 7, 1))
                d1 = jnp.where(row == 7, pltpu.roll(above, 7, 1), pltpu.roll(m1, 7, 1))
                up = jnp.concatenate([u0, u1], axis=1).astype(jnp.bfloat16)
                down = jnp.concatenate([d0, d1], axis=1).astype(jnp.bfloat16)
                for c, value in enumerate((up, same, down)):
                    stage[n // 2, :, pl.ds((3 * (n % 2) + c) * cin, cin)] = value.reshape(SPAN * EDGE, cin)

        def taps(stage, pairs, columns):
            total = None
            for b in range(3):
                window = stage[0:pairs, b * EDGE : b * EDGE + AREA, :].reshape(pairs * AREA, 6 * cin)
                term = jnp.dot(window, wide[b, :, columns], preferred_element_type=jnp.float32)
                total = term if total is None else total + term
            return total

        def emit(q, value):
            value = jnp.maximum(value + bias[...], 0.0).astype(result.dtype).T
            for n in range(2):
                mask = live[i, pl.ds(2 * q + n, 1)].astype(result.dtype)
                lanes = pl.ds(pl.multiple_of((2 * q + n) * AREA, AREA), AREA)
                result[i, :, lanes] = value[n * C : (n + 1) * C] * mask

        def advance(pair, stage):
            total = taps(stage, 2, slice(None))
            emit(jnp.maximum(pair - 1, 0), high[...] + total[:AREA, : 2 * C])
            emit(pair, total[:AREA, 2 * C :] + total[AREA:, : 2 * C])
            high[...] = total[AREA:, 2 * C :]

        @pl.when(info[groups + k] > 0)
        def _():
            mask_copy(i, brick).wait()
            high[...] = jnp.zeros_like(high)
            arrived(i, 0)
            build(stage_a, 0)

            @pl.loop(0, 2)
            def _(n):
                for c in (1, 2):

                    @pl.when(n == c - 1)
                    def _():
                        arrived(i, c)

                build(stage_b, 4 * n + 2)
                advance(4 * n, stage_a)
                build(stage_a, 4 * n + 4)
                advance(4 * n + 2, stage_b)

            emit(PAIRS - 1, high[...] + taps(stage_a, 1, slice(0, 2 * C)))

        @pl.when(jnp.logical_and(info[groups + k] == 0, k < groups // 2))
        def _():
            result[i] = jnp.zeros(result.shape[1:], result.dtype)

        for n in range(many):

            @pl.when(jnp.logical_and(i == n, filled[n]))
            def _():
                store(n).start()

    for i in range(many):

        @pl.when(filled[i])
        def _():
            store(i).wait()


def convolve(picks, info, operands, spare=0):
    cin = operands[0].shape[-1]
    wide, masks = operands[7:9]
    many = len(picks)
    flops = 2 * (PAIRS + 1) * AREA * 18 * cin * 4 * C * many
    return pl.pallas_call(
        functools.partial(conv_kernel, picks, spare),
        out_shape=[pltpu.VMEM((C, VOXELS), jnp.bfloat16)] * (many + spare),
        in_specs=[pl.BlockSpec(memory_space=pltpu.SMEM)]
        + [pl.BlockSpec(memory_space=pl.ANY)] * 9
        + [pl.BlockSpec(memory_space=pltpu.VMEM)],
        out_specs=[pl.BlockSpec(memory_space=pl.ANY)] * (many + spare),
        scratch_shapes=[
            pltpu.VMEM((many, SPAN, SPAN, 3, EDGE, cin), jnp.bfloat16),
            pltpu.VMEM(wide.shape, wide.dtype),
            pltpu.VMEM((many, EDGE, AREA), masks.dtype),
            pltpu.VMEM((2, SPAN * EDGE, 6 * cin), jnp.bfloat16),
            pltpu.VMEM((2, SPAN * EDGE, 6 * cin), jnp.bfloat16),
            pltpu.VMEM((AREA, 2 * C), jnp.float32),
            pltpu.VMEM((many, C, VOXELS), jnp.bfloat16),
            pltpu.SemaphoreType.DMA((many, 3)),
            pltpu.SemaphoreType.DMA,
            pltpu.SemaphoreType.DMA((many,)),
            pltpu.SemaphoreType.DMA((many,)),
        ],
        compiler_params=pltpu.CompilerParams(vmem_limit_bytes=54 * 1024 * 1024),
        cost_estimate=pl.CostEstimate(flops=flops, bytes_accessed=8 << 20, transcendentals=0),
    )(info, *operands)


def gather_kernel(info, *refs):
    groups = info.shape[0] // 3
    bricks, (out, held, zero, in_sems, out_sems) = refs[:groups], refs[groups:]
    me = lax.axis_index("gy")

    def load(k):
        return pltpu.make_async_copy(bricks[k], held.at[k], in_sems.at[k])

    def store(k, source):
        return pltpu.make_async_copy(source, out.at[me ^ k], out_sems.at[k])

    full = [info[2 * groups + k] > 0 for k in range(groups)]
    for k in range(groups):

        @pl.when(full[k])
        def _():
            load(k).start()

    zero[...] = jnp.zeros_like(zero)
    for k in range(groups):

        @pl.when(jnp.logical_not(full[k]))
        def _():
            store(k, zero).start()

    for k in range(groups):

        @pl.when(full[k])
        def _():
            load(k).wait()
            store(k, held.at[k]).start()

    for k in range(groups):
        store(k, zero).wait()


def gather(info, bricks):
    groups = len(bricks)
    return pl.pallas_call(
        gather_kernel,
        out_shape=jax.ShapeDtypeStruct((groups, C, VOXELS), jnp.bfloat16),
        in_specs=[pl.BlockSpec(memory_space=pltpu.SMEM)] + [pl.BlockSpec(memory_space=pl.ANY)] * groups,
        out_specs=pl.BlockSpec(memory_space=pl.ANY),
        scratch_shapes=[
            pltpu.VMEM((groups, C, VOXELS), jnp.bfloat16),
            pltpu.VMEM((C, VOXELS), jnp.bfloat16),
            pltpu.SemaphoreType.DMA((groups,)),
            pltpu.SemaphoreType.DMA((groups,)),
        ],
        compiler_params=pltpu.CompilerParams(vmem_limit_bytes=24 * 1024 * 1024),
        cost_estimate=pl.CostEstimate(flops=0, bytes_accessed=8 << 20, transcendentals=0),
    )(info, *bricks)


def shift(value, axis, up):
    count = lax.axis_size(axis)
    if up:
        return lax.ppermute(value, axis, [(i, i + 1) for i in range(count - 1)])
    return lax.ppermute(value, axis, [(i + 1, i) for i in range(count - 1)])


def per_device(features, voxel_mask, brick_mask, owner, weights, bias):
    extent_x, extent_y, extent_z, channels_in = features.shape
    bricks_x, bricks_y, bricks_z = extent_x // EDGE, extent_y // EDGE, extent_z // EDGE
    count = bricks_x * bricks_y * bricks_z
    groups = lax.axis_size("gy")
    owner = owner.reshape(count)

    x_first, x_last, y_first, y_last, word = faces(brick_mask, owner, voxel_mask, features)
    y_low = shift(y_last, "gy", True)
    y_high = shift(y_first, "gy", False)
    x_low = shift(x_last, "gx", True)
    x_high = shift(x_first, "gx", False)
    e_low = shift(jnp.concatenate([x_low[:, -1], x_high[:, -1]]), "gy", True)
    e_high = shift(jnp.concatenate([x_low[:, 0], x_high[:, 0]]), "gy", False)

    def partner(value, k):
        return lax.ppermute(value, "gy", [(i, i ^ k) for i in range(groups)])

    words = [word] + [partner(word, k) for k in range(groups // 2, groups)]
    main, masks, wide, info, packed = prepare(brick_mask, owner, words, voxel_mask, features, weights)
    wide_bias = jnp.concatenate([bias, bias])[None, :]
    operands = (main, x_low, x_high, y_low, y_high, e_low, e_high, wide, masks, wide_bias)
    packed = packed[0]

    far = list(range(groups - 1, groups // 2 - 1, -1))
    near = list(range(groups // 2 - 1, 0, -1))
    received = [None] * groups
    (brick,) = convolve((far[0],), info, operands)
    for n, k in enumerate(far):
        picks = ((near + [0])[n],) + tuple(far[n + 1 : n + 2])
        upward = [(i, i ^ k) for i in range(groups) if i < i ^ k]
        downward = [(b, a) for a, b in upward]

        def exchange(pairs, value, info, *operands):
            if not pairs:
                *made, got = convolve(picks, info, operands, spare=1)
            else:
                got = lax.ppermute(value, "gy", pairs)
                made = convolve(picks, info, operands)
            return got, *made

        branches = [functools.partial(exchange, pairs) for pairs in ([], upward, downward, upward + downward)]
        case = jnp.bitwise_and(jnp.right_shift(packed, 2 * (k - groups // 2)), 3)
        received[k], local, *ahead = lax.switch(case, branches, brick, info, *operands)
        if picks[0]:
            received[picks[0]] = partner(local, picks[0])
        else:
            received[0] = local
        brick = ahead[0] if ahead else None
    return gather(info, received)[None]


def solution(mesh):
    return jax.shard_map(
        per_device,
        mesh=mesh,
        in_specs=(
            P("gx", "gy", None, None),
            P("gx", "gy", None),
            P("gx", "gy", None),
            P("gx", "gy", None, None),
            P(),
            P(),
        ),
        out_specs=P("gx", "gy", None, None),
        check_vma=False,
    )
```

```python
import functools

import jax
import jax.numpy as jnp
from jax import lax
from jax.experimental import pallas as pl
from jax.experimental.pallas import tpu as pltpu
from jax.sharding import PartitionSpec as P

C = 64
EDGE = 16
AREA = EDGE * EDGE
VOXELS = EDGE**3
PAIRS = EDGE // 2
SPAN = EDGE + 2
LITTLE = pl.CostEstimate(flops=0, bytes_accessed=1024, transcendentals=0)


def activity(voxels, flags, bx):
    layer = lax.broadcasted_iota(jnp.int32, voxels.shape, 2) // EDGE
    chosen = jnp.zeros(voxels.shape, jnp.int32)
    for bz in range(flags.shape[2]):
        chosen = jnp.where(layer == bz, flags[bx, 0, bz], chosen)
    return (voxels * chosen).astype(jnp.float32)


def spread(values, mask):
    n, y, z, c = values.shape
    wide = jnp.broadcast_to(mask[..., None], values.shape).astype(jnp.bfloat16)
    return (values * wide).reshape(n, y, z // EDGE, EDGE, c)


def sends_kernel(flags, owner, sends):
    layers = flags.shape[2]
    for o in range(sends.shape[0]):
        sends[o] = 0
    for b in range(owner.shape[0]):
        sends[owner[b]] = flags[b // layers, 0, b % layers]


def sends_of(brick_mask, owner, groups):
    return pl.pallas_call(
        sends_kernel,
        out_shape=jax.ShapeDtypeStruct((groups,), jnp.int32),
        in_specs=[pl.BlockSpec(memory_space=pltpu.SMEM)] * 2,
        out_specs=pl.BlockSpec(memory_space=pltpu.SMEM),
        cost_estimate=LITTLE,
    )(brick_mask, owner)


def plan(owner, sends, receives, info, packed):
    groups = sends.shape[0]
    far = groups // 2
    me = lax.axis_index("gy")
    for k in range(groups):
        info[k] = 0
    for b in range(owner.shape[0]):
        info[owner[b] ^ me] = b
    total = jnp.int32(0)
    for k in range(groups):
        peer = me ^ k
        sent = sends[peer]
        info[groups + k] = sent
        info[2 * groups + k] = receives[peer] if k >= far else 1
        if k >= far:
            received = receives[peer]
            total = total | (jnp.where(peer > me, sent + 2 * received, received + 2 * sent) << (2 * (k - far)))
    packed[0] = total


def face_kernel(flags, owner, sends, receives, voxels, features, x_first, x_last, y_first, y_last, info, packed, v_raw, x_raw, y_raw, sems):
    rows = features.shape[0]
    sides = (0, rows - 1)
    columns = (0, features.shape[1] - 1)
    copies = [pltpu.make_async_copy(voxels, v_raw, sems.at[4])]
    copies += [pltpu.make_async_copy(features.at[:, pl.ds(y, 1)], y_raw.at[n], sems.at[n]) for n, y in enumerate(columns)]
    copies += [pltpu.make_async_copy(features.at[pl.ds(x, 1)], x_raw.at[n], sems.at[2 + n]) for n, x in enumerate(sides)]
    for copy in copies:
        copy.start()
    plan(owner, sends, receives, info, packed)
    for copy in copies:
        copy.wait()
    for n, out in enumerate((y_first, y_last)):
        for bx in range(rows // EDGE):
            span = slice(bx * EDGE, (bx + 1) * EDGE)
            y = columns[n]
            out[span] = spread(y_raw[n, span], activity(v_raw[span, y : y + 1], flags, bx))
    for n, out in enumerate((x_first, x_last)):
        x = sides[n]
        out[...] = spread(x_raw[n], activity(v_raw[x : x + 1], flags, x // EDGE))


def faces(brick_mask, owner, sends, receives, voxel_mask, features):
    groups = sends.shape[0]
    ex, ey, ez, cin = features.shape
    layers = ez // EDGE
    shapes = [(1, ey, layers, EDGE, cin)] * 2 + [(ex, 1, layers, EDGE, cin)] * 2
    return pl.pallas_call(
        face_kernel,
        out_shape=[jax.ShapeDtypeStruct(shape, features.dtype) for shape in shapes] + [jax.ShapeDtypeStruct((n,), jnp.int32) for n in (3 * groups, 1)],
        in_specs=[pl.BlockSpec(memory_space=pltpu.SMEM)] * 4 + [pl.BlockSpec(memory_space=pltpu.HBM)] * 2,
        out_specs=[pl.BlockSpec(memory_space=pltpu.VMEM)] * 4 + [pl.BlockSpec(memory_space=pltpu.SMEM)] * 2,
        scratch_shapes=[
            pltpu.VMEM(voxel_mask.shape, voxel_mask.dtype),
            pltpu.VMEM((2, 1, ey, ez, cin), features.dtype),
            pltpu.VMEM((2, ex, 1, ez, cin), features.dtype),
            pltpu.SemaphoreType.DMA((5,)),
        ],
        compiler_params=pltpu.CompilerParams(vmem_limit_bytes=24 * 1024 * 1024),
        cost_estimate=LITTLE,
    )(brick_mask, owner, sends, receives, *(pltpu.with_memory_space_constraint(a, pltpu.HBM) for a in (voxel_mask, features)))


SLAB = 8


def prepare_kernel(flags, voxels, features, weights, main, masks, wide):
    step = pl.program_id(0)
    n, y, z = voxels.shape
    mask = activity(voxels[...], flags, step // (EDGE // SLAB))
    main[...] = spread(features[...], mask)

    lanes = masks.shape[1]
    source = lax.broadcasted_iota(jnp.int32, (z, lanes), 0)
    lane = lax.broadcasted_iota(jnp.int32, (z, lanes), 1)
    pick = jnp.logical_and(source // EDGE == lane // AREA, source % EDGE == lane % EDGE)
    every = jnp.dot(
        mask.reshape(n * y, z).astype(jnp.bfloat16),
        jnp.where(pick, 1.0, 0.0).astype(jnp.bfloat16),
        preferred_element_type=jnp.float32,
    ).reshape(n, y, lanes)
    row = lax.broadcasted_iota(jnp.int32, (n, y, lanes), 1)
    column = lax.broadcasted_iota(jnp.int32, (n, y, lanes), 2) % AREA // EDGE
    masks[...] = jnp.sum(jnp.where(row == column, every, 0.0), axis=1)

    @pl.when(step == 0)
    def _():
        cin = weights.shape[-1]
        for b in range(3):
            for j in range(2):
                for c in range(3):
                    parts = []
                    for t in range(4):
                        a = 2 + j - t
                        tap = weights[(a * 3 + b) * 3 + c] if 0 <= a <= 2 else jnp.zeros(weights.shape[1:], weights.dtype)
                        parts.append(tap.astype(jnp.float32))
                    block = jnp.concatenate(parts, axis=0).T
                    wide[b, (3 * j + c) * cin : (3 * j + c + 1) * cin, :] = block.astype(wide.dtype)


def prepare(brick_mask, voxel_mask, features, weights):
    ex, ey, ez, cin = features.shape
    cout = weights.shape[4]
    taps = weights.transpose(0, 1, 2, 4, 3).reshape(27, cout, cin)
    return pl.pallas_call(
        prepare_kernel,
        out_shape=[
            jax.ShapeDtypeStruct((ex, ey, ez // EDGE, EDGE, cin), features.dtype),
            jax.ShapeDtypeStruct((ex, ez // EDGE * AREA), jnp.float32),
            jax.ShapeDtypeStruct((3, 6 * cin, 4 * cout), weights.dtype),
        ],
        grid=(ex // SLAB,),
        in_specs=[
            pl.BlockSpec(memory_space=pltpu.SMEM),
            pl.BlockSpec((SLAB, ey, ez), lambda i: (i, 0, 0)),
            pl.BlockSpec((SLAB, ey, ez, cin), lambda i: (i, 0, 0, 0)),
            pl.BlockSpec((27, cout, cin), lambda i: (0, 0, 0)),
        ],
        out_specs=[
            pl.BlockSpec((SLAB, ey, ez // EDGE, EDGE, cin), lambda i: (i, 0, 0, 0, 0)),
            pl.BlockSpec((SLAB, ez // EDGE * AREA), lambda i: (i, 0)),
            pl.BlockSpec((3, 6 * cin, 4 * cout), lambda i: (0, 0, 0)),
        ],
        compiler_params=pltpu.CompilerParams(vmem_limit_bytes=32 * 1024 * 1024),
        cost_estimate=pl.CostEstimate(flops=0, bytes_accessed=40 << 20, transcendentals=0),
    )(brick_mask, voxel_mask, pltpu.with_memory_space_constraint(features, pltpu.HBM), taps)


def conv_kernel(picks, spare, info, main, x_low, x_high, y_low, y_high, e_low, e_high, weights, masks, bias, *refs):
    many = len(picks)
    outs, refs = refs[:many], refs[many + spare :]
    raw, wide, live, stage_a, stage_b, high, result, raw_sems, wide_sem, live_sems, out_sems = refs
    groups = info.shape[0] // 3
    layers = main.shape[2]
    cin = main.shape[-1]
    rows = EDGE + 1
    chunks = ((0, 4), (4, 8), (12, 6))

    def place(brick):
        bz = brick % layers
        return brick // layers, bz, jnp.clip(bz - 1, 0, layers - 3)

    def start(i, brick):
        bx, _, first = place(brick)
        tiles = pl.ds(first, 3)
        for side in range(2):

            @pl.when(bx == side)
            def _():
                for c, (plane, size) in enumerate(chunks):
                    pairs = []
                    if plane <= side * rows < plane + size:
                        end = side * rows
                        pairs.append(((x_low, x_high)[side].at[0, :, tiles], raw.at[i, end, pl.ds(1, EDGE)]))
                        pairs.append((e_low.at[side, tiles], raw.at[i, end, 0]))
                        pairs.append((e_high.at[side, tiles], raw.at[i, end, rows]))
                        size -= 1
                        plane += side == 0
                    planes = pl.ds(plane, size)
                    source = pl.ds(plane - 1 + side * EDGE, size)
                    pairs.append((main.at[source, :, tiles], raw.at[i, planes, pl.ds(1, EDGE)]))
                    pairs.append((y_low.at[source, 0, tiles], raw.at[i, planes, 0]))
                    pairs.append((y_high.at[source, 0, tiles], raw.at[i, planes, rows]))
                    for a, b in pairs:
                        pltpu.make_async_copy(a, b, raw_sems.at[i, c]).start()

    def arrived(i, c):
        whole = raw.at[i, pl.ds(*chunks[c])]
        pltpu.make_async_copy(whole, whole, raw_sems.at[i, c]).wait()

    def mask_copy(i, brick):
        bx, bz, _ = place(brick)
        rows = pl.ds(pl.multiple_of(bx * EDGE, EDGE), EDGE)
        lanes = pl.ds(pl.multiple_of(bz * AREA, AREA), AREA)
        return pltpu.make_async_copy(masks.at[rows, lanes], live.at[i], live_sems.at[i])

    def store(i):
        return pltpu.make_async_copy(result.at[i], outs[i], out_sems.at[i])

    active = [info[groups + k] > 0 for k in picks]
    some = functools.reduce(jnp.logical_or, active)
    filled = [jnp.logical_or(on, k < groups // 2) for on, k in zip(active, picks)]
    load = pltpu.make_async_copy(weights, wide, wide_sem)
    for i, k in enumerate(picks):

        @pl.when(active[i])
        def _():
            start(i, info[k])
            mask_copy(i, info[k]).start()

        if i == 0:

            @pl.when(some)
            def _():
                load.start()

    @pl.when(some)
    def _():
        load.wait()

    row = lax.broadcasted_iota(jnp.int32, (SPAN, 8, cin), 1)

    @pl.loop(0, many)
    def _(i):
        k = functools.reduce(lambda old, n: jnp.where(i == n, picks[n], old), range(1, many), picks[0])
        brick = info[k]
        _, bz, first = place(brick)
        centre = bz - first
        under = jnp.maximum(centre - 1, 0)
        over = jnp.minimum(centre + 1, 2)
        has_under = (bz > 0).astype(jnp.float32)
        has_over = (bz < layers - 1).astype(jnp.float32)

        def build(stage, pair):
            for n in range(4):
                plane = jnp.minimum(2 * pair + n, SPAN - 1)
                same = raw[i, plane, :, centre]
                middle = same.astype(jnp.float32)
                m0, m1 = middle[:, :8], middle[:, 8:]
                below = raw[i, plane, :, under].astype(jnp.float32)[:, 8:] * has_under
                above = raw[i, plane, :, over].astype(jnp.float32)[:, :8] * has_over
                u0 = jnp.where(row == 0, pltpu.roll(below, 1, 1), pltpu.roll(m0, 1, 1))
                u1 = jnp.where(row == 0, pltpu.roll(m0, 1, 1), pltpu.roll(m1, 1, 1))
                d0 = jnp.where(row == 7, pltpu.roll(m1, 7, 1), pltpu.roll(m0, 7, 1))
                d1 = jnp.where(row == 7, pltpu.roll(above, 7, 1), pltpu.roll(m1, 7, 1))
                up = jnp.concatenate([u0, u1], axis=1).astype(jnp.bfloat16)
                down = jnp.concatenate([d0, d1], axis=1).astype(jnp.bfloat16)
                for c, value in enumerate((up, same, down)):
                    stage[n // 2, :, pl.ds((3 * (n % 2) + c) * cin, cin)] = value.reshape(SPAN * EDGE, cin)

        def taps(stage, pairs, columns):
            total = None
            for b in range(3):
                window = stage[0:pairs, b * EDGE : b * EDGE + AREA, :].reshape(pairs * AREA, 6 * cin)
                term = jnp.dot(window, wide[b, :, columns], preferred_element_type=jnp.float32)
                total = term if total is None else total + term
            return total

        def emit(q, value):
            value = jnp.maximum(value + bias[...], 0.0).astype(result.dtype).T
            for n in range(2):
                mask = live[i, pl.ds(2 * q + n, 1)].astype(result.dtype)
                lanes = pl.ds(pl.multiple_of((2 * q + n) * AREA, AREA), AREA)
                result[i, :, lanes] = value[n * C : (n + 1) * C] * mask

        def advance(pair, stage):
            total = taps(stage, 2, slice(None))
            emit(jnp.maximum(pair - 1, 0), high[...] + total[:AREA, : 2 * C])
            emit(pair, total[:AREA, 2 * C :] + total[AREA:, : 2 * C])
            high[...] = total[AREA:, 2 * C :]

        @pl.when(info[groups + k] > 0)
        def _():
            mask_copy(i, brick).wait()
            high[...] = jnp.zeros_like(high)
            arrived(i, 0)
            build(stage_a, 0)

            @pl.loop(0, 2)
            def _(n):
                for c in (1, 2):

                    @pl.when(n == c - 1)
                    def _():
                        arrived(i, c)

                build(stage_b, 4 * n + 2)
                advance(4 * n, stage_a)
                build(stage_a, 4 * n + 4)
                advance(4 * n + 2, stage_b)

            emit(PAIRS - 1, high[...] + taps(stage_a, 1, slice(0, 2 * C)))

        @pl.when(jnp.logical_and(info[groups + k] == 0, k < groups // 2))
        def _():
            result[i] = jnp.zeros(result.shape[1:], result.dtype)

        for n in range(many):

            @pl.when(jnp.logical_and(i == n, filled[n]))
            def _():
                store(n).start()

    for i in range(many):

        @pl.when(filled[i])
        def _():
            store(i).wait()


def convolve(picks, info, operands, spare=0):
    cin = operands[0].shape[-1]
    wide, masks = operands[7:9]
    many = len(picks)
    flops = 2 * (PAIRS + 1) * AREA * 18 * cin * 4 * C * many
    return pl.pallas_call(
        functools.partial(conv_kernel, picks, spare),
        out_shape=[pltpu.VMEM((C, VOXELS), jnp.bfloat16)] * (many + spare),
        in_specs=[pl.BlockSpec(memory_space=pltpu.SMEM)]
        + [pl.BlockSpec(memory_space=pl.ANY)] * 9
        + [pl.BlockSpec(memory_space=pltpu.VMEM)],
        out_specs=[pl.BlockSpec(memory_space=pl.ANY)] * (many + spare),
        scratch_shapes=[
            pltpu.VMEM((many, SPAN, SPAN, 3, EDGE, cin), jnp.bfloat16),
            pltpu.VMEM(wide.shape, wide.dtype),
            pltpu.VMEM((many, EDGE, AREA), masks.dtype),
            pltpu.VMEM((2, SPAN * EDGE, 6 * cin), jnp.bfloat16),
            pltpu.VMEM((2, SPAN * EDGE, 6 * cin), jnp.bfloat16),
            pltpu.VMEM((AREA, 2 * C), jnp.float32),
            pltpu.VMEM((many, C, VOXELS), jnp.bfloat16),
            pltpu.SemaphoreType.DMA((many, 3)),
            pltpu.SemaphoreType.DMA,
            pltpu.SemaphoreType.DMA((many,)),
            pltpu.SemaphoreType.DMA((many,)),
        ],
        compiler_params=pltpu.CompilerParams(vmem_limit_bytes=54 * 1024 * 1024),
        cost_estimate=pl.CostEstimate(flops=flops, bytes_accessed=8 << 20, transcendentals=0),
    )(info, *operands)


def gather_kernel(info, *refs):
    groups = info.shape[0] // 3
    bricks, (out, held, zero, in_sems, out_sems) = refs[:groups], refs[groups:]
    me = lax.axis_index("gy")

    def load(k):
        return pltpu.make_async_copy(bricks[k], held.at[k], in_sems.at[k])

    def store(k, source):
        return pltpu.make_async_copy(source, out.at[me ^ k], out_sems.at[k])

    full = [info[2 * groups + k] > 0 for k in range(groups)]
    for k in range(groups):

        @pl.when(full[k])
        def _():
            load(k).start()

    zero[...] = jnp.zeros_like(zero)
    for k in range(groups):

        @pl.when(jnp.logical_not(full[k]))
        def _():
            store(k, zero).start()

    for k in range(groups):

        @pl.when(full[k])
        def _():
            load(k).wait()
            store(k, held.at[k]).start()

    for k in range(groups):
        store(k, zero).wait()


def gather(info, bricks):
    groups = len(bricks)
    return pl.pallas_call(
        gather_kernel,
        out_shape=jax.ShapeDtypeStruct((groups, C, VOXELS), jnp.bfloat16),
        in_specs=[pl.BlockSpec(memory_space=pltpu.SMEM)] + [pl.BlockSpec(memory_space=pl.ANY)] * groups,
        out_specs=pl.BlockSpec(memory_space=pl.ANY),
        scratch_shapes=[
            pltpu.VMEM((groups, C, VOXELS), jnp.bfloat16),
            pltpu.VMEM((C, VOXELS), jnp.bfloat16),
            pltpu.SemaphoreType.DMA((groups,)),
            pltpu.SemaphoreType.DMA((groups,)),
        ],
        compiler_params=pltpu.CompilerParams(vmem_limit_bytes=24 * 1024 * 1024),
        cost_estimate=pl.CostEstimate(flops=0, bytes_accessed=8 << 20, transcendentals=0),
    )(info, *bricks)


def shift(value, axis, up):
    count = lax.axis_size(axis)
    if up:
        return lax.ppermute(value, axis, [(i, i + 1) for i in range(count - 1)])
    return lax.ppermute(value, axis, [(i + 1, i) for i in range(count - 1)])


def per_device(features, voxel_mask, brick_mask, owner, weights, bias):
    extent_x, extent_y, extent_z, channels_in = features.shape
    bricks_x, bricks_y, bricks_z = extent_x // EDGE, extent_y // EDGE, extent_z // EDGE
    count = bricks_x * bricks_y * bricks_z
    groups = lax.axis_size("gy")
    owner = owner.reshape(count)

    sends = sends_of(brick_mask, owner, groups)
    receives = lax.all_to_all(sends, "gy", split_axis=0, concat_axis=0, tiled=True)
    x_first, x_last, y_first, y_last, info, packed = faces(brick_mask, owner, sends, receives, voxel_mask, features)
    y_low = shift(y_last, "gy", True)
    y_high = shift(y_first, "gy", False)
    x_low = shift(x_last, "gx", True)
    x_high = shift(x_first, "gx", False)
    e_low = shift(jnp.concatenate([x_low[:, -1], x_high[:, -1]]), "gy", True)
    e_high = shift(jnp.concatenate([x_low[:, 0], x_high[:, 0]]), "gy", False)

    def partner(value, k):
        return lax.ppermute(value, "gy", [(i, i ^ k) for i in range(groups)])

    main, masks, wide = prepare(brick_mask, voxel_mask, features, weights)
    wide_bias = jnp.concatenate([bias, bias])[None, :]
    operands = (main, x_low, x_high, y_low, y_high, e_low, e_high, wide, masks, wide_bias)
    packed = packed[0]

    far = list(range(groups - 1, groups // 2 - 1, -1))
    near = list(range(groups // 2 - 1, 0, -1))
    received = [None] * groups
    (brick,) = convolve((far[0],), info, operands)
    for n, k in enumerate(far):
        picks = ((near + [0])[n],) + tuple(far[n + 1 : n + 2])
        upward = [(i, i ^ k) for i in range(groups) if i < i ^ k]
        downward = [(b, a) for a, b in upward]

        def exchange(pairs, value, info, *operands):
            if not pairs:
                *made, got = convolve(picks, info, operands, spare=1)
            else:
                got = lax.ppermute(value, "gy", pairs)
                made = convolve(picks, info, operands)
            return got, *made

        branches = [functools.partial(exchange, pairs) for pairs in ([], upward, downward, upward + downward)]
        case = jnp.bitwise_and(jnp.right_shift(packed, 2 * (k - groups // 2)), 3)
        received[k], local, *ahead = lax.switch(case, branches, brick, info, *operands)
        if picks[0]:
            received[picks[0]] = partner(local, picks[0])
        else:
            received[0] = local
        brick = ahead[0] if ahead else None
    return gather(info, received)[None]


def solution(mesh):
    return jax.shard_map(
        per_device,
        mesh=mesh,
        in_specs=(
            P("gx", "gy", None, None),
            P("gx", "gy", None),
            P("gx", "gy", None),
            P("gx", "gy", None, None),
            P(),
            P(),
        ),
        out_specs=P("gx", "gy", None, None),
        check_vma=False,
    )
```

```python
import functools

import jax
import jax.numpy as jnp
from jax import lax
from jax.experimental import pallas as pl
from jax.experimental.pallas import tpu as pltpu
from jax.sharding import PartitionSpec as P

C = 64
EDGE = 16
AREA = EDGE * EDGE
VOXELS = EDGE**3
PAIRS = EDGE // 2
SPAN = EDGE + 2
TRIO = 3
LITTLE = pl.CostEstimate(flops=0, bytes_accessed=1024, transcendentals=0)


def activity(voxels, flags, bx):
    layer = lax.broadcasted_iota(jnp.int32, voxels.shape, 2) // EDGE
    chosen = jnp.zeros(voxels.shape, jnp.int32)
    for bz in range(flags.shape[2]):
        chosen = jnp.where(layer == bz, flags[bx, 0, bz], chosen)
    return (voxels * chosen).astype(jnp.float32)


def spread(values, mask):
    n, y, z, c = values.shape
    wide = jnp.broadcast_to(mask[..., None], values.shape).astype(jnp.bfloat16)
    return (values * wide).reshape(n, y, z // EDGE, EDGE, c)


def sends_kernel(flags, owner, sends):
    layers = flags.shape[2]
    for o in range(sends.shape[0]):
        sends[o] = 0
    for b in range(owner.shape[0]):
        sends[owner[b]] = flags[b // layers, 0, b % layers]


def sends_of(brick_mask, owner, groups):
    return pl.pallas_call(
        sends_kernel,
        out_shape=jax.ShapeDtypeStruct((groups,), jnp.int32),
        in_specs=[pl.BlockSpec(memory_space=pltpu.SMEM)] * 2,
        out_specs=pl.BlockSpec(memory_space=pltpu.SMEM),
        cost_estimate=LITTLE,
    )(brick_mask, owner)


def plan(owner, sends, receives, info, packed):
    groups = sends.shape[0]
    far = groups // 2
    me = lax.axis_index("gy")
    for k in range(groups):
        info[k] = 0
    for b in range(owner.shape[0]):
        info[owner[b] ^ me] = b
    total = jnp.int32(0)
    for k in range(groups):
        peer = me ^ k
        sent = sends[peer]
        info[groups + k] = sent
        info[2 * groups + k] = receives[peer] if k >= far else 1
        if k >= far:
            received = receives[peer]
            total = total | (jnp.where(peer > me, sent + 2 * received, received + 2 * sent) << (2 * (k - far)))
    packed[0] = total


def face_kernel(flags, owner, sends, receives, voxels, features, x_first, x_last, y_first, y_last, info, packed, v_raw, x_raw, y_raw, sems):
    rows = features.shape[0]
    sides = (0, rows - 1)
    columns = (0, features.shape[1] - 1)
    copies = [pltpu.make_async_copy(voxels, v_raw, sems.at[4])]
    copies += [pltpu.make_async_copy(features.at[:, pl.ds(y, 1)], y_raw.at[n], sems.at[n]) for n, y in enumerate(columns)]
    copies += [pltpu.make_async_copy(features.at[pl.ds(x, 1)], x_raw.at[n], sems.at[2 + n]) for n, x in enumerate(sides)]
    for copy in copies:
        copy.start()
    plan(owner, sends, receives, info, packed)
    for copy in copies:
        copy.wait()
    for n, out in enumerate((y_first, y_last)):
        for bx in range(rows // EDGE):
            span = slice(bx * EDGE, (bx + 1) * EDGE)
            y = columns[n]
            out[span] = spread(y_raw[n, span], activity(v_raw[span, y : y + 1], flags, bx))
    for n, out in enumerate((x_first, x_last)):
        x = sides[n]
        out[...] = spread(x_raw[n], activity(v_raw[x : x + 1], flags, x // EDGE))


def faces(brick_mask, owner, sends, receives, voxel_mask, features):
    groups = sends.shape[0]
    ex, ey, ez, cin = features.shape
    layers = ez // EDGE
    shapes = [(1, ey, layers, EDGE, cin)] * 2 + [(ex, 1, layers, EDGE, cin)] * 2
    return pl.pallas_call(
        face_kernel,
        out_shape=[jax.ShapeDtypeStruct(shape, features.dtype) for shape in shapes] + [jax.ShapeDtypeStruct((n,), jnp.int32) for n in (3 * groups, 1)],
        in_specs=[pl.BlockSpec(memory_space=pltpu.SMEM)] * 4 + [pl.BlockSpec(memory_space=pltpu.HBM)] * 2,
        out_specs=[pl.BlockSpec(memory_space=pltpu.VMEM)] * 4 + [pl.BlockSpec(memory_space=pltpu.SMEM)] * 2,
        scratch_shapes=[
            pltpu.VMEM(voxel_mask.shape, voxel_mask.dtype),
            pltpu.VMEM((2, 1, ey, ez, cin), features.dtype),
            pltpu.VMEM((2, ex, 1, ez, cin), features.dtype),
            pltpu.SemaphoreType.DMA((5,)),
        ],
        compiler_params=pltpu.CompilerParams(vmem_limit_bytes=24 * 1024 * 1024),
        cost_estimate=LITTLE,
    )(brick_mask, owner, sends, receives, *(pltpu.with_memory_space_constraint(a, pltpu.HBM) for a in (voxel_mask, features)))


SLAB = 8


def prepare_kernel(flags, voxels, features, weights, main, masks, wide):
    step = pl.program_id(0)
    n, y, z = voxels.shape
    mask = activity(voxels[...], flags, step // (EDGE // SLAB))
    main[...] = spread(features[...], mask)

    lanes = masks.shape[1]
    source = lax.broadcasted_iota(jnp.int32, (z, lanes), 0)
    lane = lax.broadcasted_iota(jnp.int32, (z, lanes), 1)
    pick = jnp.logical_and(source // EDGE == lane // AREA, source % EDGE == lane % EDGE)
    every = jnp.dot(
        mask.reshape(n * y, z).astype(jnp.bfloat16),
        jnp.where(pick, 1.0, 0.0).astype(jnp.bfloat16),
        preferred_element_type=jnp.float32,
    ).reshape(n, y, lanes)
    row = lax.broadcasted_iota(jnp.int32, (n, y, lanes), 1)
    column = lax.broadcasted_iota(jnp.int32, (n, y, lanes), 2) % AREA // EDGE
    masks[...] = jnp.sum(jnp.where(row == column, every, 0.0), axis=1)

    @pl.when(step == 0)
    def _():
        cin = weights.shape[-1]
        for b in range(3):
            for j in range(2):
                for c in range(3):
                    parts = []
                    for t in range(4):
                        a = 2 + j - t
                        tap = weights[(a * 3 + b) * 3 + c] if 0 <= a <= 2 else jnp.zeros(weights.shape[1:], weights.dtype)
                        parts.append(tap.astype(jnp.float32))
                    block = jnp.concatenate(parts, axis=0).T
                    wide[b, (3 * j + c) * cin : (3 * j + c + 1) * cin, :] = block.astype(wide.dtype)


def prepare(brick_mask, voxel_mask, features, weights):
    ex, ey, ez, cin = features.shape
    cout = weights.shape[4]
    taps = weights.transpose(0, 1, 2, 4, 3).reshape(27, cout, cin)
    return pl.pallas_call(
        prepare_kernel,
        out_shape=[
            jax.ShapeDtypeStruct((ex, ey, ez // EDGE, EDGE, cin), features.dtype),
            jax.ShapeDtypeStruct((ex, ez // EDGE * AREA), jnp.float32),
            jax.ShapeDtypeStruct((3, 6 * cin, 4 * cout), weights.dtype),
        ],
        grid=(ex // SLAB,),
        in_specs=[
            pl.BlockSpec(memory_space=pltpu.SMEM),
            pl.BlockSpec((SLAB, ey, ez), lambda i: (i, 0, 0)),
            pl.BlockSpec((SLAB, ey, ez, cin), lambda i: (i, 0, 0, 0)),
            pl.BlockSpec((27, cout, cin), lambda i: (0, 0, 0)),
        ],
        out_specs=[
            pl.BlockSpec((SLAB, ey, ez // EDGE, EDGE, cin), lambda i: (i, 0, 0, 0, 0)),
            pl.BlockSpec((SLAB, ez // EDGE * AREA), lambda i: (i, 0)),
            pl.BlockSpec((3, 6 * cin, 4 * cout), lambda i: (0, 0, 0)),
        ],
        compiler_params=pltpu.CompilerParams(vmem_limit_bytes=32 * 1024 * 1024),
        cost_estimate=pl.CostEstimate(flops=0, bytes_accessed=40 << 20, transcendentals=0),
    )(brick_mask, voxel_mask, pltpu.with_memory_space_constraint(features, pltpu.HBM), taps)


def conv_kernel(picks, spare, info, main, x_low, x_high, y_low, y_high, e_low, e_high, weights, masks, bias, *refs):
    many = len(picks)
    outs, refs = refs[:many], refs[many + spare :]
    raw, wide, live, stage, total, result, raw_sems, wide_sem, live_sems, out_sems = refs
    groups = info.shape[0] // 3
    layers = main.shape[2]
    cin = main.shape[-1]
    rows = EDGE + 1
    chunks = [(n * 2 * TRIO, 2 * TRIO) for n in range(SPAN // (2 * TRIO))]

    def place(brick):
        bz = brick % layers
        return brick // layers, bz, jnp.clip(bz - 1, 0, layers - 3)

    def start(i, brick):
        bx, _, first = place(brick)
        tiles = pl.ds(first, 3)
        for side in range(2):

            @pl.when(bx == side)
            def _():
                for c, (plane, size) in enumerate(chunks):
                    pairs = []
                    if plane <= side * rows < plane + size:
                        end = side * rows
                        pairs.append(((x_low, x_high)[side].at[0, :, tiles], raw.at[i, end, pl.ds(1, EDGE)]))
                        pairs.append((e_low.at[side, tiles], raw.at[i, end, 0]))
                        pairs.append((e_high.at[side, tiles], raw.at[i, end, rows]))
                        size -= 1
                        plane += side == 0
                    planes = pl.ds(plane, size)
                    source = pl.ds(plane - 1 + side * EDGE, size)
                    pairs.append((main.at[source, :, tiles], raw.at[i, planes, pl.ds(1, EDGE)]))
                    pairs.append((y_low.at[source, 0, tiles], raw.at[i, planes, 0]))
                    pairs.append((y_high.at[source, 0, tiles], raw.at[i, planes, rows]))
                    for a, b in pairs:
                        pltpu.make_async_copy(a, b, raw_sems.at[i, c]).start()

    def arrived(i, c):
        whole = raw.at[i, pl.ds(0, 2 * TRIO)]
        pltpu.make_async_copy(whole, whole, raw_sems.at[i, c]).wait()

    def mask_copy(i, brick):
        bx, bz, _ = place(brick)
        rows = pl.ds(pl.multiple_of(bx * EDGE, EDGE), EDGE)
        lanes = pl.ds(pl.multiple_of(bz * AREA, AREA), AREA)
        return pltpu.make_async_copy(masks.at[rows, lanes], live.at[i], live_sems.at[i])

    def store(i):
        return pltpu.make_async_copy(result.at[i], outs[i], out_sems.at[i])

    active = [info[groups + k] > 0 for k in picks]
    some = functools.reduce(jnp.logical_or, active)
    filled = [jnp.logical_or(on, k < groups // 2) for on, k in zip(active, picks)]
    load = pltpu.make_async_copy(weights, wide, wide_sem)
    for i, k in enumerate(picks):

        @pl.when(active[i])
        def _():
            start(i, info[k])
            mask_copy(i, info[k]).start()

        if i == 0:

            @pl.when(some)
            def _():
                load.start()

    @pl.when(some)
    def _():
        load.wait()

    row = lax.broadcasted_iota(jnp.int32, (SPAN, 8, cin), 1)

    @pl.loop(0, many)
    def _(i):
        k = functools.reduce(lambda old, n: jnp.where(i == n, picks[n], old), range(1, many), picks[0])
        brick = info[k]
        _, bz, first = place(brick)
        centre = bz - first
        under = jnp.maximum(centre - 1, 0)
        over = jnp.minimum(centre + 1, 2)
        has_under = (bz > 0).astype(jnp.float32)
        has_over = (bz < layers - 1).astype(jnp.float32)

        def build(pair, at):
            for n in range(2):
                plane = 2 * pair + n
                same = raw[i, plane, :, centre]
                middle = same.astype(jnp.float32)
                m0, m1 = middle[:, :8], middle[:, 8:]
                below = raw[i, plane, :, under].astype(jnp.float32)[:, 8:] * has_under
                above = raw[i, plane, :, over].astype(jnp.float32)[:, :8] * has_over
                u0 = jnp.where(row == 0, pltpu.roll(below, 1, 1), pltpu.roll(m0, 1, 1))
                u1 = jnp.where(row == 0, pltpu.roll(m0, 1, 1), pltpu.roll(m1, 1, 1))
                d0 = jnp.where(row == 7, pltpu.roll(m1, 7, 1), pltpu.roll(m0, 7, 1))
                d1 = jnp.where(row == 7, pltpu.roll(above, 7, 1), pltpu.roll(m1, 7, 1))
                up = jnp.concatenate([u0, u1], axis=1).astype(jnp.bfloat16)
                down = jnp.concatenate([d0, d1], axis=1).astype(jnp.bfloat16)
                for c, value in enumerate((up, same, down)):
                    stage[at, :, pl.ds((3 * n + c) * cin, cin)] = value.reshape(SPAN * EDGE, cin)

        def emit(q, at):
            value = total[at, :, 2 * C :] + total[at + 1, :, : 2 * C]
            value = jnp.maximum(value + bias[...], 0.0).astype(result.dtype).T
            for n in range(2):
                mask = live[i, pl.ds(2 * q + n, 1)].astype(result.dtype)
                lanes = pl.ds(pl.multiple_of((2 * q + n) * AREA, AREA), AREA)
                result[i, :, lanes] = value[n * C : (n + 1) * C] * mask

        @pl.when(info[groups + k] > 0)
        def _():
            mask_copy(i, brick).wait()
            total[0] = jnp.zeros(total.shape[1:], total.dtype)

            @pl.loop(0, len(chunks))
            def _(n):
                arrived(i, n)

                @pl.loop(0, TRIO)
                def _(m):
                    build(TRIO * n + m, m)

                for b in range(3):
                    window = stage[:, b * EDGE : b * EDGE + AREA, :].reshape(TRIO * AREA, 6 * cin)
                    term = jnp.dot(window, wide[b], preferred_element_type=jnp.float32).reshape(TRIO, AREA, 4 * C)
                    total[1:] = term if b == 0 else total[1:] + term

                @pl.loop(0, TRIO)
                def _(m):
                    emit(jnp.maximum(TRIO * n + m - 1, 0), m)

                total[0] = total[TRIO]

        @pl.when(jnp.logical_and(info[groups + k] == 0, k < groups // 2))
        def _():
            result[i] = jnp.zeros(result.shape[1:], result.dtype)

        for n in range(many):

            @pl.when(jnp.logical_and(i == n, filled[n]))
            def _():
                store(n).start()

    for i in range(many):

        @pl.when(filled[i])
        def _():
            store(i).wait()


def convolve(picks, info, operands, spare=0):
    cin = operands[0].shape[-1]
    wide, masks = operands[7:9]
    many = len(picks)
    flops = 2 * (PAIRS + 1) * AREA * 18 * cin * 4 * C * many
    return pl.pallas_call(
        functools.partial(conv_kernel, picks, spare),
        out_shape=[pltpu.VMEM((C, VOXELS), jnp.bfloat16)] * (many + spare),
        in_specs=[pl.BlockSpec(memory_space=pltpu.SMEM)]
        + [pl.BlockSpec(memory_space=pl.ANY)] * 9
        + [pl.BlockSpec(memory_space=pltpu.VMEM)],
        out_specs=[pl.BlockSpec(memory_space=pl.ANY)] * (many + spare),
        scratch_shapes=[
            pltpu.VMEM((many, SPAN, SPAN, 3, EDGE, cin), jnp.bfloat16),
            pltpu.VMEM(wide.shape, wide.dtype),
            pltpu.VMEM((many, EDGE, AREA), masks.dtype),
            pltpu.VMEM((TRIO, SPAN * EDGE, 6 * cin), jnp.bfloat16),
            pltpu.VMEM((TRIO + 1, AREA, 4 * C), jnp.float32),
            pltpu.VMEM((many, C, VOXELS), jnp.bfloat16),
            pltpu.SemaphoreType.DMA((many, 3)),
            pltpu.SemaphoreType.DMA,
            pltpu.SemaphoreType.DMA((many,)),
            pltpu.SemaphoreType.DMA((many,)),
        ],
        compiler_params=pltpu.CompilerParams(vmem_limit_bytes=54 * 1024 * 1024),
        cost_estimate=pl.CostEstimate(flops=flops, bytes_accessed=8 << 20, transcendentals=0),
    )(info, *operands)


def gather_kernel(info, *refs):
    groups = info.shape[0] // 3
    bricks, (out, held, zero, in_sems, out_sems) = refs[:groups], refs[groups:]
    me = lax.axis_index("gy")

    def load(k):
        return pltpu.make_async_copy(bricks[k], held.at[k], in_sems.at[k])

    def store(k, source):
        return pltpu.make_async_copy(source, out.at[me ^ k], out_sems.at[k])

    full = [info[2 * groups + k] > 0 for k in range(groups)]
    for k in range(groups):

        @pl.when(full[k])
        def _():
            load(k).start()

    zero[...] = jnp.zeros_like(zero)
    for k in range(groups):

        @pl.when(jnp.logical_not(full[k]))
        def _():
            store(k, zero).start()

    for k in range(groups):

        @pl.when(full[k])
        def _():
            load(k).wait()
            store(k, held.at[k]).start()

    for k in range(groups):
        store(k, zero).wait()


def gather(info, bricks):
    groups = len(bricks)
    return pl.pallas_call(
        gather_kernel,
        out_shape=jax.ShapeDtypeStruct((groups, C, VOXELS), jnp.bfloat16),
        in_specs=[pl.BlockSpec(memory_space=pltpu.SMEM)] + [pl.BlockSpec(memory_space=pl.ANY)] * groups,
        out_specs=pl.BlockSpec(memory_space=pl.ANY),
        scratch_shapes=[
            pltpu.VMEM((groups, C, VOXELS), jnp.bfloat16),
            pltpu.VMEM((C, VOXELS), jnp.bfloat16),
            pltpu.SemaphoreType.DMA((groups,)),
            pltpu.SemaphoreType.DMA((groups,)),
        ],
        compiler_params=pltpu.CompilerParams(vmem_limit_bytes=24 * 1024 * 1024),
        cost_estimate=pl.CostEstimate(flops=0, bytes_accessed=8 << 20, transcendentals=0),
    )(info, *bricks)


def shift(value, axis, up):
    count = lax.axis_size(axis)
    if up:
        return lax.ppermute(value, axis, [(i, i + 1) for i in range(count - 1)])
    return lax.ppermute(value, axis, [(i + 1, i) for i in range(count - 1)])


def per_device(features, voxel_mask, brick_mask, owner, weights, bias):
    extent_x, extent_y, extent_z, channels_in = features.shape
    bricks_x, bricks_y, bricks_z = extent_x // EDGE, extent_y // EDGE, extent_z // EDGE
    count = bricks_x * bricks_y * bricks_z
    groups = lax.axis_size("gy")
    owner = owner.reshape(count)

    sends = sends_of(brick_mask, owner, groups)
    receives = lax.all_to_all(sends, "gy", split_axis=0, concat_axis=0, tiled=True)
    x_first, x_last, y_first, y_last, info, packed = faces(brick_mask, owner, sends, receives, voxel_mask, features)
    y_low = shift(y_last, "gy", True)
    y_high = shift(y_first, "gy", False)
    x_low = shift(x_last, "gx", True)
    x_high = shift(x_first, "gx", False)
    e_low = shift(jnp.concatenate([x_low[:, -1], x_high[:, -1]]), "gy", True)
    e_high = shift(jnp.concatenate([x_low[:, 0], x_high[:, 0]]), "gy", False)

    def partner(value, k):
        return lax.ppermute(value, "gy", [(i, i ^ k) for i in range(groups)])

    main, masks, wide = prepare(brick_mask, voxel_mask, features, weights)
    wide_bias = jnp.concatenate([bias, bias])[None, :]
    operands = (main, x_low, x_high, y_low, y_high, e_low, e_high, wide, masks, wide_bias)
    packed = packed[0]

    far = list(range(groups - 1, groups // 2 - 1, -1))
    near = list(range(groups // 2 - 1, 0, -1))
    received = [None] * groups
    (brick,) = convolve((far[0],), info, operands)
    for n, k in enumerate(far):
        picks = ((near + [0])[n],) + tuple(far[n + 1 : n + 2])
        upward = [(i, i ^ k) for i in range(groups) if i < i ^ k]
        downward = [(b, a) for a, b in upward]

        def exchange(pairs, value, info, *operands):
            if not pairs:
                *made, got = convolve(picks, info, operands, spare=1)
            else:
                got = lax.ppermute(value, "gy", pairs)
                made = convolve(picks, info, operands)
            return got, *made

        branches = [functools.partial(exchange, pairs) for pairs in ([], upward, downward, upward + downward)]
        case = jnp.bitwise_and(jnp.right_shift(packed, 2 * (k - groups // 2)), 3)
        received[k], local, *ahead = lax.switch(case, branches, brick, info, *operands)
        if picks[0]:
            received[picks[0]] = partner(local, picks[0])
        else:
            received[0] = local
        brick = ahead[0] if ahead else None
    return gather(info, received)[None]


def solution(mesh):
    return jax.shard_map(
        per_device,
        mesh=mesh,
        in_specs=(
            P("gx", "gy", None, None),
            P("gx", "gy", None),
            P("gx", "gy", None),
            P("gx", "gy", None, None),
            P(),
            P(),
        ),
        out_specs=P("gx", "gy", None, None),
        check_vma=False,
    )
```

```python
import functools

import jax
import jax.numpy as jnp
from jax import lax
from jax.experimental import pallas as pl
from jax.experimental.pallas import tpu as pltpu
from jax.sharding import PartitionSpec as P

C = 64
EDGE = 16
AREA = EDGE * EDGE
VOXELS = EDGE**3
PAIRS = EDGE // 2
SPAN = EDGE + 2
LITTLE = pl.CostEstimate(flops=0, bytes_accessed=1024, transcendentals=0)


def activity(voxels, flags, bx):
    layer = lax.broadcasted_iota(jnp.int32, voxels.shape, 2) // EDGE
    chosen = jnp.zeros(voxels.shape, jnp.int32)
    for bz in range(flags.shape[2]):
        chosen = jnp.where(layer == bz, flags[bx, 0, bz], chosen)
    return (voxels * chosen).astype(jnp.float32)


def spread(values, mask):
    n, y, z, c = values.shape
    wide = jnp.broadcast_to(mask[..., None], values.shape).astype(jnp.bfloat16)
    return (values * wide).reshape(n, y, z // EDGE, EDGE, c)


def sends_kernel(flags, owner, sends):
    layers = flags.shape[2]
    for o in range(sends.shape[0]):
        sends[o] = 0
    for b in range(owner.shape[0]):
        sends[owner[b]] = flags[b // layers, 0, b % layers]


def sends_of(brick_mask, owner, groups):
    return pl.pallas_call(
        sends_kernel,
        out_shape=jax.ShapeDtypeStruct((groups,), jnp.int32),
        in_specs=[pl.BlockSpec(memory_space=pltpu.SMEM)] * 2,
        out_specs=pl.BlockSpec(memory_space=pltpu.SMEM),
        cost_estimate=LITTLE,
    )(brick_mask, owner)


def plan(owner, sends, receives, info, packed):
    groups = sends.shape[0]
    far = groups // 2
    me = lax.axis_index("gy")
    for k in range(groups):
        info[k] = 0
    for b in range(owner.shape[0]):
        info[owner[b] ^ me] = b
    total = jnp.int32(0)
    for k in range(groups):
        peer = me ^ k
        sent = sends[peer]
        info[groups + k] = sent
        info[2 * groups + k] = receives[peer] if k >= far else 1
        if k >= far:
            received = receives[peer]
            total = total | (jnp.where(peer > me, sent + 2 * received, received + 2 * sent) << (2 * (k - far)))
    packed[0] = total


def face_kernel(flags, owner, sends, receives, voxels, features, x_first, x_last, y_first, y_last, info, packed, v_raw, x_raw, y_raw, sems):
    rows = features.shape[0]
    sides = (0, rows - 1)
    columns = (0, features.shape[1] - 1)
    copies = [pltpu.make_async_copy(voxels, v_raw, sems.at[4])]
    copies += [pltpu.make_async_copy(features.at[:, pl.ds(y, 1)], y_raw.at[n], sems.at[n]) for n, y in enumerate(columns)]
    copies += [pltpu.make_async_copy(features.at[pl.ds(x, 1)], x_raw.at[n], sems.at[2 + n]) for n, x in enumerate(sides)]
    for copy in copies:
        copy.start()
    plan(owner, sends, receives, info, packed)
    for copy in copies:
        copy.wait()
    for n, out in enumerate((y_first, y_last)):
        for bx in range(rows // EDGE):
            span = slice(bx * EDGE, (bx + 1) * EDGE)
            y = columns[n]
            out[span] = spread(y_raw[n, span], activity(v_raw[span, y : y + 1], flags, bx))
    for n, out in enumerate((x_first, x_last)):
        x = sides[n]
        out[...] = spread(x_raw[n], activity(v_raw[x : x + 1], flags, x // EDGE))


def faces(brick_mask, owner, sends, receives, voxel_mask, features):
    groups = sends.shape[0]
    ex, ey, ez, cin = features.shape
    layers = ez // EDGE
    shapes = [(1, ey, layers, EDGE, cin)] * 2 + [(ex, 1, layers, EDGE, cin)] * 2
    return pl.pallas_call(
        face_kernel,
        out_shape=[jax.ShapeDtypeStruct(shape, features.dtype) for shape in shapes] + [jax.ShapeDtypeStruct((n,), jnp.int32) for n in (3 * groups, 1)],
        in_specs=[pl.BlockSpec(memory_space=pltpu.SMEM)] * 4 + [pl.BlockSpec(memory_space=pltpu.HBM)] * 2,
        out_specs=[pl.BlockSpec(memory_space=pltpu.VMEM)] * 4 + [pl.BlockSpec(memory_space=pltpu.SMEM)] * 2,
        scratch_shapes=[
            pltpu.VMEM(voxel_mask.shape, voxel_mask.dtype),
            pltpu.VMEM((2, 1, ey, ez, cin), features.dtype),
            pltpu.VMEM((2, ex, 1, ez, cin), features.dtype),
            pltpu.SemaphoreType.DMA((5,)),
        ],
        compiler_params=pltpu.CompilerParams(vmem_limit_bytes=24 * 1024 * 1024),
        cost_estimate=LITTLE,
    )(brick_mask, owner, sends, receives, *(pltpu.with_memory_space_constraint(a, pltpu.HBM) for a in (voxel_mask, features)))


SLAB = 8


def prepare_kernel(flags, voxels, features, weights, main, masks, wide, picks):
    step = pl.program_id(0)
    n, y, z = voxels.shape
    lanes = masks.shape[1]
    source = lax.broadcasted_iota(jnp.int32, (z, lanes), 0)
    lane = lax.broadcasted_iota(jnp.int32, (z, lanes), 1)
    pick = jnp.logical_and(source // EDGE == lane // AREA, source % EDGE == lane % EDGE)
    picks[...] = jnp.where(pick, 1.0, 0.0).astype(jnp.bfloat16)
    row = lax.broadcasted_iota(jnp.int32, (y, lanes), 0)
    column = lax.broadcasted_iota(jnp.int32, (y, lanes), 1) % AREA // EDGE

    @pl.loop(0, n)
    def _(x):
        here = pl.ds(x, 1)
        mask = activity(voxels[here], flags, step // (EDGE // SLAB))
        main[here] = spread(features[here], mask)
        every = jnp.dot(mask[0].astype(jnp.bfloat16), picks[...], preferred_element_type=jnp.float32)
        masks[here] = jnp.sum(jnp.where(row == column, every, 0.0), axis=0, keepdims=True)

    @pl.when(step == 0)
    def _():
        cin = weights.shape[-1]
        for b in range(3):
            for j in range(2):
                for c in range(3):
                    parts = []
                    for t in range(4):
                        a = 2 + j - t
                        tap = weights[(a * 3 + b) * 3 + c] if 0 <= a <= 2 else jnp.zeros(weights.shape[1:], weights.dtype)
                        parts.append(tap.astype(jnp.float32))
                    block = jnp.concatenate(parts, axis=0).T
                    start = (6 * b + 3 * j + c) * cin
                    wide[start : start + cin, :] = block.astype(wide.dtype)


def prepare(brick_mask, voxel_mask, features, weights):
    ex, ey, ez, cin = features.shape
    cout = weights.shape[4]
    taps = weights.transpose(0, 1, 2, 4, 3).reshape(27, cout, cin)
    return pl.pallas_call(
        prepare_kernel,
        out_shape=[
            jax.ShapeDtypeStruct((ex, ey, ez // EDGE, EDGE, cin), features.dtype),
            jax.ShapeDtypeStruct((ex, ez // EDGE * AREA), jnp.float32),
            jax.ShapeDtypeStruct((18 * cin, 4 * cout), weights.dtype),
        ],
        grid=(ex // SLAB,),
        in_specs=[
            pl.BlockSpec(memory_space=pltpu.SMEM),
            pl.BlockSpec((SLAB, ey, ez), lambda i: (i, 0, 0)),
            pl.BlockSpec((SLAB, ey, ez, cin), lambda i: (i, 0, 0, 0)),
            pl.BlockSpec((27, cout, cin), lambda i: (0, 0, 0)),
        ],
        out_specs=[
            pl.BlockSpec((SLAB, ey, ez // EDGE, EDGE, cin), lambda i: (i, 0, 0, 0, 0)),
            pl.BlockSpec((SLAB, ez // EDGE * AREA), lambda i: (i, 0)),
            pl.BlockSpec((18 * cin, 4 * cout), lambda i: (0, 0)),
        ],
        scratch_shapes=[pltpu.VMEM((ez, ez // EDGE * AREA), jnp.bfloat16)],
        compiler_params=pltpu.CompilerParams(vmem_limit_bytes=32 * 1024 * 1024),
        cost_estimate=pl.CostEstimate(flops=0, bytes_accessed=40 << 20, transcendentals=0),
    )(brick_mask, voxel_mask, pltpu.with_memory_space_constraint(features, pltpu.HBM), taps)


def conv_kernel(picks, spare, info, main, x_low, x_high, y_low, y_high, e_low, e_high, weights, masks, bias, *refs):
    many = len(picks)
    outs, refs = refs[:many], refs[many + spare :]
    raw, wide, live, stage_a, stage_b, high, result, raw_sems, wide_sem, live_sems, out_sems = refs
    groups = info.shape[0] // 3
    layers = main.shape[2]
    cin = main.shape[-1]
    rows = EDGE + 1
    pieces = ((0, 6), (6, 6), (12, 5))

    def pick(i):
        return functools.reduce(lambda old, n: jnp.where(i == n, picks[n], old), range(1, many), picks[0])

    def place(brick):
        bz = brick % layers
        return brick // layers, bz, jnp.clip(bz - 1, 0, layers - 3)

    def start(i, brick):
        bx, _, first = place(brick)
        tiles = pl.ds(first, 3)
        end = bx * rows
        for side in range(2):

            @pl.when(bx == side)
            def _():
                face = (x_low, x_high)[side].at[0, :, tiles]
                pltpu.make_async_copy(face, raw.at[i, end, pl.ds(1, EDGE)], raw_sems.at[i, 3]).start()

        pltpu.make_async_copy(e_low.at[bx, tiles], raw.at[i, end, 0], raw_sems.at[i, 3]).start()
        pltpu.make_async_copy(e_high.at[bx, tiles], raw.at[i, end, rows], raw_sems.at[i, 3]).start()
        for c, (plane, size) in enumerate(pieces):
            source = pl.ds(plane + bx * (EDGE - 1), size)
            planes = pl.ds(plane + 1 - bx, size)
            pltpu.make_async_copy(main.at[source, :, tiles], raw.at[i, planes, pl.ds(1, EDGE)], raw_sems.at[i, c]).start()
            pltpu.make_async_copy(y_low.at[source, 0, tiles], raw.at[i, planes, 0], raw_sems.at[i, c]).start()
            pltpu.make_async_copy(y_high.at[source, 0, tiles], raw.at[i, planes, rows], raw_sems.at[i, c]).start()

    def arrived(i, c):
        whole = raw.at[i, pl.ds(0, pieces[c][1] if c < 3 else 1)]
        pltpu.make_async_copy(whole, whole, raw_sems.at[i, c]).wait()

    def mask_copy(i, brick):
        bx, bz, _ = place(brick)
        rows = pl.ds(pl.multiple_of(bx * EDGE, EDGE), EDGE)
        lanes = pl.ds(pl.multiple_of(bz * AREA, AREA), AREA)
        return pltpu.make_async_copy(masks.at[rows, lanes], live.at[i], live_sems.at[i])

    def store(i):
        return pltpu.make_async_copy(result.at[i], outs[i], out_sems.at[i])

    active = [info[groups + k] > 0 for k in picks]
    some = functools.reduce(jnp.logical_or, active)
    filled = [jnp.logical_or(on, k < groups // 2) for on, k in zip(active, picks)]
    load = pltpu.make_async_copy(weights, wide, wide_sem)

    @pl.when(some)
    def _():
        load.start()

    @pl.loop(0, many)
    def _(i):
        k = pick(i)

        @pl.when(info[groups + k] > 0)
        def _():
            start(i, info[k])
            mask_copy(i, info[k]).start()

    first_active = jnp.where(active[0], 0, 1)

    row = lax.broadcasted_iota(jnp.int32, (SPAN, 8, cin), 1)

    @pl.loop(0, many)
    def _(i):
        k = pick(i)
        brick = info[k]
        _, bz, first = place(brick)
        centre = bz - first
        under = jnp.maximum(centre - 1, 0)
        over = jnp.minimum(centre + 1, 2)
        has_under = (bz > 0).astype(jnp.float32)
        has_over = (bz < layers - 1).astype(jnp.float32)

        def build(stage, pair):
            for n in range(2):
                plane = 2 * pair + n
                same = raw[i, plane, :, centre]
                middle = same.astype(jnp.float32)
                m0, m1 = middle[:, :8], middle[:, 8:]
                below = raw[i, plane, :, under].astype(jnp.float32)[:, 8:] * has_under
                above = raw[i, plane, :, over].astype(jnp.float32)[:, :8] * has_over
                u0 = jnp.where(row == 0, pltpu.roll(below, 1, 1), pltpu.roll(m0, 1, 1))
                u1 = jnp.where(row == 0, pltpu.roll(m0, 1, 1), pltpu.roll(m1, 1, 1))
                d0 = jnp.where(row == 7, pltpu.roll(m1, 7, 1), pltpu.roll(m0, 7, 1))
                d1 = jnp.where(row == 7, pltpu.roll(above, 7, 1), pltpu.roll(m1, 7, 1))
                up = jnp.concatenate([u0, u1], axis=1).astype(jnp.bfloat16)
                down = jnp.concatenate([d0, d1], axis=1).astype(jnp.bfloat16)
                for c, value in enumerate((up, same, down)):
                    stage[:, pl.ds((3 * n + c) * cin, cin)] = value.reshape(SPAN * EDGE, cin)

        def taps(stage, columns):
            windows = [stage[b * EDGE : b * EDGE + AREA, :] for b in range(3)]
            return jnp.dot(jnp.concatenate(windows, axis=1), wide[:, columns], preferred_element_type=jnp.float32)

        def emit(q, low):
            value = jnp.maximum(high[...] + low + bias[...], 0.0).astype(result.dtype).T
            for n in range(2):
                mask = live[i, pl.ds(2 * q + n, 1)].astype(result.dtype)
                lanes = pl.ds(pl.multiple_of((2 * q + n) * AREA, AREA), AREA)
                result[i, :, lanes] = value[n * C : (n + 1) * C] * mask

        def advance(pair, stage):
            total = taps(stage, slice(None))
            emit(jnp.maximum(pair - 1, 0), total[:, : 2 * C])
            high[...] = total[:, 2 * C :]

        @pl.when(info[groups + k] > 0)
        def _():
            high[...] = jnp.zeros_like(high)
            arrived(i, 3)
            arrived(i, 0)
            build(stage_a, 0)
            mask_copy(i, brick).wait()

            @pl.when(i == first_active)
            def _():
                load.wait()

            @pl.loop(0, PAIRS // 2)
            def _(n):
                for c in (1, 2):

                    @pl.when(n == c)
                    def _():
                        arrived(i, c)

                build(stage_b, 2 * n + 1)
                advance(2 * n, stage_a)
                build(stage_a, 2 * n + 2)
                advance(2 * n + 1, stage_b)

            emit(PAIRS - 1, taps(stage_a, slice(0, 2 * C)))

        @pl.when(jnp.logical_and(info[groups + k] == 0, k < groups // 2))
        def _():
            result[i] = jnp.zeros(result.shape[1:], result.dtype)

        for n in range(many):

            @pl.when(jnp.logical_and(i == n, filled[n]))
            def _():
                store(n).start()

    for i in range(many):

        @pl.when(filled[i])
        def _():
            store(i).wait()


def convolve(picks, info, operands, spare=0):
    cin = operands[0].shape[-1]
    wide, masks = operands[7:9]
    many = len(picks)
    flops = 2 * (PAIRS + 1) * AREA * 18 * cin * 4 * C * many
    return pl.pallas_call(
        functools.partial(conv_kernel, picks, spare),
        out_shape=[pltpu.VMEM((C, VOXELS), jnp.bfloat16)] * (many + spare),
        in_specs=[pl.BlockSpec(memory_space=pltpu.SMEM)]
        + [pl.BlockSpec(memory_space=pl.ANY)] * 9
        + [pl.BlockSpec(memory_space=pltpu.VMEM)],
        out_specs=[pl.BlockSpec(memory_space=pl.ANY)] * (many + spare),
        scratch_shapes=[
            pltpu.VMEM((many, SPAN, SPAN, 3, EDGE, cin), jnp.bfloat16),
            pltpu.VMEM(wide.shape, wide.dtype),
            pltpu.VMEM((many, EDGE, AREA), masks.dtype),
            pltpu.VMEM((SPAN * EDGE, 6 * cin), jnp.bfloat16),
            pltpu.VMEM((SPAN * EDGE, 6 * cin), jnp.bfloat16),
            pltpu.VMEM((AREA, 2 * C), jnp.float32),
            pltpu.VMEM((many, C, VOXELS), jnp.bfloat16),
            pltpu.SemaphoreType.DMA((many, 4)),
            pltpu.SemaphoreType.DMA,
            pltpu.SemaphoreType.DMA((many,)),
            pltpu.SemaphoreType.DMA((many,)),
        ],
        compiler_params=pltpu.CompilerParams(vmem_limit_bytes=54 * 1024 * 1024),
        cost_estimate=pl.CostEstimate(flops=flops, bytes_accessed=8 << 20, transcendentals=0),
    )(info, *operands)


def gather_kernel(info, *refs):
    groups = info.shape[0] // 3
    bricks, (out, held, zero, in_sems, out_sems) = refs[:groups], refs[groups:]
    me = lax.axis_index("gy")

    def load(k):
        return pltpu.make_async_copy(bricks[k], held.at[k], in_sems.at[k])

    def store(k, source):
        return pltpu.make_async_copy(source, out.at[me ^ k], out_sems.at[k])

    full = [info[2 * groups + k] > 0 for k in range(groups)]
    for k in range(groups):

        @pl.when(full[k])
        def _():
            load(k).start()

    zero[...] = jnp.zeros_like(zero)
    for k in range(groups):

        @pl.when(jnp.logical_not(full[k]))
        def _():
            store(k, zero).start()

    for k in range(groups):

        @pl.when(full[k])
        def _():
            load(k).wait()
            store(k, held.at[k]).start()

    for k in range(groups):
        store(k, zero).wait()


def gather(info, bricks):
    groups = len(bricks)
    return pl.pallas_call(
        gather_kernel,
        out_shape=jax.ShapeDtypeStruct((groups, C, VOXELS), jnp.bfloat16),
        in_specs=[pl.BlockSpec(memory_space=pltpu.SMEM)] + [pl.BlockSpec(memory_space=pl.ANY)] * groups,
        out_specs=pl.BlockSpec(memory_space=pl.ANY),
        scratch_shapes=[
            pltpu.VMEM((groups, C, VOXELS), jnp.bfloat16),
            pltpu.VMEM((C, VOXELS), jnp.bfloat16),
            pltpu.SemaphoreType.DMA((groups,)),
            pltpu.SemaphoreType.DMA((groups,)),
        ],
        compiler_params=pltpu.CompilerParams(vmem_limit_bytes=24 * 1024 * 1024),
        cost_estimate=pl.CostEstimate(flops=0, bytes_accessed=8 << 20, transcendentals=0),
    )(info, *bricks)


def shift(value, axis, up):
    count = lax.axis_size(axis)
    if up:
        return lax.ppermute(value, axis, [(i, i + 1) for i in range(count - 1)])
    return lax.ppermute(value, axis, [(i + 1, i) for i in range(count - 1)])


def per_device(features, voxel_mask, brick_mask, owner, weights, bias):
    extent_x, extent_y, extent_z, channels_in = features.shape
    bricks_x, bricks_y, bricks_z = extent_x // EDGE, extent_y // EDGE, extent_z // EDGE
    count = bricks_x * bricks_y * bricks_z
    groups = lax.axis_size("gy")
    owner = owner.reshape(count)

    sends = sends_of(brick_mask, owner, groups)
    receives = lax.all_to_all(sends, "gy", split_axis=0, concat_axis=0, tiled=True)
    x_first, x_last, y_first, y_last, info, packed = faces(brick_mask, owner, sends, receives, voxel_mask, features)
    y_low = shift(y_last, "gy", True)
    y_high = shift(y_first, "gy", False)
    x_low = shift(x_last, "gx", True)
    x_high = shift(x_first, "gx", False)
    e_low = shift(jnp.concatenate([x_low[:, -1], x_high[:, -1]]), "gy", True)
    e_high = shift(jnp.concatenate([x_low[:, 0], x_high[:, 0]]), "gy", False)

    def partner(value, k):
        return lax.ppermute(value, "gy", [(i, i ^ k) for i in range(groups)])

    main, masks, wide = prepare(brick_mask, voxel_mask, features, weights)
    wide_bias = jnp.concatenate([bias, bias])[None, :]
    operands = (main, x_low, x_high, y_low, y_high, e_low, e_high, wide, masks, wide_bias)
    packed = packed[0]

    far = list(range(groups - 1, groups // 2 - 1, -1))
    near = list(range(groups // 2 - 1, 0, -1))
    received = [None] * groups
    (brick,) = convolve((far[0],), info, operands)
    for n, k in enumerate(far):
        picks = ((near + [0])[n],) + tuple(far[n + 1 : n + 2])
        upward = [(i, i ^ k) for i in range(groups) if i < i ^ k]
        downward = [(b, a) for a, b in upward]

        def exchange(pairs, value, info, *operands):
            if not pairs:
                *made, got = convolve(picks, info, operands, spare=1)
            else:
                got = lax.ppermute(value, "gy", pairs)
                made = convolve(picks, info, operands)
            return got, *made

        branches = [functools.partial(exchange, pairs) for pairs in ([], upward, downward, upward + downward)]
        case = jnp.bitwise_and(jnp.right_shift(packed, 2 * (k - groups // 2)), 3)
        received[k], local, *ahead = lax.switch(case, branches, brick, info, *operands)
        if picks[0]:
            received[picks[0]] = partner(local, picks[0])
        else:
            received[0] = local
        brick = ahead[0] if ahead else None
    return gather(info, received)[None]


def solution(mesh):
    return jax.shard_map(
        per_device,
        mesh=mesh,
        in_specs=(
            P("gx", "gy", None, None),
            P("gx", "gy", None),
            P("gx", "gy", None),
            P("gx", "gy", None, None),
            P(),
            P(),
        ),
        out_specs=P("gx", "gy", None, None),
        check_vma=False,
    )
```

```python
import functools

import jax
import jax.numpy as jnp
from jax import lax
from jax.experimental import pallas as pl
from jax.experimental.pallas import tpu as pltpu
from jax.sharding import PartitionSpec as P

C = 64
EDGE = 16
AREA = EDGE * EDGE
VOXELS = EDGE**3
PAIRS = EDGE // 2
SPAN = EDGE + 2
LITTLE = pl.CostEstimate(flops=0, bytes_accessed=1024, transcendentals=0)


def activity(voxels, flags, bx):
    layer = lax.broadcasted_iota(jnp.int32, voxels.shape, 2) // EDGE
    chosen = jnp.zeros(voxels.shape, jnp.int32)
    layers = voxels.shape[2] // EDGE
    for bz in range(layers):
        chosen = jnp.where(layer == bz, flags[bx * layers + bz], chosen)
    return (voxels * chosen).astype(jnp.float32)


def spread(values, mask):
    n, y, z, c = values.shape
    wide = jnp.broadcast_to(mask[..., None], values.shape).astype(jnp.bfloat16)
    return (values * wide).reshape(n, y, z // EDGE, EDGE, c)


def sends_kernel(flags, owner, sends, bricks):
    layers = flags.shape[2]
    count = owner.shape[0]
    for o in range(sends.shape[0]):
        sends[o] = 0
    for b in range(count):
        flag = flags[b // layers, 0, b % layers]
        sends[owner[b]] = flag
        bricks[b] = flag
        bricks[count + b] = owner[b]


def sends_of(brick_mask, owner, groups):
    return pl.pallas_call(
        sends_kernel,
        out_shape=[jax.ShapeDtypeStruct((n,), jnp.int32) for n in (groups, 2 * owner.shape[0])],
        in_specs=[pl.BlockSpec(memory_space=pltpu.SMEM)] * 2,
        out_specs=[pl.BlockSpec(memory_space=pltpu.SMEM)] * 2,
        cost_estimate=LITTLE,
    )(brick_mask, owner)


def plan(bricks, sends, receives, info, packed):
    groups = sends.shape[0]
    far = groups // 2
    me = lax.axis_index("gy")
    for k in range(groups):
        info[k] = 0
    count = bricks.shape[0] // 2
    for b in range(count):
        info[bricks[count + b] ^ me] = b
    total = jnp.int32(0)
    for k in range(groups):
        peer = me ^ k
        sent = sends[peer]
        info[groups + k] = sent
        info[2 * groups + k] = receives[peer] if k >= far else 1
        if k >= far:
            received = receives[peer]
            total = total | (jnp.where(peer > me, sent + 2 * received, received + 2 * sent) << (2 * (k - far)))
    packed[0] = total


def face_kernel(bricks, sends, receives, voxels, features, x_first, x_last, y_first, y_last, info, packed, v_raw, x_raw, y_raw, sems):
    rows = features.shape[0]
    sides = (0, rows - 1)
    columns = (0, features.shape[1] - 1)
    copies = [pltpu.make_async_copy(voxels, v_raw, sems.at[4])]
    copies += [pltpu.make_async_copy(features.at[:, pl.ds(y, 1)], y_raw.at[n], sems.at[n]) for n, y in enumerate(columns)]
    copies += [pltpu.make_async_copy(features.at[pl.ds(x, 1)], x_raw.at[n], sems.at[2 + n]) for n, x in enumerate(sides)]
    for copy in copies:
        copy.start()
    plan(bricks, sends, receives, info, packed)
    for copy in copies:
        copy.wait()
    for n, out in enumerate((y_first, y_last)):
        for bx in range(rows // EDGE):
            span = slice(bx * EDGE, (bx + 1) * EDGE)
            y = columns[n]
            out[span] = spread(y_raw[n, span], activity(v_raw[span, y : y + 1], bricks, bx))
    for n, out in enumerate((x_first, x_last)):
        x = sides[n]
        out[...] = spread(x_raw[n], activity(v_raw[x : x + 1], bricks, x // EDGE))


def faces(bricks, sends, receives, voxel_mask, features):
    groups = sends.shape[0]
    ex, ey, ez, cin = features.shape
    layers = ez // EDGE
    shapes = [(1, ey, layers, EDGE, cin)] * 2 + [(ex, 1, layers, EDGE, cin)] * 2
    return pl.pallas_call(
        face_kernel,
        out_shape=[jax.ShapeDtypeStruct(shape, features.dtype) for shape in shapes] + [jax.ShapeDtypeStruct((n,), jnp.int32) for n in (3 * groups, 1)],
        in_specs=[pl.BlockSpec(memory_space=pltpu.SMEM)] * 3 + [pl.BlockSpec(memory_space=pltpu.HBM)] * 2,
        out_specs=[pl.BlockSpec(memory_space=pltpu.VMEM)] * 4 + [pl.BlockSpec(memory_space=pltpu.SMEM)] * 2,
        scratch_shapes=[
            pltpu.VMEM(voxel_mask.shape, voxel_mask.dtype),
            pltpu.VMEM((2, 1, ey, ez, cin), features.dtype),
            pltpu.VMEM((2, ex, 1, ez, cin), features.dtype),
            pltpu.SemaphoreType.DMA((5,)),
        ],
        compiler_params=pltpu.CompilerParams(vmem_limit_bytes=24 * 1024 * 1024),
        cost_estimate=LITTLE,
    )(bricks, sends, receives, *(pltpu.with_memory_space_constraint(a, pltpu.HBM) for a in (voxel_mask, features)))


SLAB = 8


def prepare_kernel(flags, voxels, features, weights, main, masks, wide):
    step = pl.program_id(0)
    n, y, z = voxels.shape
    lanes = masks.shape[1]
    source = lax.broadcasted_iota(jnp.int32, (z, lanes), 0)
    lane = lax.broadcasted_iota(jnp.int32, (z, lanes), 1)
    pick = jnp.logical_and(source // EDGE == lane // AREA, source % EDGE == lane % EDGE)
    mask = activity(voxels[...], flags, step // (EDGE // SLAB))
    every = jnp.dot(
        mask.reshape(n * y, z).astype(jnp.bfloat16),
        jnp.where(pick, 1.0, 0.0).astype(jnp.bfloat16),
        preferred_element_type=jnp.float32,
    ).reshape(n, y, lanes)
    row = lax.broadcasted_iota(jnp.int32, (n, y, lanes), 1)
    column = lax.broadcasted_iota(jnp.int32, (n, y, lanes), 2) % AREA // EDGE
    masks[...] = jnp.sum(jnp.where(row == column, every, 0.0), axis=1)
    main[...] = spread(features[...], mask)

    @pl.when(step == 0)
    def _():
        cin = weights.shape[-1]
        for b in range(3):
            for j in range(2):
                for c in range(3):
                    parts = []
                    for t in range(4):
                        a = 2 + j - t
                        tap = weights[(a * 3 + b) * 3 + c] if 0 <= a <= 2 else jnp.zeros(weights.shape[1:], weights.dtype)
                        parts.append(tap.astype(jnp.float32))
                    block = jnp.concatenate(parts, axis=0).T
                    start = (6 * b + 3 * j + c) * cin
                    wide[start : start + cin, :] = block.astype(wide.dtype)


def prepare(bricks, voxel_mask, features, weights):
    ex, ey, ez, cin = features.shape
    cout = weights.shape[4]
    taps = weights.transpose(0, 1, 2, 4, 3).reshape(27, cout, cin)
    return pl.pallas_call(
        prepare_kernel,
        out_shape=[
            jax.ShapeDtypeStruct((ex, ey, ez // EDGE, EDGE, cin), features.dtype),
            jax.ShapeDtypeStruct((ex, ez // EDGE * AREA), jnp.float32),
            jax.ShapeDtypeStruct((18 * cin, 4 * cout), weights.dtype),
        ],
        grid=(ex // SLAB,),
        in_specs=[
            pl.BlockSpec(memory_space=pltpu.SMEM),
            pl.BlockSpec((SLAB, ey, ez), lambda i: (i, 0, 0)),
            pl.BlockSpec((SLAB, ey, ez, cin), lambda i: (i, 0, 0, 0)),
            pl.BlockSpec((27, cout, cin), lambda i: (0, 0, 0)),
        ],
        out_specs=[
            pl.BlockSpec((SLAB, ey, ez // EDGE, EDGE, cin), lambda i: (i, 0, 0, 0, 0)),
            pl.BlockSpec((SLAB, ez // EDGE * AREA), lambda i: (i, 0)),
            pl.BlockSpec((18 * cin, 4 * cout), lambda i: (0, 0)),
        ],
        compiler_params=pltpu.CompilerParams(vmem_limit_bytes=32 * 1024 * 1024),
        cost_estimate=pl.CostEstimate(flops=0, bytes_accessed=40 << 20, transcendentals=0),
    )(bricks, voxel_mask, pltpu.with_memory_space_constraint(features, pltpu.HBM), taps)


def conv_kernel(picks, spare, info, main, x_low, x_high, y_low, y_high, e_low, e_high, weights, masks, bias, *refs):
    many = len(picks)
    outs, refs = refs[:many], refs[many + spare :]
    raw, wide, live, stage_a, stage_b, high, result, raw_sems, wide_sem, live_sems, out_sems = refs
    groups = info.shape[0] // 3
    layers = main.shape[2]
    cin = main.shape[-1]
    rows = EDGE + 1
    pieces = ((0, 6), (6, 6), (12, 5))

    def pick(i):
        return functools.reduce(lambda old, n: jnp.where(i == n, picks[n], old), range(1, many), picks[0])

    def place(brick):
        bz = brick % layers
        return brick // layers, bz, jnp.clip(bz - 1, 0, layers - 3)

    def start(i, brick):
        bx, _, first = place(brick)
        tiles = pl.ds(first, 3)
        end = bx * rows
        for side in range(2):

            @pl.when(bx == side)
            def _():
                face = (x_low, x_high)[side].at[0, :, tiles]
                pltpu.make_async_copy(face, raw.at[i, end, pl.ds(1, EDGE)], raw_sems.at[i, 3]).start()

        pltpu.make_async_copy(e_low.at[bx, tiles], raw.at[i, end, 0], raw_sems.at[i, 3]).start()
        pltpu.make_async_copy(e_high.at[bx, tiles], raw.at[i, end, rows], raw_sems.at[i, 3]).start()
        for c, (plane, size) in enumerate(pieces):
            source = pl.ds(plane + bx * (EDGE - 1), size)
            planes = pl.ds(plane + 1 - bx, size)
            pltpu.make_async_copy(main.at[source, :, tiles], raw.at[i, planes, pl.ds(1, EDGE)], raw_sems.at[i, c]).start()
            pltpu.make_async_copy(y_low.at[source, 0, tiles], raw.at[i, planes, 0], raw_sems.at[i, c]).start()
            pltpu.make_async_copy(y_high.at[source, 0, tiles], raw.at[i, planes, rows], raw_sems.at[i, c]).start()

    def arrived(i, c):
        whole = raw.at[i, pl.ds(0, pieces[c][1] if c < 3 else 1)]
        pltpu.make_async_copy(whole, whole, raw_sems.at[i, c]).wait()

    def mask_copy(i, brick):
        bx, bz, _ = place(brick)
        rows = pl.ds(pl.multiple_of(bx * EDGE, EDGE), EDGE)
        lanes = pl.ds(pl.multiple_of(bz * AREA, AREA), AREA)
        return pltpu.make_async_copy(masks.at[rows, lanes], live.at[i], live_sems.at[i])

    def store(i):
        return pltpu.make_async_copy(result.at[i], outs[i], out_sems.at[i])

    active = [info[groups + k] > 0 for k in picks]
    some = functools.reduce(jnp.logical_or, active)
    filled = [jnp.logical_or(on, k < groups // 2) for on, k in zip(active, picks)]
    load = pltpu.make_async_copy(weights, wide, wide_sem)

    @pl.when(some)
    def _():
        load.start()

    @pl.loop(0, many)
    def _(i):
        k = pick(i)

        @pl.when(info[groups + k] > 0)
        def _():
            start(i, info[k])
            mask_copy(i, info[k]).start()

    first_active = jnp.where(active[0], 0, 1)

    row = lax.broadcasted_iota(jnp.int32, (SPAN, 8, cin), 1)

    @pl.loop(0, many)
    def _(i):
        k = pick(i)
        brick = info[k]
        _, bz, first = place(brick)
        centre = bz - first
        under = jnp.maximum(centre - 1, 0)
        over = jnp.minimum(centre + 1, 2)
        has_under = (bz > 0).astype(jnp.float32)
        has_over = (bz < layers - 1).astype(jnp.float32)

        def build(stage, pair):
            for n in range(2):
                plane = 2 * pair + n
                same = raw[i, plane, :, centre]
                middle = same.astype(jnp.float32)
                m0, m1 = middle[:, :8], middle[:, 8:]
                below = raw[i, plane, :, under].astype(jnp.float32)[:, 8:] * has_under
                above = raw[i, plane, :, over].astype(jnp.float32)[:, :8] * has_over
                u0 = jnp.where(row == 0, pltpu.roll(below, 1, 1), pltpu.roll(m0, 1, 1))
                u1 = jnp.where(row == 0, pltpu.roll(m0, 1, 1), pltpu.roll(m1, 1, 1))
                d0 = jnp.where(row == 7, pltpu.roll(m1, 7, 1), pltpu.roll(m0, 7, 1))
                d1 = jnp.where(row == 7, pltpu.roll(above, 7, 1), pltpu.roll(m1, 7, 1))
                up = jnp.concatenate([u0, u1], axis=1).astype(jnp.bfloat16)
                down = jnp.concatenate([d0, d1], axis=1).astype(jnp.bfloat16)
                for c, value in enumerate((up, same, down)):
                    stage[:, pl.ds((3 * n + c) * cin, cin)] = value.reshape(SPAN * EDGE, cin)

        def taps(stage, columns):
            windows = [stage[b * EDGE : b * EDGE + AREA, :] for b in range(3)]
            return jnp.dot(jnp.concatenate(windows, axis=1), wide[:, columns], preferred_element_type=jnp.float32)

        def emit(q, low):
            value = jnp.maximum(high[...] + low + bias[...], 0.0).astype(result.dtype).T
            for n in range(2):
                mask = live[i, pl.ds(2 * q + n, 1)].astype(result.dtype)
                lanes = pl.ds(pl.multiple_of((2 * q + n) * AREA, AREA), AREA)
                result[i, :, lanes] = value[n * C : (n + 1) * C] * mask

        def advance(pair, stage):
            total = taps(stage, slice(None))
            emit(jnp.maximum(pair - 1, 0), total[:, : 2 * C])
            high[...] = total[:, 2 * C :]

        @pl.when(info[groups + k] > 0)
        def _():
            high[...] = jnp.zeros_like(high)
            arrived(i, 3)
            arrived(i, 0)
            build(stage_a, 0)
            mask_copy(i, brick).wait()

            @pl.when(i == first_active)
            def _():
                load.wait()

            @pl.loop(0, PAIRS // 2)
            def _(n):
                for c in (1, 2):

                    @pl.when(n == c)
                    def _():
                        arrived(i, c)

                build(stage_b, 2 * n + 1)
                advance(2 * n, stage_a)
                build(stage_a, 2 * n + 2)
                advance(2 * n + 1, stage_b)

            emit(PAIRS - 1, taps(stage_a, slice(0, 2 * C)))

        @pl.when(jnp.logical_and(info[groups + k] == 0, k < groups // 2))
        def _():
            result[i] = jnp.zeros(result.shape[1:], result.dtype)

        for n in range(many):

            @pl.when(jnp.logical_and(i == n, filled[n]))
            def _():
                store(n).start()

    for i in range(many):

        @pl.when(filled[i])
        def _():
            store(i).wait()


def convolve(picks, info, operands, spare=0):
    cin = operands[0].shape[-1]
    wide, masks = operands[7:9]
    many = len(picks)
    flops = 2 * (PAIRS + 1) * AREA * 18 * cin * 4 * C * many
    return pl.pallas_call(
        functools.partial(conv_kernel, picks, spare),
        out_shape=[pltpu.VMEM((C, VOXELS), jnp.bfloat16)] * (many + spare),
        in_specs=[pl.BlockSpec(memory_space=pltpu.SMEM)]
        + [pl.BlockSpec(memory_space=pl.ANY)] * 9
        + [pl.BlockSpec(memory_space=pltpu.VMEM)],
        out_specs=[pl.BlockSpec(memory_space=pl.ANY)] * (many + spare),
        scratch_shapes=[
            pltpu.VMEM((many, SPAN, SPAN, 3, EDGE, cin), jnp.bfloat16),
            pltpu.VMEM(wide.shape, wide.dtype),
            pltpu.VMEM((many, EDGE, AREA), masks.dtype),
            pltpu.VMEM((SPAN * EDGE, 6 * cin), jnp.bfloat16),
            pltpu.VMEM((SPAN * EDGE, 6 * cin), jnp.bfloat16),
            pltpu.VMEM((AREA, 2 * C), jnp.float32),
            pltpu.VMEM((many, C, VOXELS), jnp.bfloat16),
            pltpu.SemaphoreType.DMA((many, 4)),
            pltpu.SemaphoreType.DMA,
            pltpu.SemaphoreType.DMA((many,)),
            pltpu.SemaphoreType.DMA((many,)),
        ],
        compiler_params=pltpu.CompilerParams(vmem_limit_bytes=54 * 1024 * 1024),
        cost_estimate=pl.CostEstimate(flops=flops, bytes_accessed=8 << 20, transcendentals=0),
    )(info, *operands)


def gather_kernel(info, *refs):
    groups = info.shape[0] // 3
    bricks, (out, held, zero, in_sems, out_sems) = refs[:groups], refs[groups:]
    me = lax.axis_index("gy")

    def load(k):
        return pltpu.make_async_copy(bricks[k], held.at[k], in_sems.at[k])

    def store(k, source):
        return pltpu.make_async_copy(source, out.at[me ^ k], out_sems.at[k])

    full = [info[2 * groups + k] > 0 for k in range(groups)]
    for k in range(groups):

        @pl.when(full[k])
        def _():
            load(k).start()

    zero[...] = jnp.zeros_like(zero)
    for k in range(groups):

        @pl.when(jnp.logical_not(full[k]))
        def _():
            store(k, zero).start()

    for k in range(groups):

        @pl.when(full[k])
        def _():
            load(k).wait()
            store(k, held.at[k]).start()

    for k in range(groups):
        store(k, zero).wait()


def gather(info, bricks):
    groups = len(bricks)
    return pl.pallas_call(
        gather_kernel,
        out_shape=jax.ShapeDtypeStruct((groups, C, VOXELS), jnp.bfloat16),
        in_specs=[pl.BlockSpec(memory_space=pltpu.SMEM)] + [pl.BlockSpec(memory_space=pl.ANY)] * groups,
        out_specs=pl.BlockSpec(memory_space=pl.ANY),
        scratch_shapes=[
            pltpu.VMEM((groups, C, VOXELS), jnp.bfloat16),
            pltpu.VMEM((C, VOXELS), jnp.bfloat16),
            pltpu.SemaphoreType.DMA((groups,)),
            pltpu.SemaphoreType.DMA((groups,)),
        ],
        compiler_params=pltpu.CompilerParams(vmem_limit_bytes=24 * 1024 * 1024),
        cost_estimate=pl.CostEstimate(flops=0, bytes_accessed=8 << 20, transcendentals=0),
    )(info, *bricks)


def shift(value, axis, up):
    count = lax.axis_size(axis)
    if up:
        return lax.ppermute(value, axis, [(i, i + 1) for i in range(count - 1)])
    return lax.ppermute(value, axis, [(i + 1, i) for i in range(count - 1)])


def per_device(features, voxel_mask, brick_mask, owner, weights, bias):
    extent_x, extent_y, extent_z, channels_in = features.shape
    bricks_x, bricks_y, bricks_z = extent_x // EDGE, extent_y // EDGE, extent_z // EDGE
    count = bricks_x * bricks_y * bricks_z
    groups = lax.axis_size("gy")
    owner = owner.reshape(count)

    sends, bricks = sends_of(brick_mask, owner, groups)
    receives = lax.all_to_all(sends, "gy", split_axis=0, concat_axis=0, tiled=True)
    x_first, x_last, y_first, y_last, info, packed = faces(bricks, sends, receives, voxel_mask, features)
    y_low = shift(y_last, "gy", True)
    y_high = shift(y_first, "gy", False)
    x_low = shift(x_last, "gx", True)
    x_high = shift(x_first, "gx", False)
    e_low = shift(jnp.concatenate([x_low[:, -1], x_high[:, -1]]), "gy", True)
    e_high = shift(jnp.concatenate([x_low[:, 0], x_high[:, 0]]), "gy", False)

    def partner(value, k):
        return lax.ppermute(value, "gy", [(i, i ^ k) for i in range(groups)])

    main, masks, wide = prepare(bricks, voxel_mask, features, weights)
    wide_bias = jnp.concatenate([bias, bias])[None, :]
    operands = (main, x_low, x_high, y_low, y_high, e_low, e_high, wide, masks, wide_bias)
    packed = packed[0]

    far = list(range(groups - 1, groups // 2 - 1, -1))
    near = list(range(groups // 2 - 1, 0, -1))
    received = [None] * groups
    (brick,) = convolve((far[0],), info, operands)
    for n, k in enumerate(far):
        picks = ((near + [0])[n],) + tuple(far[n + 1 : n + 2])
        upward = [(i, i ^ k) for i in range(groups) if i < i ^ k]
        downward = [(b, a) for a, b in upward]

        def exchange(pairs, value, info, *operands):
            if not pairs:
                *made, got = convolve(picks, info, operands, spare=1)
            else:
                got = lax.ppermute(value, "gy", pairs)
                made = convolve(picks, info, operands)
            return got, *made

        branches = [functools.partial(exchange, pairs) for pairs in ([], upward, downward, upward + downward)]
        case = jnp.bitwise_and(jnp.right_shift(packed, 2 * (k - groups // 2)), 3)
        received[k], local, *ahead = lax.switch(case, branches, brick, info, *operands)
        if picks[0]:
            received[picks[0]] = partner(local, picks[0])
        else:
            received[0] = local
        brick = ahead[0] if ahead else None
    return gather(info, received)[None]


def solution(mesh):
    return jax.shard_map(
        per_device,
        mesh=mesh,
        in_specs=(
            P("gx", "gy", None, None),
            P("gx", "gy", None),
            P("gx", "gy", None),
            P("gx", "gy", None, None),
            P(),
            P(),
        ),
        out_specs=P("gx", "gy", None, None),
        check_vma=False,
    )
```

```python
import functools

import jax
import jax.numpy as jnp
from jax import lax
from jax.experimental import pallas as pl
from jax.experimental.pallas import tpu as pltpu
from jax.sharding import PartitionSpec as P

C = 64
EDGE = 16
AREA = EDGE * EDGE
VOXELS = EDGE**3
PAIRS = EDGE // 2
SPAN = EDGE + 2
LITTLE = pl.CostEstimate(flops=0, bytes_accessed=1024, transcendentals=0)


def activity(voxels, flags, bx):
    layer = lax.broadcasted_iota(jnp.int32, voxels.shape, 2) // EDGE
    chosen = jnp.zeros(voxels.shape, jnp.int32)
    layers = voxels.shape[2] // EDGE
    for bz in range(layers):
        chosen = jnp.where(layer == bz, flags[bx * layers + bz], chosen)
    return (voxels * chosen).astype(jnp.float32)


def spread(values, mask):
    n, y, z, c = values.shape
    wide = jnp.broadcast_to(mask[..., None], values.shape).astype(jnp.bfloat16)
    return (values * wide).reshape(n, y, z // EDGE, EDGE, c)


def plan_kernel(bricks, sends, receives, info, packed):
    groups = sends.shape[0]
    far = groups // 2
    me = lax.axis_index("gy")
    for k in range(groups):
        info[k] = 0
    count = bricks.shape[0] // 2
    for b in range(count):
        info[bricks[count + b] ^ me] = b
    total = jnp.int32(0)
    for k in range(groups):
        peer = me ^ k
        sent = sends[peer]
        info[groups + k] = sent
        info[2 * groups + k] = receives[peer] if k >= far else 1
        if k >= far:
            received = receives[peer]
            total = total | (jnp.where(peer > me, sent + 2 * received, received + 2 * sent) << (2 * (k - far)))
    packed[0] = total


def plan(bricks, sends, receives):
    groups = sends.shape[0]
    return pl.pallas_call(
        plan_kernel,
        out_shape=[jax.ShapeDtypeStruct((n,), jnp.int32) for n in (3 * groups, 1)],
        in_specs=[pl.BlockSpec(memory_space=pltpu.SMEM)] * 3,
        out_specs=[pl.BlockSpec(memory_space=pltpu.SMEM)] * 2,
        cost_estimate=LITTLE,
    )(bricks, sends, receives)


def face_kernel(flags, owner, voxels, features, x_first, x_last, y_first, y_last, bricks, v_raw, x_raw, y_raw, sems):
    rows = features.shape[0]
    sides = (0, rows - 1)
    columns = (0, features.shape[1] - 1)
    copies = [pltpu.make_async_copy(voxels, v_raw, sems.at[4])]
    copies += [pltpu.make_async_copy(features.at[:, pl.ds(y, 1)], y_raw.at[n], sems.at[n]) for n, y in enumerate(columns)]
    copies += [pltpu.make_async_copy(features.at[pl.ds(x, 1)], x_raw.at[n], sems.at[2 + n]) for n, x in enumerate(sides)]
    for copy in copies:
        copy.start()
    count = owner.shape[0]
    layers = flags.shape[2]
    for b in range(count):
        bricks[b] = flags[b // layers, 0, b % layers]
        bricks[count + b] = owner[b]
    for copy in copies:
        copy.wait()
    for n, out in enumerate((y_first, y_last)):
        for bx in range(rows // EDGE):
            span = slice(bx * EDGE, (bx + 1) * EDGE)
            y = columns[n]
            out[span] = spread(y_raw[n, span], activity(v_raw[span, y : y + 1], bricks, bx))
    for n, out in enumerate((x_first, x_last)):
        x = sides[n]
        out[...] = spread(x_raw[n], activity(v_raw[x : x + 1], bricks, x // EDGE))


def faces(brick_mask, owner, voxel_mask, features):
    ex, ey, ez, cin = features.shape
    layers = ez // EDGE
    shapes = [(1, ey, layers, EDGE, cin)] * 2 + [(ex, 1, layers, EDGE, cin)] * 2
    return pl.pallas_call(
        face_kernel,
        out_shape=[jax.ShapeDtypeStruct(shape, features.dtype) for shape in shapes] + [jax.ShapeDtypeStruct((2 * owner.shape[0],), jnp.int32)],
        in_specs=[pl.BlockSpec(memory_space=pltpu.SMEM)] * 2 + [pl.BlockSpec(memory_space=pltpu.HBM)] * 2,
        out_specs=[pl.BlockSpec(memory_space=pltpu.VMEM)] * 4 + [pl.BlockSpec(memory_space=pltpu.SMEM)],
        scratch_shapes=[
            pltpu.VMEM(voxel_mask.shape, voxel_mask.dtype),
            pltpu.VMEM((2, 1, ey, ez, cin), features.dtype),
            pltpu.VMEM((2, ex, 1, ez, cin), features.dtype),
            pltpu.SemaphoreType.DMA((5,)),
        ],
        compiler_params=pltpu.CompilerParams(vmem_limit_bytes=24 * 1024 * 1024),
        cost_estimate=LITTLE,
    )(brick_mask, owner, *(pltpu.with_memory_space_constraint(a, pltpu.HBM) for a in (voxel_mask, features)))


SLAB = 8


def prepare_kernel(flags, voxels, features, weights, main, masks, wide, sends):
    step = pl.program_id(0)
    n, y, z = voxels.shape
    lanes = masks.shape[1]
    source = lax.broadcasted_iota(jnp.int32, (z, lanes), 0)
    lane = lax.broadcasted_iota(jnp.int32, (z, lanes), 1)
    pick = jnp.logical_and(source // EDGE == lane // AREA, source % EDGE == lane % EDGE)
    mask = activity(voxels[...], flags, step // (EDGE // SLAB))
    every = jnp.dot(
        mask.reshape(n * y, z).astype(jnp.bfloat16),
        jnp.where(pick, 1.0, 0.0).astype(jnp.bfloat16),
        preferred_element_type=jnp.float32,
    ).reshape(n, y, lanes)
    row = lax.broadcasted_iota(jnp.int32, (n, y, lanes), 1)
    column = lax.broadcasted_iota(jnp.int32, (n, y, lanes), 2) % AREA // EDGE
    masks[...] = jnp.sum(jnp.where(row == column, every, 0.0), axis=1)
    main[...] = spread(features[...], mask)

    @pl.when(step == 0)
    def _():
        count = flags.shape[0] // 2
        for o in range(sends.shape[0]):
            sends[o] = 0
        for b in range(count):
            sends[flags[count + b]] = flags[b]
        cin = weights.shape[-1]
        for b in range(3):
            for j in range(2):
                for c in range(3):
                    parts = []
                    for t in range(4):
                        a = 2 + j - t
                        tap = weights[(a * 3 + b) * 3 + c] if 0 <= a <= 2 else jnp.zeros(weights.shape[1:], weights.dtype)
                        parts.append(tap.astype(jnp.float32))
                    block = jnp.concatenate(parts, axis=0).T
                    start = (6 * b + 3 * j + c) * cin
                    wide[start : start + cin, :] = block.astype(wide.dtype)


def prepare(bricks, voxel_mask, features, weights, groups):
    ex, ey, ez, cin = features.shape
    cout = weights.shape[4]
    taps = weights.transpose(0, 1, 2, 4, 3).reshape(27, cout, cin)
    return pl.pallas_call(
        prepare_kernel,
        out_shape=[
            jax.ShapeDtypeStruct((ex, ey, ez // EDGE, EDGE, cin), features.dtype),
            jax.ShapeDtypeStruct((ex, ez // EDGE * AREA), jnp.float32),
            jax.ShapeDtypeStruct((18 * cin, 4 * cout), weights.dtype),
            jax.ShapeDtypeStruct((groups,), jnp.int32),
        ],
        grid=(ex // SLAB,),
        in_specs=[
            pl.BlockSpec(memory_space=pltpu.SMEM),
            pl.BlockSpec((SLAB, ey, ez), lambda i: (i, 0, 0)),
            pl.BlockSpec((SLAB, ey, ez, cin), lambda i: (i, 0, 0, 0)),
            pl.BlockSpec((27, cout, cin), lambda i: (0, 0, 0)),
        ],
        out_specs=[
            pl.BlockSpec((SLAB, ey, ez // EDGE, EDGE, cin), lambda i: (i, 0, 0, 0, 0)),
            pl.BlockSpec((SLAB, ez // EDGE * AREA), lambda i: (i, 0)),
            pl.BlockSpec((18 * cin, 4 * cout), lambda i: (0, 0)),
            pl.BlockSpec(memory_space=pltpu.SMEM),
        ],
        compiler_params=pltpu.CompilerParams(vmem_limit_bytes=32 * 1024 * 1024),
        cost_estimate=pl.CostEstimate(flops=0, bytes_accessed=40 << 20, transcendentals=0),
    )(bricks, voxel_mask, pltpu.with_memory_space_constraint(features, pltpu.HBM), taps)


def conv_kernel(picks, spare, info, main, x_low, x_high, y_low, y_high, e_low, e_high, weights, masks, bias, *refs):
    many = len(picks)
    outs, refs = refs[:many], refs[many + spare :]
    raw, wide, live, stage_a, stage_b, high, result, raw_sems, wide_sem, live_sems, out_sems = refs
    groups = info.shape[0] // 3
    layers = main.shape[2]
    cin = main.shape[-1]
    rows = EDGE + 1
    pieces = ((0, 6), (6, 6), (12, 5))

    def pick(i):
        return functools.reduce(lambda old, n: jnp.where(i == n, picks[n], old), range(1, many), picks[0])

    def place(brick):
        bz = brick % layers
        return brick // layers, bz, jnp.clip(bz - 1, 0, layers - 3)

    def start(i, brick):
        bx, _, first = place(brick)
        tiles = pl.ds(first, 3)
        end = bx * rows
        for side in range(2):

            @pl.when(bx == side)
            def _():
                face = (x_low, x_high)[side].at[0, :, tiles]
                pltpu.make_async_copy(face, raw.at[i, end, pl.ds(1, EDGE)], raw_sems.at[i, 3]).start()

        pltpu.make_async_copy(e_low.at[bx, tiles], raw.at[i, end, 0], raw_sems.at[i, 3]).start()
        pltpu.make_async_copy(e_high.at[bx, tiles], raw.at[i, end, rows], raw_sems.at[i, 3]).start()
        for c, (plane, size) in enumerate(pieces):
            source = pl.ds(plane + bx * (EDGE - 1), size)
            planes = pl.ds(plane + 1 - bx, size)
            pltpu.make_async_copy(main.at[source, :, tiles], raw.at[i, planes, pl.ds(1, EDGE)], raw_sems.at[i, c]).start()
            pltpu.make_async_copy(y_low.at[source, 0, tiles], raw.at[i, planes, 0], raw_sems.at[i, c]).start()
            pltpu.make_async_copy(y_high.at[source, 0, tiles], raw.at[i, planes, rows], raw_sems.at[i, c]).start()

    def arrived(i, c):
        whole = raw.at[i, pl.ds(0, pieces[c][1] if c < 3 else 1)]
        pltpu.make_async_copy(whole, whole, raw_sems.at[i, c]).wait()

    def mask_copy(i, brick):
        bx, bz, _ = place(brick)
        rows = pl.ds(pl.multiple_of(bx * EDGE, EDGE), EDGE)
        lanes = pl.ds(pl.multiple_of(bz * AREA, AREA), AREA)
        return pltpu.make_async_copy(masks.at[rows, lanes], live.at[i], live_sems.at[i])

    def store(i):
        return pltpu.make_async_copy(result.at[i], outs[i], out_sems.at[i])

    active = [info[groups + k] > 0 for k in picks]
    some = functools.reduce(jnp.logical_or, active)
    filled = [jnp.logical_or(on, k < groups // 2) for on, k in zip(active, picks)]
    load = pltpu.make_async_copy(weights, wide, wide_sem)

    @pl.when(some)
    def _():
        load.start()

    @pl.loop(0, many)
    def _(i):
        k = pick(i)

        @pl.when(info[groups + k] > 0)
        def _():
            start(i, info[k])
            mask_copy(i, info[k]).start()

    first_active = jnp.where(active[0], 0, 1)

    row = lax.broadcasted_iota(jnp.int32, (SPAN, 8, cin), 1)

    @pl.loop(0, many)
    def _(i):
        k = pick(i)
        brick = info[k]
        _, bz, first = place(brick)
        centre = bz - first
        under = jnp.maximum(centre - 1, 0)
        over = jnp.minimum(centre + 1, 2)
        has_under = (bz > 0).astype(jnp.float32)
        has_over = (bz < layers - 1).astype(jnp.float32)

        def build(stage, pair):
            for n in range(2):
                plane = 2 * pair + n
                same = raw[i, plane, :, centre]
                middle = same.astype(jnp.float32)
                m0, m1 = middle[:, :8], middle[:, 8:]
                below = raw[i, plane, :, under].astype(jnp.float32)[:, 8:] * has_under
                above = raw[i, plane, :, over].astype(jnp.float32)[:, :8] * has_over
                u0 = jnp.where(row == 0, pltpu.roll(below, 1, 1), pltpu.roll(m0, 1, 1))
                u1 = jnp.where(row == 0, pltpu.roll(m0, 1, 1), pltpu.roll(m1, 1, 1))
                d0 = jnp.where(row == 7, pltpu.roll(m1, 7, 1), pltpu.roll(m0, 7, 1))
                d1 = jnp.where(row == 7, pltpu.roll(above, 7, 1), pltpu.roll(m1, 7, 1))
                up = jnp.concatenate([u0, u1], axis=1).astype(jnp.bfloat16)
                down = jnp.concatenate([d0, d1], axis=1).astype(jnp.bfloat16)
                for c, value in enumerate((up, same, down)):
                    stage[:, pl.ds((3 * n + c) * cin, cin)] = value.reshape(SPAN * EDGE, cin)

        def taps(stage, columns):
            windows = [stage[b * EDGE : b * EDGE + AREA, :] for b in range(3)]
            return jnp.dot(jnp.concatenate(windows, axis=1), wide[:, columns], preferred_element_type=jnp.float32)

        def emit(q, low):
            value = jnp.maximum(high[...] + low + bias[...], 0.0).astype(result.dtype).T
            for n in range(2):
                mask = live[i, pl.ds(2 * q + n, 1)].astype(result.dtype)
                lanes = pl.ds(pl.multiple_of((2 * q + n) * AREA, AREA), AREA)
                result[i, :, lanes] = value[n * C : (n + 1) * C] * mask

        def advance(pair, stage):
            total = taps(stage, slice(None))
            emit(jnp.maximum(pair - 1, 0), total[:, : 2 * C])
            high[...] = total[:, 2 * C :]

        @pl.when(info[groups + k] > 0)
        def _():
            high[...] = jnp.zeros_like(high)
            arrived(i, 3)
            arrived(i, 0)
            build(stage_a, 0)
            mask_copy(i, brick).wait()

            @pl.when(i == first_active)
            def _():
                load.wait()

            @pl.loop(0, PAIRS // 2)
            def _(n):
                for c in (1, 2):

                    @pl.when(n == c)
                    def _():
                        arrived(i, c)

                build(stage_b, 2 * n + 1)
                advance(2 * n, stage_a)
                build(stage_a, 2 * n + 2)
                advance(2 * n + 1, stage_b)

            emit(PAIRS - 1, taps(stage_a, slice(0, 2 * C)))

        @pl.when(jnp.logical_and(info[groups + k] == 0, k < groups // 2))
        def _():
            result[i] = jnp.zeros(result.shape[1:], result.dtype)

        for n in range(many):

            @pl.when(jnp.logical_and(i == n, filled[n]))
            def _():
                store(n).start()

    for i in range(many):

        @pl.when(filled[i])
        def _():
            store(i).wait()


def convolve(picks, info, operands, spare=0):
    cin = operands[0].shape[-1]
    wide, masks = operands[7:9]
    many = len(picks)
    flops = 2 * (PAIRS + 1) * AREA * 18 * cin * 4 * C * many
    return pl.pallas_call(
        functools.partial(conv_kernel, picks, spare),
        out_shape=[pltpu.VMEM((C, VOXELS), jnp.bfloat16)] * (many + spare),
        in_specs=[pl.BlockSpec(memory_space=pltpu.SMEM)]
        + [pl.BlockSpec(memory_space=pl.ANY)] * 9
        + [pl.BlockSpec(memory_space=pltpu.VMEM)],
        out_specs=[pl.BlockSpec(memory_space=pl.ANY)] * (many + spare),
        scratch_shapes=[
            pltpu.VMEM((many, SPAN, SPAN, 3, EDGE, cin), jnp.bfloat16),
            pltpu.VMEM(wide.shape, wide.dtype),
            pltpu.VMEM((many, EDGE, AREA), masks.dtype),
            pltpu.VMEM((SPAN * EDGE, 6 * cin), jnp.bfloat16),
            pltpu.VMEM((SPAN * EDGE, 6 * cin), jnp.bfloat16),
            pltpu.VMEM((AREA, 2 * C), jnp.float32),
            pltpu.VMEM((many, C, VOXELS), jnp.bfloat16),
            pltpu.SemaphoreType.DMA((many, 4)),
            pltpu.SemaphoreType.DMA,
            pltpu.SemaphoreType.DMA((many,)),
            pltpu.SemaphoreType.DMA((many,)),
        ],
        compiler_params=pltpu.CompilerParams(vmem_limit_bytes=54 * 1024 * 1024),
        cost_estimate=pl.CostEstimate(flops=flops, bytes_accessed=8 << 20, transcendentals=0),
    )(info, *operands)


def gather_kernel(info, *refs):
    groups = info.shape[0] // 3
    bricks, (out, held, zero, in_sems, out_sems) = refs[:groups], refs[groups:]
    me = lax.axis_index("gy")

    def load(k):
        return pltpu.make_async_copy(bricks[k], held.at[k], in_sems.at[k])

    def store(k, source):
        return pltpu.make_async_copy(source, out.at[me ^ k], out_sems.at[k])

    full = [info[2 * groups + k] > 0 for k in range(groups)]
    for k in range(groups):

        @pl.when(full[k])
        def _():
            load(k).start()

    zero[...] = jnp.zeros_like(zero)
    for k in range(groups):

        @pl.when(jnp.logical_not(full[k]))
        def _():
            store(k, zero).start()

    for k in range(groups):

        @pl.when(full[k])
        def _():
            load(k).wait()
            store(k, held.at[k]).start()

    for k in range(groups):
        store(k, zero).wait()


def gather(info, bricks):
    groups = len(bricks)
    return pl.pallas_call(
        gather_kernel,
        out_shape=jax.ShapeDtypeStruct((groups, C, VOXELS), jnp.bfloat16),
        in_specs=[pl.BlockSpec(memory_space=pltpu.SMEM)] + [pl.BlockSpec(memory_space=pl.ANY)] * groups,
        out_specs=pl.BlockSpec(memory_space=pl.ANY),
        scratch_shapes=[
            pltpu.VMEM((groups, C, VOXELS), jnp.bfloat16),
            pltpu.VMEM((C, VOXELS), jnp.bfloat16),
            pltpu.SemaphoreType.DMA((groups,)),
            pltpu.SemaphoreType.DMA((groups,)),
        ],
        compiler_params=pltpu.CompilerParams(vmem_limit_bytes=24 * 1024 * 1024),
        cost_estimate=pl.CostEstimate(flops=0, bytes_accessed=8 << 20, transcendentals=0),
    )(info, *bricks)


def shift(value, axis, up):
    count = lax.axis_size(axis)
    if up:
        return lax.ppermute(value, axis, [(i, i + 1) for i in range(count - 1)])
    return lax.ppermute(value, axis, [(i + 1, i) for i in range(count - 1)])


def per_device(features, voxel_mask, brick_mask, owner, weights, bias):
    extent_x, extent_y, extent_z, channels_in = features.shape
    bricks_x, bricks_y, bricks_z = extent_x // EDGE, extent_y // EDGE, extent_z // EDGE
    count = bricks_x * bricks_y * bricks_z
    groups = lax.axis_size("gy")
    owner = owner.reshape(count)

    x_first, x_last, y_first, y_last, bricks = faces(brick_mask, owner, voxel_mask, features)
    y_low = shift(y_last, "gy", True)
    y_high = shift(y_first, "gy", False)
    x_low = shift(x_last, "gx", True)
    x_high = shift(x_first, "gx", False)
    e_low = shift(jnp.concatenate([x_low[:, -1], x_high[:, -1]]), "gy", True)
    e_high = shift(jnp.concatenate([x_low[:, 0], x_high[:, 0]]), "gy", False)

    def partner(value, k):
        return lax.ppermute(value, "gy", [(i, i ^ k) for i in range(groups)])

    main, masks, wide, sends = prepare(bricks, voxel_mask, features, weights, groups)
    receives = lax.all_to_all(sends, "gy", split_axis=0, concat_axis=0, tiled=True)
    info, packed = plan(bricks, sends, receives)
    wide_bias = jnp.concatenate([bias, bias])[None, :]
    operands = (main, x_low, x_high, y_low, y_high, e_low, e_high, wide, masks, wide_bias)
    packed = packed[0]

    far = list(range(groups - 1, groups // 2 - 1, -1))
    near = list(range(groups // 2 - 1, 0, -1))
    received = [None] * groups
    (brick,) = convolve((far[0],), info, operands)
    for n, k in enumerate(far):
        picks = ((near + [0])[n],) + tuple(far[n + 1 : n + 2])
        upward = [(i, i ^ k) for i in range(groups) if i < i ^ k]
        downward = [(b, a) for a, b in upward]

        def exchange(pairs, value, info, *operands):
            if not pairs:
                *made, got = convolve(picks, info, operands, spare=1)
            else:
                got = lax.ppermute(value, "gy", pairs)
                made = convolve(picks, info, operands)
            return got, *made

        branches = [functools.partial(exchange, pairs) for pairs in ([], upward, downward, upward + downward)]
        case = jnp.bitwise_and(jnp.right_shift(packed, 2 * (k - groups // 2)), 3)
        received[k], local, *ahead = lax.switch(case, branches, brick, info, *operands)
        if picks[0]:
            received[picks[0]] = partner(local, picks[0])
        else:
            received[0] = local
        brick = ahead[0] if ahead else None
    return gather(info, received)[None]


def solution(mesh):
    return jax.shard_map(
        per_device,
        mesh=mesh,
        in_specs=(
            P("gx", "gy", None, None),
            P("gx", "gy", None),
            P("gx", "gy", None),
            P("gx", "gy", None, None),
            P(),
            P(),
        ),
        out_specs=P("gx", "gy", None, None),
        check_vma=False,
    )
```

```python
import functools

import jax
import jax.numpy as jnp
from jax import lax
from jax.experimental import pallas as pl
from jax.experimental.pallas import tpu as pltpu
from jax.sharding import PartitionSpec as P

C = 64
EDGE = 16
AREA = EDGE * EDGE
VOXELS = EDGE**3
PAIRS = EDGE // 2
SPAN = EDGE + 2
LITTLE = pl.CostEstimate(flops=0, bytes_accessed=1024, transcendentals=0)


def activity(voxels, flags, bx):
    layer = lax.broadcasted_iota(jnp.int32, voxels.shape, 2) // EDGE
    chosen = jnp.zeros(voxels.shape, jnp.int32)
    layers = voxels.shape[2] // EDGE
    for bz in range(layers):
        chosen = jnp.where(layer == bz, flags[bx * layers + bz], chosen)
    return (voxels * chosen).astype(jnp.float32)


def spread(values, mask):
    n, y, z, c = values.shape
    wide = jnp.broadcast_to(mask[..., None], values.shape).astype(jnp.bfloat16)
    return (values * wide).reshape(n, y, z // EDGE, EDGE, c)


def plan_kernel(bricks, sends, receives, info, packed):
    groups = sends.shape[0]
    far = groups // 2
    me = lax.axis_index("gy")
    for k in range(groups):
        info[k] = 0
    count = bricks.shape[0] // 2
    for b in range(count):
        info[bricks[count + b] ^ me] = b
    total = jnp.int32(0)
    for k in range(groups):
        peer = me ^ k
        sent = sends[peer, 0]
        info[groups + k] = sent
        info[2 * groups + k] = receives[peer, 0] if k >= far else 1
        if k >= far:
            received = receives[peer, 0]
            total = total | (jnp.where(peer > me, sent + 2 * received, received + 2 * sent) << (2 * (k - far)))
    packed[0] = total


def plan(bricks, sends, receives):
    groups = sends.shape[0]
    return pl.pallas_call(
        plan_kernel,
        out_shape=[jax.ShapeDtypeStruct((n,), jnp.int32) for n in (3 * groups, 1)],
        in_specs=[pl.BlockSpec(memory_space=pltpu.SMEM)] * 3,
        out_specs=[pl.BlockSpec(memory_space=pltpu.SMEM)] * 2,
        cost_estimate=LITTLE,
    )(bricks, sends, receives)


def face_kernel(flags, owner, voxels, features, x_first, x_last, y_first, y_last, bricks, sends, v_raw, x_raw, y_raw, sems):
    rows = features.shape[0]
    sides = (0, rows - 1)
    columns = (0, features.shape[1] - 1)
    copies = [pltpu.make_async_copy(voxels, v_raw, sems.at[4])]
    copies += [pltpu.make_async_copy(features.at[:, pl.ds(y, 1)], y_raw.at[n], sems.at[n]) for n, y in enumerate(columns)]
    copies += [pltpu.make_async_copy(features.at[pl.ds(x, 1)], x_raw.at[n], sems.at[2 + n]) for n, x in enumerate(sides)]
    for copy in copies:
        copy.start()
    count = owner.shape[0]
    layers = flags.shape[2]
    for o in range(sends.shape[0]):
        sends[o, 0] = 0
    for b in range(count):
        flag = flags[b // layers, 0, b % layers]
        sends[owner[b], 0] = flag
        bricks[b] = flag
        bricks[count + b] = owner[b]
    for copy in copies:
        copy.wait()
    for n, out in enumerate((y_first, y_last)):
        for bx in range(rows // EDGE):
            span = slice(bx * EDGE, (bx + 1) * EDGE)
            y = columns[n]
            out[span] = spread(y_raw[n, span], activity(v_raw[span, y : y + 1], bricks, bx))
    for n, out in enumerate((x_first, x_last)):
        x = sides[n]
        out[...] = spread(x_raw[n], activity(v_raw[x : x + 1], bricks, x // EDGE))


def faces(brick_mask, owner, voxel_mask, features, groups):
    ex, ey, ez, cin = features.shape
    layers = ez // EDGE
    shapes = [(1, ey, layers, EDGE, cin)] * 2 + [(ex, 1, layers, EDGE, cin)] * 2
    return pl.pallas_call(
        face_kernel,
        out_shape=[jax.ShapeDtypeStruct(shape, features.dtype) for shape in shapes] + [jax.ShapeDtypeStruct(n, jnp.int32) for n in ((2 * owner.shape[0],), (groups, 128))],
        in_specs=[pl.BlockSpec(memory_space=pltpu.SMEM)] * 2 + [pl.BlockSpec(memory_space=pltpu.HBM)] * 2,
        out_specs=[pl.BlockSpec(memory_space=pltpu.VMEM)] * 4 + [pl.BlockSpec(memory_space=pltpu.SMEM)] * 2,
        scratch_shapes=[
            pltpu.VMEM(voxel_mask.shape, voxel_mask.dtype),
            pltpu.VMEM((2, 1, ey, ez, cin), features.dtype),
            pltpu.VMEM((2, ex, 1, ez, cin), features.dtype),
            pltpu.SemaphoreType.DMA((5,)),
        ],
        compiler_params=pltpu.CompilerParams(vmem_limit_bytes=24 * 1024 * 1024),
        cost_estimate=LITTLE,
    )(brick_mask, owner, *(pltpu.with_memory_space_constraint(a, pltpu.HBM) for a in (voxel_mask, features)))


SLAB = 8


def prepare_kernel(flags, voxels, features, weights, main, masks, wide):
    step = pl.program_id(0)
    n, y, z = voxels.shape
    lanes = masks.shape[1]
    source = lax.broadcasted_iota(jnp.int32, (z, lanes), 0)
    lane = lax.broadcasted_iota(jnp.int32, (z, lanes), 1)
    pick = jnp.logical_and(source // EDGE == lane // AREA, source % EDGE == lane % EDGE)
    mask = activity(voxels[...], flags, step // (EDGE // SLAB))
    every = jnp.dot(
        mask.reshape(n * y, z).astype(jnp.bfloat16),
        jnp.where(pick, 1.0, 0.0).astype(jnp.bfloat16),
        preferred_element_type=jnp.float32,
    ).reshape(n, y, lanes)
    row = lax.broadcasted_iota(jnp.int32, (n, y, lanes), 1)
    column = lax.broadcasted_iota(jnp.int32, (n, y, lanes), 2) % AREA // EDGE
    masks[...] = jnp.sum(jnp.where(row == column, every, 0.0), axis=1)
    main[...] = spread(features[...], mask)

    @pl.when(step == 0)
    def _():
        cin = weights.shape[-1]
        for b in range(3):
            for j in range(2):
                for c in range(3):
                    parts = []
                    for t in range(4):
                        a = 2 + j - t
                        tap = weights[(a * 3 + b) * 3 + c] if 0 <= a <= 2 else jnp.zeros(weights.shape[1:], weights.dtype)
                        parts.append(tap.astype(jnp.float32))
                    block = jnp.concatenate(parts, axis=0).T
                    start = (6 * b + 3 * j + c) * cin
                    wide[start : start + cin, :] = block.astype(wide.dtype)


def prepare(bricks, voxel_mask, features, weights):
    ex, ey, ez, cin = features.shape
    cout = weights.shape[4]
    taps = weights.transpose(0, 1, 2, 4, 3).reshape(27, cout, cin)
    return pl.pallas_call(
        prepare_kernel,
        out_shape=[
            jax.ShapeDtypeStruct((ex, ey, ez // EDGE, EDGE, cin), features.dtype),
            jax.ShapeDtypeStruct((ex, ez // EDGE * AREA), jnp.float32),
            jax.ShapeDtypeStruct((18 * cin, 4 * cout), weights.dtype),
        ],
        grid=(ex // SLAB,),
        in_specs=[
            pl.BlockSpec(memory_space=pltpu.SMEM),
            pl.BlockSpec((SLAB, ey, ez), lambda i: (i, 0, 0)),
            pl.BlockSpec((SLAB, ey, ez, cin), lambda i: (i, 0, 0, 0)),
            pl.BlockSpec((27, cout, cin), lambda i: (0, 0, 0)),
        ],
        out_specs=[
            pl.BlockSpec((SLAB, ey, ez // EDGE, EDGE, cin), lambda i: (i, 0, 0, 0, 0)),
            pl.BlockSpec((SLAB, ez // EDGE * AREA), lambda i: (i, 0)),
            pl.BlockSpec((18 * cin, 4 * cout), lambda i: (0, 0)),
        ],
        compiler_params=pltpu.CompilerParams(vmem_limit_bytes=32 * 1024 * 1024),
        cost_estimate=pl.CostEstimate(flops=0, bytes_accessed=40 << 20, transcendentals=0),
    )(bricks, voxel_mask, pltpu.with_memory_space_constraint(features, pltpu.HBM), taps)


def conv_kernel(picks, spare, info, main, x_low, x_high, y_low, y_high, e_low, e_high, weights, masks, bias, *refs):
    many = len(picks)
    outs, refs = refs[:many], refs[many + spare :]
    raw, wide, live, stage_a, stage_b, high, result, raw_sems, wide_sem, live_sems, out_sems = refs
    groups = info.shape[0] // 3
    layers = main.shape[2]
    cin = main.shape[-1]
    rows = EDGE + 1
    pieces = ((0, 6), (6, 6), (12, 5))

    def pick(i):
        return functools.reduce(lambda old, n: jnp.where(i == n, picks[n], old), range(1, many), picks[0])

    def place(brick):
        bz = brick % layers
        return brick // layers, bz, jnp.clip(bz - 1, 0, layers - 3)

    def start(i, brick):
        bx, _, first = place(brick)
        tiles = pl.ds(first, 3)
        end = bx * rows
        for side in range(2):

            @pl.when(bx == side)
            def _():
                face = (x_low, x_high)[side].at[0, :, tiles]
                pltpu.make_async_copy(face, raw.at[i, end, pl.ds(1, EDGE)], raw_sems.at[i, 3]).start()

        pltpu.make_async_copy(e_low.at[bx, tiles], raw.at[i, end, 0], raw_sems.at[i, 3]).start()
        pltpu.make_async_copy(e_high.at[bx, tiles], raw.at[i, end, rows], raw_sems.at[i, 3]).start()
        for c, (plane, size) in enumerate(pieces):
            source = pl.ds(plane + bx * (EDGE - 1), size)
            planes = pl.ds(plane + 1 - bx, size)
            pltpu.make_async_copy(main.at[source, :, tiles], raw.at[i, planes, pl.ds(1, EDGE)], raw_sems.at[i, c]).start()
            pltpu.make_async_copy(y_low.at[source, 0, tiles], raw.at[i, planes, 0], raw_sems.at[i, c]).start()
            pltpu.make_async_copy(y_high.at[source, 0, tiles], raw.at[i, planes, rows], raw_sems.at[i, c]).start()

    def arrived(i, c):
        whole = raw.at[i, pl.ds(0, pieces[c][1] if c < 3 else 1)]
        pltpu.make_async_copy(whole, whole, raw_sems.at[i, c]).wait()

    def mask_copy(i, brick):
        bx, bz, _ = place(brick)
        rows = pl.ds(pl.multiple_of(bx * EDGE, EDGE), EDGE)
        lanes = pl.ds(pl.multiple_of(bz * AREA, AREA), AREA)
        return pltpu.make_async_copy(masks.at[rows, lanes], live.at[i], live_sems.at[i])

    def store(i):
        return pltpu.make_async_copy(result.at[i], outs[i], out_sems.at[i])

    active = [info[groups + k] > 0 for k in picks]
    some = functools.reduce(jnp.logical_or, active)
    filled = [jnp.logical_or(on, k < groups // 2) for on, k in zip(active, picks)]
    load = pltpu.make_async_copy(weights, wide, wide_sem)

    @pl.when(some)
    def _():
        load.start()

    @pl.loop(0, many)
    def _(i):
        k = pick(i)

        @pl.when(info[groups + k] > 0)
        def _():
            start(i, info[k])
            mask_copy(i, info[k]).start()

    first_active = jnp.where(active[0], 0, 1)

    row = lax.broadcasted_iota(jnp.int32, (SPAN, 8, cin), 1)

    @pl.loop(0, many)
    def _(i):
        k = pick(i)
        brick = info[k]
        _, bz, first = place(brick)
        centre = bz - first
        under = jnp.maximum(centre - 1, 0)
        over = jnp.minimum(centre + 1, 2)
        has_under = (bz > 0).astype(jnp.float32)
        has_over = (bz < layers - 1).astype(jnp.float32)

        def build(stage, pair):
            for n in range(2):
                plane = 2 * pair + n
                same = raw[i, plane, :, centre]
                middle = same.astype(jnp.float32)
                m0, m1 = middle[:, :8], middle[:, 8:]
                below = raw[i, plane, :, under].astype(jnp.float32)[:, 8:] * has_under
                above = raw[i, plane, :, over].astype(jnp.float32)[:, :8] * has_over
                u0 = jnp.where(row == 0, pltpu.roll(below, 1, 1), pltpu.roll(m0, 1, 1))
                u1 = jnp.where(row == 0, pltpu.roll(m0, 1, 1), pltpu.roll(m1, 1, 1))
                d0 = jnp.where(row == 7, pltpu.roll(m1, 7, 1), pltpu.roll(m0, 7, 1))
                d1 = jnp.where(row == 7, pltpu.roll(above, 7, 1), pltpu.roll(m1, 7, 1))
                up = jnp.concatenate([u0, u1], axis=1).astype(jnp.bfloat16)
                down = jnp.concatenate([d0, d1], axis=1).astype(jnp.bfloat16)
                for c, value in enumerate((up, same, down)):
                    stage[:, pl.ds((3 * n + c) * cin, cin)] = value.reshape(SPAN * EDGE, cin)

        def taps(stage, columns):
            windows = [stage[b * EDGE : b * EDGE + AREA, :] for b in range(3)]
            return jnp.dot(jnp.concatenate(windows, axis=1), wide[:, columns], preferred_element_type=jnp.float32)

        def emit(q, low):
            value = jnp.maximum(high[...] + low + bias[...], 0.0).astype(result.dtype).T
            for n in range(2):
                mask = live[i, pl.ds(2 * q + n, 1)].astype(result.dtype)
                lanes = pl.ds(pl.multiple_of((2 * q + n) * AREA, AREA), AREA)
                result[i, :, lanes] = value[n * C : (n + 1) * C] * mask

        def advance(pair, stage):
            total = taps(stage, slice(None))
            emit(jnp.maximum(pair - 1, 0), total[:, : 2 * C])
            high[...] = total[:, 2 * C :]

        @pl.when(info[groups + k] > 0)
        def _():
            high[...] = jnp.zeros_like(high)
            arrived(i, 3)
            arrived(i, 0)
            build(stage_a, 0)
            mask_copy(i, brick).wait()

            @pl.when(i == first_active)
            def _():
                load.wait()

            @pl.loop(0, PAIRS // 2)
            def _(n):
                for c in (1, 2):

                    @pl.when(n == c)
                    def _():
                        arrived(i, c)

                build(stage_b, 2 * n + 1)
                advance(2 * n, stage_a)
                build(stage_a, 2 * n + 2)
                advance(2 * n + 1, stage_b)

            emit(PAIRS - 1, taps(stage_a, slice(0, 2 * C)))

        @pl.when(jnp.logical_and(info[groups + k] == 0, k < groups // 2))
        def _():
            result[i] = jnp.zeros(result.shape[1:], result.dtype)

        for n in range(many):

            @pl.when(jnp.logical_and(i == n, filled[n]))
            def _():
                store(n).start()

    for i in range(many):

        @pl.when(filled[i])
        def _():
            store(i).wait()


def convolve(picks, info, operands, spare=0):
    cin = operands[0].shape[-1]
    wide, masks = operands[7:9]
    many = len(picks)
    flops = 2 * (PAIRS + 1) * AREA * 18 * cin * 4 * C * many
    return pl.pallas_call(
        functools.partial(conv_kernel, picks, spare),
        out_shape=[pltpu.VMEM((C, VOXELS), jnp.bfloat16)] * (many + spare),
        in_specs=[pl.BlockSpec(memory_space=pltpu.SMEM)]
        + [pl.BlockSpec(memory_space=pl.ANY)] * 9
        + [pl.BlockSpec(memory_space=pltpu.VMEM)],
        out_specs=[pl.BlockSpec(memory_space=pl.ANY)] * (many + spare),
        scratch_shapes=[
            pltpu.VMEM((many, SPAN, SPAN, 3, EDGE, cin), jnp.bfloat16),
            pltpu.VMEM(wide.shape, wide.dtype),
            pltpu.VMEM((many, EDGE, AREA), masks.dtype),
            pltpu.VMEM((SPAN * EDGE, 6 * cin), jnp.bfloat16),
            pltpu.VMEM((SPAN * EDGE, 6 * cin), jnp.bfloat16),
            pltpu.VMEM((AREA, 2 * C), jnp.float32),
            pltpu.VMEM((many, C, VOXELS), jnp.bfloat16),
            pltpu.SemaphoreType.DMA((many, 4)),
            pltpu.SemaphoreType.DMA,
            pltpu.SemaphoreType.DMA((many,)),
            pltpu.SemaphoreType.DMA((many,)),
        ],
        compiler_params=pltpu.CompilerParams(vmem_limit_bytes=54 * 1024 * 1024),
        cost_estimate=pl.CostEstimate(flops=flops, bytes_accessed=8 << 20, transcendentals=0),
    )(info, *operands)


def gather_kernel(info, *refs):
    groups = info.shape[0] // 3
    bricks, (out, held, zero, in_sems, out_sems) = refs[:groups], refs[groups:]
    me = lax.axis_index("gy")

    def load(k):
        return pltpu.make_async_copy(bricks[k], held.at[k], in_sems.at[k])

    def store(k, source):
        return pltpu.make_async_copy(source, out.at[me ^ k], out_sems.at[k])

    full = [info[2 * groups + k] > 0 for k in range(groups)]
    for k in range(groups):

        @pl.when(full[k])
        def _():
            load(k).start()

    zero[...] = jnp.zeros_like(zero)
    for k in range(groups):

        @pl.when(jnp.logical_not(full[k]))
        def _():
            store(k, zero).start()

    for k in range(groups):

        @pl.when(full[k])
        def _():
            load(k).wait()
            store(k, held.at[k]).start()

    for k in range(groups):
        store(k, zero).wait()


def gather(info, bricks):
    groups = len(bricks)
    return pl.pallas_call(
        gather_kernel,
        out_shape=jax.ShapeDtypeStruct((groups, C, VOXELS), jnp.bfloat16),
        in_specs=[pl.BlockSpec(memory_space=pltpu.SMEM)] + [pl.BlockSpec(memory_space=pl.ANY)] * groups,
        out_specs=pl.BlockSpec(memory_space=pl.ANY),
        scratch_shapes=[
            pltpu.VMEM((groups, C, VOXELS), jnp.bfloat16),
            pltpu.VMEM((C, VOXELS), jnp.bfloat16),
            pltpu.SemaphoreType.DMA((groups,)),
            pltpu.SemaphoreType.DMA((groups,)),
        ],
        compiler_params=pltpu.CompilerParams(vmem_limit_bytes=24 * 1024 * 1024),
        cost_estimate=pl.CostEstimate(flops=0, bytes_accessed=8 << 20, transcendentals=0),
    )(info, *bricks)


def shift(value, axis, up):
    count = lax.axis_size(axis)
    if up:
        return lax.ppermute(value, axis, [(i, i + 1) for i in range(count - 1)])
    return lax.ppermute(value, axis, [(i + 1, i) for i in range(count - 1)])


def per_device(features, voxel_mask, brick_mask, owner, weights, bias):
    extent_x, extent_y, extent_z, channels_in = features.shape
    bricks_x, bricks_y, bricks_z = extent_x // EDGE, extent_y // EDGE, extent_z // EDGE
    count = bricks_x * bricks_y * bricks_z
    groups = lax.axis_size("gy")
    owner = owner.reshape(count)

    x_first, x_last, y_first, y_last, bricks, sends = faces(brick_mask, owner, voxel_mask, features, groups)
    y_low = shift(y_last, "gy", True)
    y_high = shift(y_first, "gy", False)
    x_low = shift(x_last, "gx", True)
    x_high = shift(x_first, "gx", False)
    e_low = shift(jnp.concatenate([x_low[:, -1], x_high[:, -1]]), "gy", True)
    e_high = shift(jnp.concatenate([x_low[:, 0], x_high[:, 0]]), "gy", False)

    def partner(value, k):
        return lax.ppermute(value, "gy", [(i, i ^ k) for i in range(groups)])

    receives = lax.all_to_all(sends, "gy", split_axis=0, concat_axis=0, tiled=True)
    main, masks, wide = prepare(bricks, voxel_mask, features, weights)
    info, packed = plan(bricks, sends, receives)
    wide_bias = jnp.concatenate([bias, bias])[None, :]
    operands = (main, x_low, x_high, y_low, y_high, e_low, e_high, wide, masks, wide_bias)
    packed = packed[0]

    far = list(range(groups - 1, groups // 2 - 1, -1))
    near = list(range(groups // 2 - 1, 0, -1))
    received = [None] * groups
    (brick,) = convolve((far[0],), info, operands)
    for n, k in enumerate(far):
        picks = ((near + [0])[n],) + tuple(far[n + 1 : n + 2])
        upward = [(i, i ^ k) for i in range(groups) if i < i ^ k]
        downward = [(b, a) for a, b in upward]

        def exchange(pairs, value, info, *operands):
            if not pairs:
                *made, got = convolve(picks, info, operands, spare=1)
            else:
                got = lax.ppermute(value, "gy", pairs)
                made = convolve(picks, info, operands)
            return got, *made

        branches = [functools.partial(exchange, pairs) for pairs in ([], upward, downward, upward + downward)]
        case = jnp.bitwise_and(jnp.right_shift(packed, 2 * (k - groups // 2)), 3)
        received[k], local, *ahead = lax.switch(case, branches, brick, info, *operands)
        if picks[0]:
            received[picks[0]] = partner(local, picks[0])
        else:
            received[0] = local
        brick = ahead[0] if ahead else None
    return gather(info, received)[None]


def solution(mesh):
    return jax.shard_map(
        per_device,
        mesh=mesh,
        in_specs=(
            P("gx", "gy", None, None),
            P("gx", "gy", None),
            P("gx", "gy", None),
            P("gx", "gy", None, None),
            P(),
            P(),
        ),
        out_specs=P("gx", "gy", None, None),
        check_vma=False,
    )
```

```python
import functools

import jax
import jax.numpy as jnp
from jax import lax
from jax.experimental import pallas as pl
from jax.experimental.pallas import tpu as pltpu
from jax.sharding import PartitionSpec as P

C = 64
EDGE = 16
AREA = EDGE * EDGE
VOXELS = EDGE**3
PAIRS = EDGE // 2
SPAN = EDGE + 2
LITTLE = pl.CostEstimate(flops=0, bytes_accessed=1024, transcendentals=0)


def activity(voxels, flags, bx):
    layer = lax.broadcasted_iota(jnp.int32, voxels.shape, 2) // EDGE
    chosen = jnp.zeros(voxels.shape, jnp.int32)
    layers = voxels.shape[2] // EDGE
    for bz in range(layers):
        chosen = jnp.where(layer == bz, flags[bx * layers + bz], chosen)
    return (voxels * chosen).astype(jnp.float32)


def spread(values, mask):
    n, y, z, c = values.shape
    wide = jnp.broadcast_to(mask[..., None], values.shape).astype(jnp.bfloat16)
    return (values * wide).reshape(n, y, z // EDGE, EDGE, c)


def plan_kernel(bricks, sends, receives, info, packed):
    groups = sends.shape[0]
    far = groups // 2
    me = lax.axis_index("gy")
    for k in range(groups):
        info[k] = 0
    count = bricks.shape[0] // 2
    for b in range(count):
        info[bricks[count + b] ^ me] = b
    total = jnp.int32(0)
    for k in range(groups):
        peer = me ^ k
        sent = sends[peer, 0]
        info[groups + k] = sent
        info[2 * groups + k] = receives[peer, 0] if k >= far else 1
        if k >= far:
            received = receives[peer, 0]
            total = total | (jnp.where(peer > me, sent + 2 * received, received + 2 * sent) << (2 * (k - far)))
    packed[0] = total


def plan(bricks, sends, receives):
    groups = sends.shape[0]
    return pl.pallas_call(
        plan_kernel,
        out_shape=[jax.ShapeDtypeStruct((n,), jnp.int32) for n in (3 * groups, 1)],
        in_specs=[pl.BlockSpec(memory_space=pltpu.SMEM)] * 3,
        out_specs=[pl.BlockSpec(memory_space=pltpu.SMEM)] * 2,
        cost_estimate=LITTLE,
    )(bricks, sends, receives)


def face_kernel(flags, owner, voxels, features, x_first, x_last, y_first, y_last, bricks, v_raw, x_raw, y_raw, sems):
    rows = features.shape[0]
    sides = (0, rows - 1)
    columns = (0, features.shape[1] - 1)
    copies = [pltpu.make_async_copy(voxels, v_raw, sems.at[4])]
    copies += [pltpu.make_async_copy(features.at[:, pl.ds(y, 1)], y_raw.at[n], sems.at[n]) for n, y in enumerate(columns)]
    copies += [pltpu.make_async_copy(features.at[pl.ds(x, 1)], x_raw.at[n], sems.at[2 + n]) for n, x in enumerate(sides)]
    for copy in copies:
        copy.start()
    count = owner.shape[0]
    layers = flags.shape[2]
    for b in range(count):
        bricks[b] = flags[b // layers, 0, b % layers]
        bricks[count + b] = owner[b]
    for copy in copies:
        copy.wait()
    for n, out in enumerate((y_first, y_last)):
        for bx in range(rows // EDGE):
            span = slice(bx * EDGE, (bx + 1) * EDGE)
            y = columns[n]
            out[span] = spread(y_raw[n, span], activity(v_raw[span, y : y + 1], bricks, bx))
    for n, out in enumerate((x_first, x_last)):
        x = sides[n]
        out[...] = spread(x_raw[n], activity(v_raw[x : x + 1], bricks, x // EDGE))


def faces(brick_mask, owner, voxel_mask, features):
    ex, ey, ez, cin = features.shape
    layers = ez // EDGE
    shapes = [(1, ey, layers, EDGE, cin)] * 2 + [(ex, 1, layers, EDGE, cin)] * 2
    return pl.pallas_call(
        face_kernel,
        out_shape=[jax.ShapeDtypeStruct(shape, features.dtype) for shape in shapes] + [jax.ShapeDtypeStruct((2 * owner.shape[0],), jnp.int32)],
        in_specs=[pl.BlockSpec(memory_space=pltpu.SMEM)] * 2 + [pl.BlockSpec(memory_space=pltpu.HBM)] * 2,
        out_specs=[pl.BlockSpec(memory_space=pltpu.VMEM)] * 4 + [pl.BlockSpec(memory_space=pltpu.SMEM)],
        scratch_shapes=[
            pltpu.VMEM(voxel_mask.shape, voxel_mask.dtype),
            pltpu.VMEM((2, 1, ey, ez, cin), features.dtype),
            pltpu.VMEM((2, ex, 1, ez, cin), features.dtype),
            pltpu.SemaphoreType.DMA((5,)),
        ],
        compiler_params=pltpu.CompilerParams(vmem_limit_bytes=24 * 1024 * 1024),
        cost_estimate=LITTLE,
    )(brick_mask, owner, *(pltpu.with_memory_space_constraint(a, pltpu.HBM) for a in (voxel_mask, features)))


SLAB = 8


def prepare_kernel(flags, voxels, features, weights, main, masks, wide, sends):
    step = pl.program_id(0)
    n, y, z = voxels.shape
    lanes = masks.shape[1]
    source = lax.broadcasted_iota(jnp.int32, (z, lanes), 0)
    lane = lax.broadcasted_iota(jnp.int32, (z, lanes), 1)
    pick = jnp.logical_and(source // EDGE == lane // AREA, source % EDGE == lane % EDGE)
    mask = activity(voxels[...], flags, step // (EDGE // SLAB))
    every = jnp.dot(
        mask.reshape(n * y, z).astype(jnp.bfloat16),
        jnp.where(pick, 1.0, 0.0).astype(jnp.bfloat16),
        preferred_element_type=jnp.float32,
    ).reshape(n, y, lanes)
    row = lax.broadcasted_iota(jnp.int32, (n, y, lanes), 1)
    column = lax.broadcasted_iota(jnp.int32, (n, y, lanes), 2) % AREA // EDGE
    masks[...] = jnp.sum(jnp.where(row == column, every, 0.0), axis=1)
    turned = jnp.swapaxes(mask, 1, 2).reshape(n * z, y).astype(jnp.bfloat16)
    cin = features.shape[3]
    same = lax.broadcasted_iota(jnp.int32, (y, y * cin), 0) == lax.broadcasted_iota(jnp.int32, (y, y * cin), 1) // cin
    wider = jnp.dot(turned, jnp.where(same, 1.0, 0.0).astype(jnp.bfloat16), preferred_element_type=jnp.float32)
    wider = wider.astype(jnp.bfloat16).reshape(n, z, y * cin)
    for c in range(y):
        part = features[:, c] * wider[:, :, c * cin : (c + 1) * cin]
        main[:, c] = part.reshape(n, z // EDGE, EDGE, cin)

    @pl.when(step == 0)
    def _():
        count = flags.shape[0] // 2
        for o in range(sends.shape[0]):
            sends[o, 0] = 0
        for b in range(count):
            sends[flags[count + b], 0] = flags[b]
        cin = weights.shape[-1]
        for b in range(3):
            for j in range(2):
                for c in range(3):
                    parts = []
                    for t in range(4):
                        a = 2 + j - t
                        tap = weights[(a * 3 + b) * 3 + c] if 0 <= a <= 2 else jnp.zeros(weights.shape[1:], weights.dtype)
                        parts.append(tap.astype(jnp.float32))
                    block = jnp.concatenate(parts, axis=0).T
                    start = (6 * b + 3 * j + c) * cin
                    wide[start : start + cin, :] = block.astype(wide.dtype)


def prepare(bricks, voxel_mask, features, weights, groups):
    ex, ey, ez, cin = features.shape
    cout = weights.shape[4]
    taps = weights.transpose(0, 1, 2, 4, 3).reshape(27, cout, cin)
    return pl.pallas_call(
        prepare_kernel,
        out_shape=[
            jax.ShapeDtypeStruct((ex, ey, ez // EDGE, EDGE, cin), features.dtype),
            jax.ShapeDtypeStruct((ex, ez // EDGE * AREA), jnp.float32),
            jax.ShapeDtypeStruct((18 * cin, 4 * cout), weights.dtype),
            jax.ShapeDtypeStruct((groups, 128), jnp.int32),
        ],
        grid=(ex // SLAB,),
        in_specs=[
            pl.BlockSpec(memory_space=pltpu.SMEM),
            pl.BlockSpec((SLAB, ey, ez), lambda i: (i, 0, 0)),
            pl.BlockSpec((SLAB, ey, ez, cin), lambda i: (i, 0, 0, 0)),
            pl.BlockSpec((27, cout, cin), lambda i: (0, 0, 0)),
        ],
        out_specs=[
            pl.BlockSpec((SLAB, ey, ez // EDGE, EDGE, cin), lambda i: (i, 0, 0, 0, 0)),
            pl.BlockSpec((SLAB, ez // EDGE * AREA), lambda i: (i, 0)),
            pl.BlockSpec((18 * cin, 4 * cout), lambda i: (0, 0)),
            pl.BlockSpec(memory_space=pltpu.SMEM),
        ],
        compiler_params=pltpu.CompilerParams(vmem_limit_bytes=32 * 1024 * 1024),
        cost_estimate=pl.CostEstimate(flops=0, bytes_accessed=40 << 20, transcendentals=0),
    )(bricks, voxel_mask, pltpu.with_memory_space_constraint(features, pltpu.HBM), taps)


def conv_kernel(picks, spare, info, main, x_low, x_high, y_low, y_high, e_low, e_high, weights, masks, bias, *refs):
    many = len(picks)
    outs, refs = refs[:many], refs[many + spare :]
    raw, wide, live, stage_a, stage_b, high, result, raw_sems, wide_sem, live_sems, out_sems = refs
    groups = info.shape[0] // 3
    layers = main.shape[2]
    cin = main.shape[-1]
    rows = EDGE + 1
    pieces = ((0, 6), (6, 6), (12, 5))

    def pick(i):
        return functools.reduce(lambda old, n: jnp.where(i == n, picks[n], old), range(1, many), picks[0])

    def place(brick):
        bz = brick % layers
        return brick // layers, bz, jnp.clip(bz - 1, 0, layers - 3)

    def start(i, brick):
        bx, _, first = place(brick)
        tiles = pl.ds(first, 3)
        end = bx * rows
        for side in range(2):

            @pl.when(bx == side)
            def _():
                face = (x_low, x_high)[side].at[0, :, tiles]
                pltpu.make_async_copy(face, raw.at[i, end, pl.ds(1, EDGE)], raw_sems.at[i, 3]).start()

        pltpu.make_async_copy(e_low.at[bx, tiles], raw.at[i, end, 0], raw_sems.at[i, 3]).start()
        pltpu.make_async_copy(e_high.at[bx, tiles], raw.at[i, end, rows], raw_sems.at[i, 3]).start()
        for c, (plane, size) in enumerate(pieces):
            source = pl.ds(plane + bx * (EDGE - 1), size)
            planes = pl.ds(plane + 1 - bx, size)
            pltpu.make_async_copy(main.at[source, :, tiles], raw.at[i, planes, pl.ds(1, EDGE)], raw_sems.at[i, c]).start()
            pltpu.make_async_copy(y_low.at[source, 0, tiles], raw.at[i, planes, 0], raw_sems.at[i, c]).start()
            pltpu.make_async_copy(y_high.at[source, 0, tiles], raw.at[i, planes, rows], raw_sems.at[i, c]).start()

    def arrived(i, c):
        whole = raw.at[i, pl.ds(0, pieces[c][1] if c < 3 else 1)]
        pltpu.make_async_copy(whole, whole, raw_sems.at[i, c]).wait()

    def mask_copy(i, brick):
        bx, bz, _ = place(brick)
        rows = pl.ds(pl.multiple_of(bx * EDGE, EDGE), EDGE)
        lanes = pl.ds(pl.multiple_of(bz * AREA, AREA), AREA)
        return pltpu.make_async_copy(masks.at[rows, lanes], live.at[i], live_sems.at[i])

    def store(i):
        return pltpu.make_async_copy(result.at[i], outs[i], out_sems.at[i])

    active = [info[groups + k] > 0 for k in picks]
    some = functools.reduce(jnp.logical_or, active)
    filled = [jnp.logical_or(on, k < groups // 2) for on, k in zip(active, picks)]
    load = pltpu.make_async_copy(weights, wide, wide_sem)

    @pl.when(some)
    def _():
        load.start()

    @pl.loop(0, many)
    def _(i):
        k = pick(i)

        @pl.when(info[groups + k] > 0)
        def _():
            start(i, info[k])
            mask_copy(i, info[k]).start()

    first_active = jnp.where(active[0], 0, 1)

    row = lax.broadcasted_iota(jnp.int32, (SPAN, 8, cin), 1)

    @pl.loop(0, many)
    def _(i):
        k = pick(i)
        brick = info[k]
        _, bz, first = place(brick)
        centre = bz - first
        under = jnp.maximum(centre - 1, 0)
        over = jnp.minimum(centre + 1, 2)
        has_under = (bz > 0).astype(jnp.float32)
        has_over = (bz < layers - 1).astype(jnp.float32)

        def build(stage, pair):
            for n in range(2):
                plane = 2 * pair + n
                same = raw[i, plane, :, centre]
                middle = same.astype(jnp.float32)
                m0, m1 = middle[:, :8], middle[:, 8:]
                below = raw[i, plane, :, under].astype(jnp.float32)[:, 8:] * has_under
                above = raw[i, plane, :, over].astype(jnp.float32)[:, :8] * has_over
                u0 = jnp.where(row == 0, pltpu.roll(below, 1, 1), pltpu.roll(m0, 1, 1))
                u1 = jnp.where(row == 0, pltpu.roll(m0, 1, 1), pltpu.roll(m1, 1, 1))
                d0 = jnp.where(row == 7, pltpu.roll(m1, 7, 1), pltpu.roll(m0, 7, 1))
                d1 = jnp.where(row == 7, pltpu.roll(above, 7, 1), pltpu.roll(m1, 7, 1))
                up = jnp.concatenate([u0, u1], axis=1).astype(jnp.bfloat16)
                down = jnp.concatenate([d0, d1], axis=1).astype(jnp.bfloat16)
                for c, value in enumerate((up, same, down)):
                    stage[:, pl.ds((3 * n + c) * cin, cin)] = value.reshape(SPAN * EDGE, cin)

        def taps(stage, columns):
            windows = [stage[b * EDGE : b * EDGE + AREA, :] for b in range(3)]
            return jnp.dot(jnp.concatenate(windows, axis=1), wide[:, columns], preferred_element_type=jnp.float32)

        def emit(q, low):
            value = jnp.maximum(high[...] + low + bias[...], 0.0).astype(result.dtype).T
            for n in range(2):
                mask = live[i, pl.ds(2 * q + n, 1)].astype(result.dtype)
                lanes = pl.ds(pl.multiple_of((2 * q + n) * AREA, AREA), AREA)
                result[i, :, lanes] = value[n * C : (n + 1) * C] * mask

        def advance(pair, stage):
            total = taps(stage, slice(None))
            emit(jnp.maximum(pair - 1, 0), total[:, : 2 * C])
            high[...] = total[:, 2 * C :]

        @pl.when(info[groups + k] > 0)
        def _():
            high[...] = jnp.zeros_like(high)
            arrived(i, 3)
            arrived(i, 0)
            build(stage_a, 0)
            mask_copy(i, brick).wait()

            @pl.when(i == first_active)
            def _():
                load.wait()

            @pl.loop(0, PAIRS // 2)
            def _(n):
                for c in (1, 2):

                    @pl.when(n == c)
                    def _():
                        arrived(i, c)

                build(stage_b, 2 * n + 1)
                advance(2 * n, stage_a)
                build(stage_a, 2 * n + 2)
                advance(2 * n + 1, stage_b)

            emit(PAIRS - 1, taps(stage_a, slice(0, 2 * C)))

        @pl.when(jnp.logical_and(info[groups + k] == 0, k < groups // 2))
        def _():
            result[i] = jnp.zeros(result.shape[1:], result.dtype)

        for n in range(many):

            @pl.when(jnp.logical_and(i == n, filled[n]))
            def _():
                store(n).start()

    for i in range(many):

        @pl.when(filled[i])
        def _():
            store(i).wait()


def convolve(picks, info, operands, spare=0):
    cin = operands[0].shape[-1]
    wide, masks = operands[7:9]
    many = len(picks)
    flops = 2 * (PAIRS + 1) * AREA * 18 * cin * 4 * C * many
    return pl.pallas_call(
        functools.partial(conv_kernel, picks, spare),
        out_shape=[pltpu.VMEM((C, VOXELS), jnp.bfloat16)] * (many + spare),
        in_specs=[pl.BlockSpec(memory_space=pltpu.SMEM)]
        + [pl.BlockSpec(memory_space=pl.ANY)] * 9
        + [pl.BlockSpec(memory_space=pltpu.VMEM)],
        out_specs=[pl.BlockSpec(memory_space=pl.ANY)] * (many + spare),
        scratch_shapes=[
            pltpu.VMEM((many, SPAN, SPAN, 3, EDGE, cin), jnp.bfloat16),
            pltpu.VMEM(wide.shape, wide.dtype),
            pltpu.VMEM((many, EDGE, AREA), masks.dtype),
            pltpu.VMEM((SPAN * EDGE, 6 * cin), jnp.bfloat16),
            pltpu.VMEM((SPAN * EDGE, 6 * cin), jnp.bfloat16),
            pltpu.VMEM((AREA, 2 * C), jnp.float32),
            pltpu.VMEM((many, C, VOXELS), jnp.bfloat16),
            pltpu.SemaphoreType.DMA((many, 4)),
            pltpu.SemaphoreType.DMA,
            pltpu.SemaphoreType.DMA((many,)),
            pltpu.SemaphoreType.DMA((many,)),
        ],
        compiler_params=pltpu.CompilerParams(vmem_limit_bytes=54 * 1024 * 1024),
        cost_estimate=pl.CostEstimate(flops=flops, bytes_accessed=8 << 20, transcendentals=0),
    )(info, *operands)


def gather_kernel(info, *refs):
    groups = info.shape[0] // 3
    bricks, (out, held, zero, in_sems, out_sems) = refs[:groups], refs[groups:]
    me = lax.axis_index("gy")

    def load(k):
        return pltpu.make_async_copy(bricks[k], held.at[k], in_sems.at[k])

    def store(k, source):
        return pltpu.make_async_copy(source, out.at[me ^ k], out_sems.at[k])

    full = [info[2 * groups + k] > 0 for k in range(groups)]
    for k in range(groups):

        @pl.when(full[k])
        def _():
            load(k).start()

    zero[...] = jnp.zeros_like(zero)
    for k in range(groups):

        @pl.when(jnp.logical_not(full[k]))
        def _():
            store(k, zero).start()

    for k in range(groups):

        @pl.when(full[k])
        def _():
            load(k).wait()
            store(k, held.at[k]).start()

    for k in range(groups):
        store(k, zero).wait()


def gather(info, bricks):
    groups = len(bricks)
    return pl.pallas_call(
        gather_kernel,
        out_shape=jax.ShapeDtypeStruct((groups, C, VOXELS), jnp.bfloat16),
        in_specs=[pl.BlockSpec(memory_space=pltpu.SMEM)] + [pl.BlockSpec(memory_space=pl.ANY)] * groups,
        out_specs=pl.BlockSpec(memory_space=pl.ANY),
        scratch_shapes=[
            pltpu.VMEM((groups, C, VOXELS), jnp.bfloat16),
            pltpu.VMEM((C, VOXELS), jnp.bfloat16),
            pltpu.SemaphoreType.DMA((groups,)),
            pltpu.SemaphoreType.DMA((groups,)),
        ],
        compiler_params=pltpu.CompilerParams(vmem_limit_bytes=24 * 1024 * 1024),
        cost_estimate=pl.CostEstimate(flops=0, bytes_accessed=8 << 20, transcendentals=0),
    )(info, *bricks)


def shift(value, axis, up):
    count = lax.axis_size(axis)
    if up:
        return lax.ppermute(value, axis, [(i, i + 1) for i in range(count - 1)])
    return lax.ppermute(value, axis, [(i + 1, i) for i in range(count - 1)])


def per_device(features, voxel_mask, brick_mask, owner, weights, bias):
    extent_x, extent_y, extent_z, channels_in = features.shape
    bricks_x, bricks_y, bricks_z = extent_x // EDGE, extent_y // EDGE, extent_z // EDGE
    count = bricks_x * bricks_y * bricks_z
    groups = lax.axis_size("gy")
    owner = owner.reshape(count)

    x_first, x_last, y_first, y_last, bricks = faces(brick_mask, owner, voxel_mask, features)
    y_low = shift(y_last, "gy", True)
    y_high = shift(y_first, "gy", False)
    x_low = shift(x_last, "gx", True)
    x_high = shift(x_first, "gx", False)
    e_low = shift(jnp.concatenate([x_low[:, -1], x_high[:, -1]]), "gy", True)
    e_high = shift(jnp.concatenate([x_low[:, 0], x_high[:, 0]]), "gy", False)

    def partner(value, k):
        return lax.ppermute(value, "gy", [(i, i ^ k) for i in range(groups)])

    main, masks, wide, sends = prepare(bricks, voxel_mask, features, weights, groups)
    receives = lax.all_to_all(sends, "gy", split_axis=0, concat_axis=0, tiled=True)
    info, packed = plan(bricks, sends, receives)
    wide_bias = jnp.concatenate([bias, bias])[None, :]
    operands = (main, x_low, x_high, y_low, y_high, e_low, e_high, wide, masks, wide_bias)
    packed = packed[0]

    far = list(range(groups - 1, groups // 2 - 1, -1))
    near = list(range(groups // 2 - 1, 0, -1))
    received = [None] * groups
    (brick,) = convolve((far[0],), info, operands)
    for n, k in enumerate(far):
        picks = ((near + [0])[n],) + tuple(far[n + 1 : n + 2])
        upward = [(i, i ^ k) for i in range(groups) if i < i ^ k]
        downward = [(b, a) for a, b in upward]

        def exchange(pairs, value, info, *operands):
            if not pairs:
                *made, got = convolve(picks, info, operands, spare=1)
            else:
                got = lax.ppermute(value, "gy", pairs)
                made = convolve(picks, info, operands)
            return got, *made

        branches = [functools.partial(exchange, pairs) for pairs in ([], upward, downward, upward + downward)]
        case = jnp.bitwise_and(jnp.right_shift(packed, 2 * (k - groups // 2)), 3)
        received[k], local, *ahead = lax.switch(case, branches, brick, info, *operands)
        if picks[0]:
            received[picks[0]] = partner(local, picks[0])
        else:
            received[0] = local
        brick = ahead[0] if ahead else None
    return gather(info, received)[None]


def solution(mesh):
    return jax.shard_map(
        per_device,
        mesh=mesh,
        in_specs=(
            P("gx", "gy", None, None),
            P("gx", "gy", None),
            P("gx", "gy", None),
            P("gx", "gy", None, None),
            P(),
            P(),
        ),
        out_specs=P("gx", "gy", None, None),
        check_vma=False,
    )
```

```python
import functools

import jax
import jax.numpy as jnp
from jax import lax
from jax.experimental import pallas as pl
from jax.experimental.pallas import tpu as pltpu
from jax.sharding import PartitionSpec as P

C = 64
EDGE = 16
AREA = EDGE * EDGE
VOXELS = EDGE**3
PAIRS = EDGE // 2
SPAN = EDGE + 2
LITTLE = pl.CostEstimate(flops=0, bytes_accessed=1024, transcendentals=0)


def activity(voxels, flags, bx):
    layer = lax.broadcasted_iota(jnp.int32, voxels.shape, 2) // EDGE
    chosen = jnp.zeros(voxels.shape, jnp.int32)
    layers = voxels.shape[2] // EDGE
    for bz in range(layers):
        chosen = jnp.where(layer == bz, flags[bx * layers + bz], chosen)
    return (voxels * chosen).astype(jnp.float32)


def spread(values, mask):
    n, y, z, c = values.shape
    wide = jnp.broadcast_to(mask[..., None], values.shape).astype(jnp.bfloat16)
    return (values * wide).reshape(n, y, z // EDGE, EDGE, c)


def plan_kernel(bricks, sends, receives, info, packed):
    groups = sends.shape[0]
    far = groups // 2
    me = lax.axis_index("gy")
    for k in range(groups):
        info[k] = 0
    count = bricks.shape[0] // 2
    for b in range(count):
        info[bricks[count + b] ^ me] = b
    total = jnp.int32(0)
    for k in range(groups):
        peer = me ^ k
        sent = sends[peer, 0]
        info[groups + k] = sent
        info[2 * groups + k] = receives[peer, 0] if k >= far else 1
        if k >= far:
            received = receives[peer, 0]
            total = total | (jnp.where(peer > me, sent + 2 * received, received + 2 * sent) << (2 * (k - far)))
    packed[0] = total


def plan(bricks, sends, receives):
    groups = sends.shape[0]
    return pl.pallas_call(
        plan_kernel,
        out_shape=[jax.ShapeDtypeStruct((n,), jnp.int32) for n in (3 * groups, 1)],
        in_specs=[pl.BlockSpec(memory_space=pltpu.SMEM)] * 3,
        out_specs=[pl.BlockSpec(memory_space=pltpu.SMEM)] * 2,
        cost_estimate=LITTLE,
    )(bricks, sends, receives)


def face_kernel(flags, owner, voxels, features, x_first, x_last, y_first, y_last, bricks, v_raw, x_raw, y_raw, sems):
    rows = features.shape[0]
    sides = (0, rows - 1)
    columns = (0, features.shape[1] - 1)
    copies = [pltpu.make_async_copy(voxels, v_raw, sems.at[4])]
    copies += [pltpu.make_async_copy(features.at[:, pl.ds(y, 1)], y_raw.at[n], sems.at[n]) for n, y in enumerate(columns)]
    copies += [pltpu.make_async_copy(features.at[pl.ds(x, 1)], x_raw.at[n], sems.at[2 + n]) for n, x in enumerate(sides)]
    for copy in copies:
        copy.start()
    count = owner.shape[0]
    layers = flags.shape[2]
    for b in range(count):
        bricks[b] = flags[b // layers, 0, b % layers]
        bricks[count + b] = owner[b]
    for copy in copies:
        copy.wait()
    for n, out in enumerate((y_first, y_last)):
        for bx in range(rows // EDGE):
            span = slice(bx * EDGE, (bx + 1) * EDGE)
            y = columns[n]
            out[span] = spread(y_raw[n, span], activity(v_raw[span, y : y + 1], bricks, bx))
    for n, out in enumerate((x_first, x_last)):
        x = sides[n]
        out[...] = spread(x_raw[n], activity(v_raw[x : x + 1], bricks, x // EDGE))


def faces(brick_mask, owner, voxel_mask, features):
    ex, ey, ez, cin = features.shape
    layers = ez // EDGE
    shapes = [(1, ey, layers, EDGE, cin)] * 2 + [(ex, 1, layers, EDGE, cin)] * 2
    return pl.pallas_call(
        face_kernel,
        out_shape=[jax.ShapeDtypeStruct(shape, features.dtype) for shape in shapes] + [jax.ShapeDtypeStruct((2 * owner.shape[0],), jnp.int32)],
        in_specs=[pl.BlockSpec(memory_space=pltpu.SMEM)] * 2 + [pl.BlockSpec(memory_space=pltpu.HBM)] * 2,
        out_specs=[pl.BlockSpec(memory_space=pltpu.VMEM)] * 4 + [pl.BlockSpec(memory_space=pltpu.SMEM)],
        scratch_shapes=[
            pltpu.VMEM(voxel_mask.shape, voxel_mask.dtype),
            pltpu.VMEM((2, 1, ey, ez, cin), features.dtype),
            pltpu.VMEM((2, ex, 1, ez, cin), features.dtype),
            pltpu.SemaphoreType.DMA((5,)),
        ],
        compiler_params=pltpu.CompilerParams(vmem_limit_bytes=24 * 1024 * 1024),
        cost_estimate=LITTLE,
    )(*(pltpu.with_memory_space_constraint(a, pltpu.HBM) for a in (brick_mask, owner, voxel_mask, features)))


SLAB = 8


def prepare_kernel(flags, voxels, features, weights, main, masks, wide, sends):
    step = pl.program_id(0)
    n, y, z = voxels.shape
    lanes = masks.shape[1]
    source = lax.broadcasted_iota(jnp.int32, (z, lanes), 0)
    lane = lax.broadcasted_iota(jnp.int32, (z, lanes), 1)
    pick = jnp.logical_and(source // EDGE == lane // AREA, source % EDGE == lane % EDGE)
    mask = activity(voxels[...], flags, step // (EDGE // SLAB))
    every = jnp.dot(
        mask.reshape(n * y, z).astype(jnp.bfloat16),
        jnp.where(pick, 1.0, 0.0).astype(jnp.bfloat16),
        preferred_element_type=jnp.float32,
    ).reshape(n, y, lanes)
    row = lax.broadcasted_iota(jnp.int32, (n, y, lanes), 1)
    column = lax.broadcasted_iota(jnp.int32, (n, y, lanes), 2) % AREA // EDGE
    masks[...] = jnp.sum(jnp.where(row == column, every, 0.0), axis=1)
    turned = jnp.swapaxes(mask, 1, 2).reshape(n * z, y).astype(jnp.bfloat16)
    cin = features.shape[3]
    same = lax.broadcasted_iota(jnp.int32, (y, y * cin), 0) == lax.broadcasted_iota(jnp.int32, (y, y * cin), 1) // cin
    wider = jnp.dot(turned, jnp.where(same, 1.0, 0.0).astype(jnp.bfloat16), preferred_element_type=jnp.float32)
    wider = wider.astype(jnp.bfloat16).reshape(n, z, y * cin)
    for c in range(y):
        part = features[:, c] * wider[:, :, c * cin : (c + 1) * cin]
        main[:, c] = part.reshape(n, z // EDGE, EDGE, cin)

    @pl.when(step == 0)
    def _():
        count = flags.shape[0] // 2
        for o in range(sends.shape[0]):
            sends[o, 0] = 0
        for b in range(count):
            sends[flags[count + b], 0] = flags[b]
        cin = weights.shape[-1]
        for b in range(3):
            for j in range(2):
                for c in range(3):
                    parts = []
                    for t in range(4):
                        a = 2 + j - t
                        tap = weights[(a * 3 + b) * 3 + c] if 0 <= a <= 2 else jnp.zeros(weights.shape[1:], weights.dtype)
                        parts.append(tap.astype(jnp.float32))
                    block = jnp.concatenate(parts, axis=0).T
                    start = (6 * b + 3 * j + c) * cin
                    wide[start : start + cin, :] = block.astype(wide.dtype)


def prepare(bricks, voxel_mask, features, weights, groups):
    ex, ey, ez, cin = features.shape
    cout = weights.shape[4]
    taps = weights.transpose(0, 1, 2, 4, 3).reshape(27, cout, cin)
    return pl.pallas_call(
        prepare_kernel,
        out_shape=[
            jax.ShapeDtypeStruct((ex, ey, ez // EDGE, EDGE, cin), features.dtype),
            jax.ShapeDtypeStruct((ex, ez // EDGE * AREA), jnp.float32),
            jax.ShapeDtypeStruct((18 * cin, 4 * cout), weights.dtype),
            jax.ShapeDtypeStruct((groups, 128), jnp.int32),
        ],
        grid=(ex // SLAB,),
        in_specs=[
            pl.BlockSpec(memory_space=pltpu.SMEM),
            pl.BlockSpec((SLAB, ey, ez), lambda i: (i, 0, 0)),
            pl.BlockSpec((SLAB, ey, ez, cin), lambda i: (i, 0, 0, 0)),
            pl.BlockSpec((27, cout, cin), lambda i: (0, 0, 0)),
        ],
        out_specs=[
            pl.BlockSpec((SLAB, ey, ez // EDGE, EDGE, cin), lambda i: (i, 0, 0, 0, 0)),
            pl.BlockSpec((SLAB, ez // EDGE * AREA), lambda i: (i, 0)),
            pl.BlockSpec((18 * cin, 4 * cout), lambda i: (0, 0)),
            pl.BlockSpec(memory_space=pltpu.SMEM),
        ],
        compiler_params=pltpu.CompilerParams(vmem_limit_bytes=32 * 1024 * 1024),
        cost_estimate=pl.CostEstimate(flops=0, bytes_accessed=40 << 20, transcendentals=0),
    )(bricks, voxel_mask, pltpu.with_memory_space_constraint(features, pltpu.HBM), taps)


def conv_kernel(picks, spare, info, main, x_low, x_high, y_low, y_high, e_low, e_high, weights, masks, bias, *refs):
    many = len(picks)
    outs, refs = refs[:many], refs[many + spare :]
    raw, wide, live, stage_a, stage_b, high, result, raw_sems, wide_sem, live_sems, out_sems = refs
    groups = info.shape[0] // 3
    layers = main.shape[2]
    cin = main.shape[-1]
    rows = EDGE + 1
    pieces = ((0, 6), (6, 6), (12, 5))

    def pick(i):
        return functools.reduce(lambda old, n: jnp.where(i == n, picks[n], old), range(1, many), picks[0])

    def place(brick):
        bz = brick % layers
        return brick // layers, bz, jnp.clip(bz - 1, 0, layers - 3)

    def start(i, brick):
        bx, _, first = place(brick)
        tiles = pl.ds(first, 3)
        end = bx * rows
        for side in range(2):

            @pl.when(bx == side)
            def _():
                face = (x_low, x_high)[side].at[0, :, tiles]
                pltpu.make_async_copy(face, raw.at[i, end, pl.ds(1, EDGE)], raw_sems.at[i, 3]).start()

        pltpu.make_async_copy(e_low.at[bx, tiles], raw.at[i, end, 0], raw_sems.at[i, 3]).start()
        pltpu.make_async_copy(e_high.at[bx, tiles], raw.at[i, end, rows], raw_sems.at[i, 3]).start()
        for c, (plane, size) in enumerate(pieces):
            source = pl.ds(plane + bx * (EDGE - 1), size)
            planes = pl.ds(plane + 1 - bx, size)
            pltpu.make_async_copy(main.at[source, :, tiles], raw.at[i, planes, pl.ds(1, EDGE)], raw_sems.at[i, c]).start()
            pltpu.make_async_copy(y_low.at[source, 0, tiles], raw.at[i, planes, 0], raw_sems.at[i, c]).start()
            pltpu.make_async_copy(y_high.at[source, 0, tiles], raw.at[i, planes, rows], raw_sems.at[i, c]).start()

    def arrived(i, c):
        whole = raw.at[i, pl.ds(0, pieces[c][1] if c < 3 else 1)]
        pltpu.make_async_copy(whole, whole, raw_sems.at[i, c]).wait()

    def mask_copy(i, brick):
        bx, bz, _ = place(brick)
        rows = pl.ds(pl.multiple_of(bx * EDGE, EDGE), EDGE)
        lanes = pl.ds(pl.multiple_of(bz * AREA, AREA), AREA)
        return pltpu.make_async_copy(masks.at[rows, lanes], live.at[i], live_sems.at[i])

    def store(i):
        return pltpu.make_async_copy(result.at[i], outs[i], out_sems.at[i])

    active = [info[groups + k] > 0 for k in picks]
    some = functools.reduce(jnp.logical_or, active)
    filled = [jnp.logical_or(on, k < groups // 2) for on, k in zip(active, picks)]
    load = pltpu.make_async_copy(weights, wide, wide_sem)

    @pl.when(some)
    def _():
        load.start()

    @pl.loop(0, many)
    def _(i):
        k = pick(i)

        @pl.when(info[groups + k] > 0)
        def _():
            start(i, info[k])
            mask_copy(i, info[k]).start()

    first_active = jnp.where(active[0], 0, 1)

    row = lax.broadcasted_iota(jnp.int32, (SPAN, 8, cin), 1)

    @pl.loop(0, many)
    def _(i):
        k = pick(i)
        brick = info[k]
        _, bz, first = place(brick)
        centre = bz - first
        under = jnp.maximum(centre - 1, 0)
        over = jnp.minimum(centre + 1, 2)
        has_under = (bz > 0).astype(jnp.float32)
        has_over = (bz < layers - 1).astype(jnp.float32)

        def build(stage, pair):
            for n in range(2):
                plane = 2 * pair + n
                same = raw[i, plane, :, centre]
                middle = same.astype(jnp.float32)
                m0, m1 = middle[:, :8], middle[:, 8:]
                below = raw[i, plane, :, under].astype(jnp.float32)[:, 8:] * has_under
                above = raw[i, plane, :, over].astype(jnp.float32)[:, :8] * has_over
                u0 = jnp.where(row == 0, pltpu.roll(below, 1, 1), pltpu.roll(m0, 1, 1))
                u1 = jnp.where(row == 0, pltpu.roll(m0, 1, 1), pltpu.roll(m1, 1, 1))
                d0 = jnp.where(row == 7, pltpu.roll(m1, 7, 1), pltpu.roll(m0, 7, 1))
                d1 = jnp.where(row == 7, pltpu.roll(above, 7, 1), pltpu.roll(m1, 7, 1))
                up = jnp.concatenate([u0, u1], axis=1).astype(jnp.bfloat16)
                down = jnp.concatenate([d0, d1], axis=1).astype(jnp.bfloat16)
                for c, value in enumerate((up, same, down)):
                    stage[:, pl.ds((3 * n + c) * cin, cin)] = value.reshape(SPAN * EDGE, cin)

        def taps(stage, columns):
            windows = [stage[b * EDGE : b * EDGE + AREA, :] for b in range(3)]
            return jnp.dot(jnp.concatenate(windows, axis=1), wide[:, columns], preferred_element_type=jnp.float32)

        def emit(q, low):
            value = jnp.maximum(high[...] + low + bias[...], 0.0).astype(result.dtype).T
            for n in range(2):
                mask = live[i, pl.ds(2 * q + n, 1)].astype(result.dtype)
                lanes = pl.ds(pl.multiple_of((2 * q + n) * AREA, AREA), AREA)
                result[i, :, lanes] = value[n * C : (n + 1) * C] * mask

        def advance(pair, stage):
            total = taps(stage, slice(None))
            emit(jnp.maximum(pair - 1, 0), total[:, : 2 * C])
            high[...] = total[:, 2 * C :]

        @pl.when(info[groups + k] > 0)
        def _():
            high[...] = jnp.zeros_like(high)
            arrived(i, 3)
            arrived(i, 0)
            build(stage_a, 0)
            mask_copy(i, brick).wait()

            @pl.when(i == first_active)
            def _():
                load.wait()

            @pl.loop(0, PAIRS // 2)
            def _(n):
                for c in (1, 2):

                    @pl.when(n == c)
                    def _():
                        arrived(i, c)

                build(stage_b, 2 * n + 1)
                advance(2 * n, stage_a)
                build(stage_a, 2 * n + 2)
                advance(2 * n + 1, stage_b)

            emit(PAIRS - 1, taps(stage_a, slice(0, 2 * C)))

        @pl.when(jnp.logical_and(info[groups + k] == 0, k < groups // 2))
        def _():
            result[i] = jnp.zeros(result.shape[1:], result.dtype)

        for n in range(many):

            @pl.when(jnp.logical_and(i == n, filled[n]))
            def _():
                store(n).start()

    for i in range(many):

        @pl.when(filled[i])
        def _():
            store(i).wait()


def convolve(picks, info, operands, spare=0):
    cin = operands[0].shape[-1]
    wide, masks = operands[7:9]
    many = len(picks)
    flops = 2 * (PAIRS + 1) * AREA * 18 * cin * 4 * C * many
    return pl.pallas_call(
        functools.partial(conv_kernel, picks, spare),
        out_shape=[pltpu.VMEM((C, VOXELS), jnp.bfloat16)] * (many + spare),
        in_specs=[pl.BlockSpec(memory_space=pltpu.SMEM)]
        + [pl.BlockSpec(memory_space=pl.ANY)] * 9
        + [pl.BlockSpec(memory_space=pltpu.VMEM)],
        out_specs=[pl.BlockSpec(memory_space=pl.ANY)] * (many + spare),
        scratch_shapes=[
            pltpu.VMEM((many, SPAN, SPAN, 3, EDGE, cin), jnp.bfloat16),
            pltpu.VMEM(wide.shape, wide.dtype),
            pltpu.VMEM((many, EDGE, AREA), masks.dtype),
            pltpu.VMEM((SPAN * EDGE, 6 * cin), jnp.bfloat16),
            pltpu.VMEM((SPAN * EDGE, 6 * cin), jnp.bfloat16),
            pltpu.VMEM((AREA, 2 * C), jnp.float32),
            pltpu.VMEM((many, C, VOXELS), jnp.bfloat16),
            pltpu.SemaphoreType.DMA((many, 4)),
            pltpu.SemaphoreType.DMA,
            pltpu.SemaphoreType.DMA((many,)),
            pltpu.SemaphoreType.DMA((many,)),
        ],
        compiler_params=pltpu.CompilerParams(vmem_limit_bytes=54 * 1024 * 1024),
        cost_estimate=pl.CostEstimate(flops=flops, bytes_accessed=8 << 20, transcendentals=0),
    )(info, *operands)


def gather_kernel(info, *refs):
    groups = info.shape[0] // 3
    bricks, (out, held, zero, in_sems, out_sems) = refs[:groups], refs[groups:]
    me = lax.axis_index("gy")

    def load(k):
        return pltpu.make_async_copy(bricks[k], held.at[k - groups // 2], in_sems.at[k])

    def store(k, source):
        return pltpu.make_async_copy(source, out.at[me ^ k], out_sems.at[k])

    near = groups // 2
    full = [info[2 * groups + k] > 0 for k in range(groups)]
    for k in range(near, groups):

        @pl.when(full[k])
        def _():
            load(k).start()

    for k in range(near):
        store(k, bricks[k]).start()
    zero[...] = jnp.zeros_like(zero)
    for k in range(near, groups):

        @pl.when(jnp.logical_not(full[k]))
        def _():
            store(k, zero).start()

    for k in range(near, groups):

        @pl.when(full[k])
        def _():
            load(k).wait()
            store(k, held.at[k - near]).start()

    for k in range(groups):
        store(k, zero).wait()


def gather(info, bricks):
    groups = len(bricks)
    return pl.pallas_call(
        gather_kernel,
        out_shape=jax.ShapeDtypeStruct((groups, C, VOXELS), jnp.bfloat16),
        in_specs=[pl.BlockSpec(memory_space=pltpu.SMEM)] + [pl.BlockSpec(memory_space=pl.ANY)] * groups,
        out_specs=pl.BlockSpec(memory_space=pl.ANY),
        scratch_shapes=[
            pltpu.VMEM((groups // 2, C, VOXELS), jnp.bfloat16),
            pltpu.VMEM((C, VOXELS), jnp.bfloat16),
            pltpu.SemaphoreType.DMA((groups,)),
            pltpu.SemaphoreType.DMA((groups,)),
        ],
        compiler_params=pltpu.CompilerParams(vmem_limit_bytes=24 * 1024 * 1024),
        cost_estimate=pl.CostEstimate(flops=0, bytes_accessed=8 << 20, transcendentals=0),
    )(info, *(pltpu.with_memory_space_constraint(b, pltpu.VMEM) for b in bricks[: groups // 2]), *bricks[groups // 2 :])


def shift(value, axis, up):
    count = lax.axis_size(axis)
    if up:
        return lax.ppermute(value, axis, [(i, i + 1) for i in range(count - 1)])
    return lax.ppermute(value, axis, [(i + 1, i) for i in range(count - 1)])


def per_device(features, voxel_mask, brick_mask, owner, weights, bias):
    extent_x, extent_y, extent_z, channels_in = features.shape
    bricks_x, bricks_y, bricks_z = extent_x // EDGE, extent_y // EDGE, extent_z // EDGE
    count = bricks_x * bricks_y * bricks_z
    groups = lax.axis_size("gy")
    owner = owner.reshape(count)

    x_first, x_last, y_first, y_last, bricks = faces(brick_mask, owner, voxel_mask, features)
    y_low = shift(y_last, "gy", True)
    y_high = shift(y_first, "gy", False)
    x_low = shift(x_last, "gx", True)
    x_high = shift(x_first, "gx", False)
    e_low = shift(jnp.concatenate([x_low[:, -1], x_high[:, -1]]), "gy", True)
    e_high = shift(jnp.concatenate([x_low[:, 0], x_high[:, 0]]), "gy", False)

    def partner(value, k):
        return lax.ppermute(value, "gy", [(i, i ^ k) for i in range(groups)])

    main, masks, wide, sends = prepare(bricks, voxel_mask, features, weights, groups)
    receives = lax.all_to_all(sends, "gy", split_axis=0, concat_axis=0, tiled=True)
    info, packed = plan(bricks, sends, receives)
    wide_bias = jnp.concatenate([bias, bias])[None, :]
    operands = (main, x_low, x_high, y_low, y_high, e_low, e_high, wide, masks, wide_bias)
    packed = packed[0]

    far = list(range(groups - 1, groups // 2 - 1, -1))
    near = list(range(groups // 2 - 1, 0, -1))
    received = [None] * groups
    (brick,) = convolve((far[0],), info, operands)
    for n, k in enumerate(far):
        picks = ((near + [0])[n],) + tuple(far[n + 1 : n + 2])
        upward = [(i, i ^ k) for i in range(groups) if i < i ^ k]
        downward = [(b, a) for a, b in upward]

        def exchange(pairs, value, info, *operands):
            if not pairs:
                *made, got = convolve(picks, info, operands, spare=1)
            else:
                got = lax.ppermute(value, "gy", pairs)
                made = convolve(picks, info, operands)
            return got, *made

        branches = [functools.partial(exchange, pairs) for pairs in ([], upward, downward, upward + downward)]
        case = jnp.bitwise_and(jnp.right_shift(packed, 2 * (k - groups // 2)), 3)
        received[k], local, *ahead = lax.switch(case, branches, brick, info, *operands)
        if picks[0]:
            received[picks[0]] = partner(local, picks[0])
        else:
            received[0] = local
        brick = ahead[0] if ahead else None
    return gather(info, received)[None]


def solution(mesh):
    return jax.shard_map(
        per_device,
        mesh=mesh,
        in_specs=(
            P("gx", "gy", None, None),
            P("gx", "gy", None),
            P("gx", "gy", None),
            P("gx", "gy", None, None),
            P(),
            P(),
        ),
        out_specs=P("gx", "gy", None, None),
        check_vma=False,
    )
```
